32 devices in a mesh: grp: 2 (over x), tile: 4 (over z), tm: 4 (over y, core).
Axes of the slice: x: 2, y: 2, z: 4, core: 2. Of those that a mesh axis runs over, the one named last changes fastest.
Arguments:
- pixels: bfloat16 [6, 96, 400, 800], P('grp', 'tm', 'tile'), parts along dimension 0, may hold values from 0.049804688 to 1
- offsets: int32 [6, 20, 40, 2], P('grp'), parts along dimension 0, may hold values from -6 to 6
- subaperture_valid_mask: int32 [6, 96, 20, 40], P('grp', 'tm', 'tile'), parts along dimension 0, may hold values 0 or 1
- frame_count: int32 [8], P(('grp', 'tm')), parts along dimension 0, may hold values from 12 to 24, as said below
- slope_to_modes: bfloat16 [2, 3, 20, 40, 256], P(None, None, 'tile'), may hold values from -0.59765625 to 0.59765625
- process_noise: float32 [256], replicated, may hold values from 0.0002 to 0.2
- mode_gain: float32 [256], replicated, may hold values from 0.5 to 2
Outputs:
- smoothed_modes: float32 [192, 256], P(('grp', 'tm'), 'tile'), parts along dimension 0
- smoothed_variance: float32 [192, 256], P(('grp', 'tm'), 'tile'), parts along dimension 0
The draws below stay inside these ranges and needn't reach their ends.
There are 2 independent parts, one for each index of `grp`. The reference program is written for one: setup_inputs(seed, part) draws one part's arguments, and reference() takes and returns one part's arrays. A program takes and returns all parts, laid end to end along the dimension named above; an argument that names none is the same for every part. Nothing has to cross between parts.
Inputs may be any that keep to these rules, and one draw needn't show every extreme that they name: `frame_count`: some block has all 24 frames live.
All inputs are finite; a program needn't handle non-finite values. No bound on the sum of `subaperture_valid_mask` on one device may be relied on, other than what follows from the above.
Results may differ from the reference program's by a relative error of at most 0.00094.
Values may be sent and summed in bfloat16 or wider, within the bound.
No kernel may reach another device: no remote copies, remote signals or barrier semaphores. Data moves between devices by JAX's collectives and lax.ppermute only.
A program may use at most 128 MiB of HBM per device.

```python
import math
import jax
import jax.numpy as jnp
from jax import lax

SENSOR_COUNT = 3
SUBAPERTURE_SIDE = 20
MAX_WINDOW_SHIFT = 6
SUBAPERTURE_COLS = 40
FR_DEV = 24
ABERRATION_MODES = 256
SUBAPERTURE_ROWS = 20
PULSE_FRAMES = 96
BLOCKS = 4
NSUB = 2400


def draw_frame_count(key, part):
    key = jax.random.fold_in(key, 7)
    counts = jax.random.randint(key, (BLOCKS,), FR_DEV // 2, FR_DEV + 1)
    chosen_block = jax.random.randint(jax.random.fold_in(key, 1), (), 0, BLOCKS)
    block_ids = jnp.arange(BLOCKS, dtype=jnp.int32)
    counts = jnp.where(block_ids == chosen_block, FR_DEV, counts)
    counts = jnp.where(block_ids == (chosen_block + 1) % BLOCKS, FR_DEV // 2, counts)
    return counts.astype(jnp.int32)


def set_ends(values, key, least, top_value):
    shape = values.shape
    spot = [jax.random.randint(jax.random.fold_in(key, axis), (), 0, shape[axis]) for axis in range(len(shape))]
    values = values.at[tuple(spot)].set(least)
    longest = shape.index(max(shape))
    spot[longest] = (spot[longest] + 1) % shape[longest]
    return values.at[tuple(spot)].set(top_value)


def level_of(stream_key, extent, pieces, smallest, high):
    loudness = 1.0
    for position, blocks in pieces:
        heights = jax.random.uniform(jax.random.fold_in(jax.random.fold_in(stream_key, 6), position), (blocks,), jnp.float32, smallest / len(pieces), high / len(pieces))
        loudness = loudness * jnp.repeat(jnp.exp(heights), extent[position] // blocks).reshape((-1,) + (1,) * (len(extent) - 1 - position))
    return loudness


def bell_draw(own_key, dims, spread, limit, shards=(), kind=jnp.bfloat16):
    result = spread * jax.random.normal(own_key, dims, jnp.float32)
    if shards:
        result = result * level_of(own_key, dims, shards, -0.22, 0.18)
    return jnp.clip(result, -limit, limit).astype(kind)


def setup_inputs(seed: int = 0, part: int = 0) -> dict:
    arg_keys = jax.random.split(jax.random.key(seed), 8)
    own_keys = jax.random.split(jax.random.fold_in(arg_keys[7], part), 8)
    pixels = jnp.clip(jnp.exp(math.log(1.0) - 2.9996462 * jax.random.uniform(own_keys[0], (SENSOR_COUNT, PULSE_FRAMES, SUBAPERTURE_ROWS * SUBAPERTURE_SIDE, SUBAPERTURE_COLS * SUBAPERTURE_SIDE), jnp.float32) ** level_of(own_keys[0], (SENSOR_COUNT, PULSE_FRAMES, SUBAPERTURE_ROWS * SUBAPERTURE_SIDE, SUBAPERTURE_COLS * SUBAPERTURE_SIDE), ((1, 4), (2, 4)), -0.2, 0.2)), 0.049804688, 1.0).astype(jnp.bfloat16)
    offsets = set_ends(jax.random.randint(own_keys[1], (SENSOR_COUNT, SUBAPERTURE_ROWS, SUBAPERTURE_COLS, 2), -MAX_WINDOW_SHIFT, MAX_WINDOW_SHIFT + 1), jax.random.fold_in(own_keys[1], 1), -MAX_WINDOW_SHIFT, MAX_WINDOW_SHIFT).astype(jnp.int32)
    subaperture_valid_mask = set_ends((jax.random.randint(own_keys[2], (SENSOR_COUNT, PULSE_FRAMES, SUBAPERTURE_ROWS, SUBAPERTURE_COLS), 0, 4) < 3).astype(jnp.int32), jax.random.fold_in(own_keys[2], 1), 0, 1)
    frame_count = draw_frame_count(jax.random.fold_in(jax.random.fold_in(arg_keys[7], part), 71), part)
    slope_to_modes = bell_draw(arg_keys[4], (2, SENSOR_COUNT, SUBAPERTURE_ROWS, SUBAPERTURE_COLS, ABERRATION_MODES), 0.1, 0.59765625, ((2, 4),))
    process_noise = jnp.clip(jnp.exp(jax.random.uniform(arg_keys[5], (ABERRATION_MODES,), jnp.float32, math.log(0.0002), math.log(0.2))), 0.0002, 0.2)
    mode_gain = jnp.clip(jnp.exp(jax.random.uniform(arg_keys[6], (ABERRATION_MODES,), jnp.float32, math.log(0.5), math.log(2.0))), 0.5, 2.0)
    return dict(pixels=pixels, offsets=offsets, subaperture_valid_mask=subaperture_valid_mask, frame_count=frame_count, slope_to_modes=slope_to_modes, process_noise=process_noise, mode_gain=mode_gain)


def window_moments(picture, first_row_offset, col_start):
    pixel_steps = jnp.arange(SUBAPERTURE_SIDE, dtype=jnp.int32)
    row_index = first_row_offset[..., None] + pixel_steps
    col_index = col_start[..., None] + pixel_steps
    sensor_index = jnp.arange(picture.shape[0], dtype=jnp.int32)[:, None, None, None, None, None]
    frame_index = jnp.arange(picture.shape[1], dtype=jnp.int32)[None, :, None, None, None, None]
    window = picture[sensor_index, frame_index, row_index[:, None, :, :, :, None], col_index[:, None, :, :, None, :]]
    centred = pixel_steps.astype(jnp.float32) - (SUBAPERTURE_SIDE - 1) / 2.0
    row_sums = jnp.sum(window.astype(jnp.float32), axis=-1)
    col_sums = jnp.sum(window.astype(jnp.float32), axis=-2)
    flux_sum = jnp.sum(row_sums, axis=-1)
    along_rows = jnp.sum(row_sums * centred, axis=-1)
    along_cols = jnp.sum(col_sums * centred, axis=-1)
    return flux_sum, along_cols, along_rows


def reference(pixels, offsets, subaperture_valid_mask, frame_count, slope_to_modes, process_noise, mode_gain):
    first_row_offset = (jnp.arange(SUBAPERTURE_ROWS, dtype=jnp.int32) * SUBAPERTURE_SIDE + MAX_WINDOW_SHIFT)[None, :, None] + offsets[..., 0]
    col_start = (jnp.arange(SUBAPERTURE_COLS, dtype=jnp.int32) * SUBAPERTURE_SIDE + MAX_WINDOW_SHIFT)[None, None, :] + offsets[..., 1]

    def one_frame(frame_index):
        single = lax.dynamic_slice_in_dim(pixels, frame_index, 1, 1)
        single = jnp.pad(single, ((0, 0), (0, 0), (MAX_WINDOW_SHIFT, MAX_WINDOW_SHIFT), (MAX_WINDOW_SHIFT, MAX_WINDOW_SHIFT)))
        flux_sum, along_cols, along_rows = window_moments(single, first_row_offset, col_start)
        return flux_sum[:, 0], along_cols[:, 0], along_rows[:, 0]

    flux_sum, along_cols, along_rows = lax.map(one_frame, jnp.arange(PULSE_FRAMES, dtype=jnp.int32))
    mask_float = jnp.transpose(subaperture_valid_mask, (1, 0, 2, 3)).astype(jnp.float32)
    slopes = jnp.stack((along_cols / flux_sum, along_rows / flux_sum), 0)
    slope_terms = (slopes * mask_float).astype(jnp.bfloat16)
    mode_sums = jnp.einsum("xfsij,xsijm->fm", slope_terms.astype(jnp.float32), slope_to_modes.astype(jnp.float32), precision=lax.Precision.HIGHEST)
    counts = jnp.sum(mask_float, axis=(1, 2, 3))
    frame_ids = jnp.arange(PULSE_FRAMES, dtype=jnp.int32)
    frame_live = ((frame_ids % FR_DEV) < frame_count[frame_ids // FR_DEV]).astype(jnp.float32)[:, None]
    info_mean = mode_gain[None, :] * mode_sums * frame_live
    info_prec = mode_gain[None, :] * counts[:, None] * frame_live / NSUB

    first_var = 1.0 / (1.0 + info_prec[0])
    first_mean = first_var * info_mean[0]

    def filter_step(running, element):
        mean_prev, var_prev = running
        mean_info, prec_info = element
        predicted = var_prev + process_noise
        var_next = 1.0 / (1.0 / predicted + prec_info)
        mean_next = var_next * (mean_prev / predicted + mean_info)
        return (mean_next, var_next), (mean_next, var_next)

    final_state, (filter_means, filter_vars) = lax.scan(filter_step, (first_mean, first_var), (info_mean[1:], info_prec[1:]))
    mean_filt = jnp.concatenate((first_mean[None], filter_means), 0)
    var_filt = jnp.concatenate((first_var[None], filter_vars), 0)

    def smooth_step(running, element):
        mean_next, var_next = running
        mean_here, var_here = element
        smooth_gain = var_here / (var_here + process_noise)
        mean_new = (1.0 - smooth_gain) * mean_here + smooth_gain * mean_next
        var_new = smooth_gain * smooth_gain * var_next + var_here * (1.0 - smooth_gain)
        return (mean_new, var_new), (mean_new, var_new)

    final_back, (back_means, back_vars) = lax.scan(smooth_step, (mean_filt[-1], var_filt[-1]), (mean_filt[:-1], var_filt[:-1]), reverse=True)
    smoothed_modes = jnp.concatenate((back_means, mean_filt[-1:]), 0)
    smoothed_variance = jnp.concatenate((back_vars, var_filt[-1:]), 0)
    return smoothed_modes, smoothed_variance
```

```python
import functools

import jax
import jax.numpy as jnp
from jax import lax
from jax.experimental import pallas as pl
from jax.experimental.pallas import tpu as pltpu
from jax.sharding import PartitionSpec as P

SIDE = 20
CENTRE = (SIDE - 1) / 2.0
LANES = 128
VMEM_LIMIT = 56 * 1024 * 1024
VMEM = pl.BlockSpec(memory_space=pltpu.VMEM)
HBM = pl.BlockSpec(memory_space=pl.ANY)


def slot_of(strip, sensor):
    return (strip + 1 + sensor) % 3


def lane_iota(rows=1):
    return lax.broadcasted_iota(jnp.int32, (rows, LANES), 1)


def in_slot(lane, slot, cols):
    return (lane >= slot * cols) & (lane < (slot + 1) * cols)


def by_slot(lane, cols, values):
    out = jnp.zeros_like(values[0])
    for q, v in enumerate(values):
        out = jnp.where(in_slot(lane, q, cols), v, out)
    return out


def spread(v, cols):
    rows = v.shape[0]
    return jnp.concatenate([v, v, v, jnp.zeros((rows, LANES - 3 * cols), v.dtype)], axis=1)


def side_by_side(a, b, c):
    rows, cols = a.shape
    return jnp.concatenate([a, b, c, jnp.zeros((rows, LANES - 3 * cols), a.dtype)], axis=1)


def rotate(x, slots, cols):
    lane = lane_iota()
    shift = slots * cols
    near = pltpu.roll(x, shift, axis=1)
    far = pltpu.roll(x, LANES - 3 * cols + shift, axis=1)
    return jnp.where(lane >= shift, near, far)


def chunk_moments(x_ref, geo, w_ref, frames):
    rows, width = x_ref.shape
    col_pos = geo[0:1, :]
    row_pos = geo[1:2, :]
    base = lax.broadcasted_iota(jnp.int32, (16, LANES), 0).astype(jnp.float32) - col_pos
    for t in range(width // 16):
        d = base + float(16 * t)
        inside = jnp.abs(d) < 10.0
        w_ref[16 * t : 16 * t + 16, 0:LANES] = jnp.where(inside, 1.0, 0.0).astype(jnp.bfloat16)
        w_ref[16 * t : 16 * t + 16, LANES:] = jnp.where(inside, d, 0.0).astype(jnp.bfloat16)
    r = jnp.dot(x_ref[...], w_ref[...], preferred_element_type=jnp.float32)
    flux = jnp.zeros((frames, LANES), jnp.float32)
    cols = jnp.zeros((frames, LANES), jnp.float32)
    lines = jnp.zeros((frames, LANES), jnp.float32)
    for y in range(rows // frames):
        d = float(y) - row_pos
        inside = jnp.abs(d) < 10.0
        one = jnp.where(inside, 1.0, 0.0)
        centred = jnp.where(inside, d, 0.0)
        rf = r[y * frames : (y + 1) * frames, 0:LANES]
        rc = r[y * frames : (y + 1) * frames, LANES:]
        flux = flux + one * rf
        cols = cols + one * rc
        lines = lines + centred * rf
    return flux, cols, lines


def kernel_edge(sub_rows, sub_cols, frames, x_hbm, off_ref, p_ref, geo_ref, up_ref, down_ref, buf, w_ref, sem):
    sensors = x_hbm.shape[0]
    block = SIDE * frames
    last = sub_rows - 1

    def copy(s, e):
        start = pl.multiple_of(e * last * block, block)
        return pltpu.make_async_copy(
            x_hbm.at[s, pl.ds(start, block)], buf.at[2 * s + e], sem.at[2 * s + e]
        )

    for s in range(sensors):
        for e in range(2):
            copy(s, e).start()

    lane = lane_iota()
    index = lane - sub_cols * (lane >= sub_cols).astype(jnp.int32)
    index = index - sub_cols * (lane >= 2 * sub_cols).astype(jnp.int32)
    col_base = (SIDE * index).astype(jnp.float32) + CENTRE
    tile = lax.axis_index("tile")
    total_rows = off_ref.shape[1]
    for s in range(sensors):
        spread_rows = []
        for k in range(-1, sub_rows + 1):
            row = jnp.clip(tile * sub_rows + k, 0, total_rows - 1)
            v = off_ref[s, row].astype(jnp.float32)
            spread_rows.append(spread(v, sub_cols))
        for i in range(sub_rows):
            cs = [None] * 3
            rs = [None] * 3
            for k in (i - 1, i, i + 1):
                q = slot_of(k, s)
                v = spread_rows[k + 1]
                cs[q] = v[1:2] + col_base
                rs[q] = v[0:1] + (SIDE * (k - i) + CENTRE)
            used = lane < 3 * sub_cols
            col_pos = jnp.where(used, by_slot(lane, sub_cols, cs), -1000.0)
            row_pos = jnp.where(used, by_slot(lane, sub_cols, rs), -1000.0)
            geo_ref[s * sub_rows + i, 0:1, :] = col_pos
            geo_ref[s * sub_rows + i, 1:2, :] = row_pos

    def step(n, carry):
        s = n // 2
        e = n - 2 * s
        copy(s, e).wait()
        flux, cols, lines = chunk_moments(
            buf.at[n], geo_ref[s * sub_rows + e * last], w_ref, frames
        )
        p_ref[n, 0] = flux
        p_ref[n, 1] = cols
        p_ref[n, 2] = lines
        return carry

    lax.fori_loop(0, 2 * sensors, step, 0)
    for m in range(3):
        down = [None] * 3
        up = [None] * 3
        for s in range(sensors):
            down[slot_of(-1, s)] = p_ref[2 * s, m]
            up[slot_of(sub_rows, s)] = p_ref[2 * s + 1, m]
        down_ref[m] = by_slot(lane, sub_cols, down)
        up_ref[m] = by_slot(lane, sub_cols, up)


def slope_pair(flux, cols, lines, mask):
    live = mask > 0.0
    safe = jnp.where(live, flux, 1.0)
    sx = jnp.where(live, cols / safe, 0.0) * mask
    sy = jnp.where(live, lines / safe, 0.0) * mask
    return sx.astype(jnp.bfloat16), sy.astype(jnp.bfloat16)


def stacked(modes_ref, x, picks):
    parts = [modes_ref[x, s, k].astype(jnp.float32) for s, k in picks]
    used = sum(p.shape[0] for p in parts)
    parts.append(jnp.zeros((LANES - used, parts[0].shape[1]), jnp.float32))
    return jnp.concatenate(parts, axis=0).astype(jnp.bfloat16)


def kernel_inner(
    sub_rows, sub_cols, frames, x_hbm, geo_ref, pe_ref, mask_ref, modes_ref,
    pm_ref, edge_ref, em_ref, count_ref, buf, w_ref, acc_ref, sem,
):
    sensors = x_hbm.shape[0]
    block = SIDE * frames
    inner = sub_rows - 2
    last = sub_rows - 1

    def copy(s, i):
        start = pl.multiple_of((i + 1) * block, block)
        return pltpu.make_async_copy(
            x_hbm.at[s, pl.ds(start, block)], buf.at[inner * s + i], sem.at[inner * s + i]
        )

    for s in range(sensors):
        for i in range(inner):
            copy(s, i).start()

    lane = lane_iota()

    def step(n, carry):
        s = n // inner
        i = n - inner * s
        copy(s, i).wait()
        flux, cols, lines = chunk_moments(
            buf.at[n], geo_ref[s * sub_rows + i + 1], w_ref, frames
        )
        acc_ref[n, 0] = flux
        acc_ref[n, 1] = cols
        acc_ref[n, 2] = lines
        return carry

    lax.fori_loop(0, inner * sensors, step, 0)

    def partial(s, i, m):
        if i == 0:
            return pe_ref[2 * s, m]
        if i == last:
            return pe_ref[2 * s + 1, m]
        return acc_ref[inner * s + i - 1, m]

    def strip_total(s, k, m):
        total = None
        for i in (k - 1, k, k + 1):
            if 0 <= i <= last:
                v = partial(s, i, m)
                total = v if total is None else total + v
        return total

    masks = {}
    for s in range(sensors):
        for k in range(sub_rows):
            masks[s, k] = mask_ref[s, k].astype(jnp.float32)
    count = None
    for e, k in enumerate((0, last)):
        order = [None] * 3
        for s in range(sensors):
            order[slot_of(k, s)] = s
        m = side_by_side(*[masks[s, k] for s in order])
        em_ref[e] = m
        count = m if count is None else count + m
        for mom in range(3):
            edge_ref[e, mom] = by_slot(lane, sub_cols, [strip_total(s, k, mom) for s in order])
    modes = jnp.zeros((frames, modes_ref.shape[-1]), jnp.float32)
    for s in range(sensors):
        for g in range(1, last, 3):
            strips = list(range(g, min(g + 3, last)))
            order = sorted(strips, key=lambda k: slot_of(k, s))
            mask = side_by_side(*[masks[s, k] for k in order])
            count = count + mask
            mom = [
                by_slot(lane, sub_cols, [strip_total(s, k, m) for k in order]) for m in range(3)
            ]
            pair = slope_pair(mom[0], mom[1], mom[2], mask)
            for x in range(2):
                modes = modes + jnp.dot(
                    pair[x],
                    stacked(modes_ref, x, [(s, k) for k in order]),
                    preferred_element_type=jnp.float32,
                )
    pm_ref[...] = modes
    count_ref[...] = jnp.broadcast_to(jnp.sum(count, axis=1, keepdims=True), count_ref.shape)


def kernel_join(
    sub_rows, sub_cols, frames, tiles, blocks, total_subaps,
    live_ref, from_before_ref, from_after_ref, pm_ref, edge_ref, em_ref, count_ref, modes_ref, gain_ref,
    out_ref,
):
    sensors = modes_ref.shape[1]
    last = sub_rows - 1
    modes = pm_ref[...]
    for e, k in enumerate((0, last)):
        halo_ref = (from_before_ref, from_after_ref)[e]
        halo_strip = (sub_rows, -1)[e]
        turn = (slot_of(k, 0) - slot_of(halo_strip, 0)) % 3
        order = [None] * 3
        for s in range(sensors):
            order[slot_of(k, s)] = s
        mom = [edge_ref[e, m] + rotate(halo_ref[m], turn, sub_cols) for m in range(3)]
        pair = slope_pair(mom[0], mom[1], mom[2], em_ref[e])
        for x in range(2):
            modes = modes + jnp.dot(
                pair[x],
                stacked(modes_ref, x, [(s, k) for s in order]),
                preferred_element_type=jnp.float32,
            )
    gain = gain_ref[...]
    frame = lax.broadcasted_iota(jnp.int32, (frames, 1), 0)
    live = (frame < live_ref[0]).astype(jnp.float32)
    info_mean = gain * modes * live
    count = count_ref[...]
    count = jnp.concatenate([count] * (modes.shape[1] // LANES), axis=1)
    info_prec = gain * count * live / total_subaps
    share = modes.shape[1] // tiles
    for t in range(tiles):
        piece = jnp.concatenate(
            [info_mean[:, t * share : (t + 1) * share], info_prec[:, t * share : (t + 1) * share]],
            axis=1,
        )
        for b in range(blocks):
            out_ref[t * blocks + b] = piece


def shifted(x, by, fill, back):
    rows = x.shape[0]
    if by % 8 == 0:
        pad = jnp.full((by, x.shape[1]), fill, x.dtype)
        if back:
            return jnp.concatenate([x[by:], pad], axis=0)
        return jnp.concatenate([pad, x[: rows - by]], axis=0)
    row = lax.broadcasted_iota(jnp.int32, (rows, 1), 0)
    if back:
        return jnp.where(row < rows - by, pltpu.roll(x, rows - by, axis=0), fill)
    return jnp.where(row >= by, pltpu.roll(x, by, axis=0), fill)


def kernel_smooth(tiles, blocks, frames, in_ref, noise_ref, mean_ref, var_ref, mean_scr, var_scr):
    share = mean_ref.shape[1]
    total = blocks * frames
    tile = lax.axis_index("tile")
    time = lax.axis_index("tm")
    noise_all = noise_ref[...]
    q = jnp.zeros((1, share), jnp.float32)
    for t in range(tiles):
        q = jnp.where(tile == t, noise_all[:, t * share : (t + 1) * share], q)
    summed = []
    for b in range(blocks):
        v = in_ref[b]
        for t in range(1, tiles):
            v = v + in_ref[t * blocks + b]
        summed.append(v)
    both = jnp.concatenate(summed, axis=0)
    info_mean = both[:, :share]
    prec = both[:, share:]
    row = lax.broadcasted_iota(jnp.int32, (total, 1), 0)
    first = row == 0
    retain = 1.0 / (1.0 + q * prec)
    a = jnp.where(first, 0.0, retain)
    c = jnp.where(first, 1.0 / (1.0 + prec), q * retain)
    b = c * info_mean
    e = a * info_mean
    j = a * prec
    by = 1
    while by < total:
        a1 = shifted(a, by, 1.0, False)
        b1 = shifted(b, by, 0.0, False)
        c1 = shifted(c, by, 0.0, False)
        e1 = shifted(e, by, 0.0, False)
        j1 = shifted(j, by, 0.0, False)
        damp = 1.0 / (1.0 + c1 * j)
        left = a * damp
        right = a1 * damp
        b = left * (b1 + c1 * e) + b
        c = left * a * c1 + c
        e, j = right * (e - j * b1) + e1, right * a1 * j + j1
        a = left * a1
        by *= 2
    g = jnp.where(row == total - 1, 0.0, c / (c + q))
    m = (1.0 - g) * b
    v = c * (1.0 - g)
    by = 1
    while by < total:
        g1 = shifted(g, by, 1.0, True)
        m1 = shifted(m, by, 0.0, True)
        v1 = shifted(v, by, 0.0, True)
        m = g * m1 + m
        v = g * g * v1 + v
        g = g * g1
        by *= 2
    mean_scr[...] = m
    var_scr[...] = v
    start = pl.multiple_of(time * frames, 8)
    mean_ref[...] = mean_scr[pl.ds(start, frames), :]
    var_ref[...] = var_scr[pl.ds(start, frames), :]


def body(pixels, offsets, mask, frame_count, slope_to_modes, process_noise, mode_gain):
    sensors, frames, lines, width = pixels.shape
    sub_rows, sub_cols = mask.shape[2], mask.shape[3]
    modes = process_noise.shape[0]
    tiles = lax.axis_size("tile")
    blocks = lax.axis_size("tm")
    share = modes // tiles
    total_subaps = sensors * sub_rows * tiles * sub_cols
    f32 = jnp.float32
    x = jnp.transpose(pixels, (0, 2, 1, 3)).reshape(sensors, lines * frames, width)
    off = jnp.transpose(offsets, (0, 1, 3, 2))
    msk = jnp.transpose(mask, (0, 2, 1, 3))
    block = SIDE * frames
    inner = sub_rows - 2
    params = pltpu.CompilerParams(vmem_limit_bytes=VMEM_LIMIT)

    def cost(chunks):
        return pl.CostEstimate(
            flops=2 * chunks * block * width * 256, bytes_accessed=chunks * block * width * 2, transcendentals=0
        )

    parts, geo, up, down = pl.pallas_call(
        functools.partial(kernel_edge, sub_rows, sub_cols, frames),
        out_shape=(
            jax.ShapeDtypeStruct((2 * sensors, 3, frames, LANES), f32),
            jax.ShapeDtypeStruct((sensors * sub_rows, 8, LANES), f32),
            jax.ShapeDtypeStruct((3, frames, LANES), f32),
            jax.ShapeDtypeStruct((3, frames, LANES), f32),
        ),
        in_specs=[HBM, VMEM],
        out_specs=(VMEM, VMEM, VMEM, VMEM),
        scratch_shapes=[
            pltpu.VMEM((2 * sensors, block, width), jnp.bfloat16),
            pltpu.VMEM((width, 2 * LANES), jnp.bfloat16),
            pltpu.SemaphoreType.DMA((2 * sensors,)),
        ],
        compiler_params=params,
        cost_estimate=cost(2 * sensors),
        name="edge_moments",
    )(x, off)
    onward = [(i, i + 1) for i in range(tiles - 1)]
    backward = [(j, i) for i, j in onward]
    from_before = lax.ppermute(up, "tile", onward)
    from_after = lax.ppermute(down, "tile", backward)
    partial_modes, edge, edge_mask, count = pl.pallas_call(
        functools.partial(kernel_inner, sub_rows, sub_cols, frames),
        out_shape=(
            jax.ShapeDtypeStruct((frames, modes), f32),
            jax.ShapeDtypeStruct((2, 3, frames, LANES), f32),
            jax.ShapeDtypeStruct((2, frames, LANES), f32),
            jax.ShapeDtypeStruct((frames, LANES), f32),
        ),
        in_specs=[HBM, VMEM, VMEM, VMEM, VMEM],
        out_specs=(VMEM, VMEM, VMEM, VMEM),
        scratch_shapes=[
            pltpu.VMEM((inner * sensors, block, width), jnp.bfloat16),
            pltpu.VMEM((width, 2 * LANES), jnp.bfloat16),
            pltpu.VMEM((inner * sensors, 3, frames, LANES), f32),
            pltpu.SemaphoreType.DMA((inner * sensors,)),
        ],
        compiler_params=params,
        cost_estimate=cost(inner * sensors),
        name="inner_moments",
    )(x, geo, parts, msk, slope_to_modes)
    payload = pl.pallas_call(
        functools.partial(kernel_join, sub_rows, sub_cols, frames, tiles, blocks, float(total_subaps)),
        out_shape=jax.ShapeDtypeStruct((tiles * blocks, frames, 2 * share), f32),
        in_specs=[pl.BlockSpec(memory_space=pltpu.SMEM)] + [VMEM] * 8,
        out_specs=VMEM,
        compiler_params=params,
        name="join_halo",
    )(
        frame_count, from_before, from_after, partial_modes, edge, edge_mask, count,
        slope_to_modes, mode_gain.reshape(1, modes),
    )
    info = lax.all_to_all(payload, ("tile", "tm"), 0, 0)
    return pl.pallas_call(
        functools.partial(kernel_smooth, tiles, blocks, frames),
        out_shape=(
            jax.ShapeDtypeStruct((frames, share), f32),
            jax.ShapeDtypeStruct((frames, share), f32),
        ),
        in_specs=[VMEM, VMEM],
        out_specs=(VMEM, VMEM),
        scratch_shapes=[
            pltpu.VMEM((blocks * frames, share), f32),
            pltpu.VMEM((blocks * frames, share), f32),
        ],
        compiler_params=params,
        name="smooth",
    )(info, process_noise.reshape(1, modes))


def solution(mesh):
    return jax.shard_map(
        body,
        mesh=mesh,
        in_specs=(
            P("grp", "tm", "tile", None),
            P("grp", None, None, None),
            P("grp", "tm", "tile", None),
            P(("grp", "tm")),
            P(None, None, "tile", None, None),
            P(),
            P(),
        ),
        out_specs=(P(("grp", "tm"), "tile"), P(("grp", "tm"), "tile")),
        check_vma=False,
    )
```

```python
import functools

import jax
import jax.numpy as jnp
from jax import lax
from jax.experimental import pallas as pl
from jax.experimental.pallas import tpu as pltpu
from jax.sharding import PartitionSpec as P

SIDE = 20
CENTRE = (SIDE - 1) / 2.0
LANES = 128
VMEM_LIMIT = 56 * 1024 * 1024
VMEM = pl.BlockSpec(memory_space=pltpu.VMEM)
HBM = pl.BlockSpec(memory_space=pl.ANY)


def slot_of(strip, sensor):
    return (strip + 1 + sensor) % 3


def lane_iota(rows=1):
    return lax.broadcasted_iota(jnp.int32, (rows, LANES), 1)


def in_slot(lane, slot, cols):
    return (lane >= slot * cols) & (lane < (slot + 1) * cols)


def by_slot(lane, cols, values):
    out = jnp.zeros_like(values[0])
    for q, v in enumerate(values):
        out = jnp.where(in_slot(lane, q, cols), v, out)
    return out


def spread(v, cols):
    rows = v.shape[0]
    return jnp.concatenate([v, v, v, jnp.zeros((rows, LANES - 3 * cols), v.dtype)], axis=1)


def side_by_side(a, b, c):
    rows, cols = a.shape
    return jnp.concatenate([a, b, c, jnp.zeros((rows, LANES - 3 * cols), a.dtype)], axis=1)


def rotate(x, slots, cols):
    lane = lane_iota()
    shift = slots * cols
    near = pltpu.roll(x, shift, axis=1)
    far = pltpu.roll(x, LANES - 3 * cols + shift, axis=1)
    return jnp.where(lane >= shift, near, far)


def build_weights(geo, w_ref):
    base = lax.broadcasted_iota(jnp.int32, (16, LANES), 0).astype(jnp.float32) - geo[0:1, :]
    for t in range(w_ref.shape[0] // 16):
        d = base + float(16 * t)
        inside = jnp.abs(d) < 10.0
        w_ref[16 * t : 16 * t + 16, 0:LANES] = jnp.where(inside, 1.0, 0.0).astype(jnp.bfloat16)
        w_ref[16 * t : 16 * t + 16, LANES:] = jnp.where(inside, d, 0.0).astype(jnp.bfloat16)


def row_sums(geo, r_ref, p_ref, frames):
    row_pos = geo[1:2, :]
    flux = jnp.zeros((frames, LANES), jnp.float32)
    cols = jnp.zeros((frames, LANES), jnp.float32)
    lines = jnp.zeros((frames, LANES), jnp.float32)
    for y in range(r_ref.shape[0] // frames):
        d = float(y) - row_pos
        inside = jnp.abs(d) < 10.0
        one = jnp.where(inside, 1.0, 0.0)
        centred = jnp.where(inside, d, 0.0)
        rf = r_ref[y * frames : (y + 1) * frames, 0:LANES]
        rc = r_ref[y * frames : (y + 1) * frames, LANES:]
        flux = flux + one * rf
        cols = cols + one * rc
        lines = lines + centred * rf
    p_ref[0] = flux
    p_ref[1] = cols
    p_ref[2] = lines


def geometry(geo_ref, off_ref, sensors, sub_rows, sub_cols):
    lane = lane_iota()
    index = lane - sub_cols * (lane >= sub_cols).astype(jnp.int32)
    index = index - sub_cols * (lane >= 2 * sub_cols).astype(jnp.int32)
    col_base = (SIDE * index).astype(jnp.float32) + CENTRE
    used = lane < 3 * sub_cols
    tile = lax.axis_index("tile")
    total_rows = off_ref.shape[1]
    for s in range(sensors):
        spread_rows = []
        for k in range(-1, sub_rows + 1):
            row = jnp.clip(tile * sub_rows + k, 0, total_rows - 1)
            v = off_ref[s, row].astype(jnp.float32)
            spread_rows.append(spread(v, sub_cols))
        for i in range(sub_rows):
            cs = [None] * 3
            rs = [None] * 3
            for k in (i - 1, i, i + 1):
                q = slot_of(k, s)
                v = spread_rows[k + 1]
                cs[q] = v[1:2] + col_base
                rs[q] = v[0:1] + (SIDE * (k - i) + CENTRE)
            geo_ref[s, i, 0:1, :] = jnp.where(used, by_slot(lane, sub_cols, cs), -1000.0)
            geo_ref[s, i, 1:2, :] = jnp.where(used, by_slot(lane, sub_cols, rs), -1000.0)


def slope_pair(flux, cols, lines, mask):
    live = mask > 0.0
    safe = jnp.where(live, flux, 1.0)
    sx = jnp.where(live, cols / safe, 0.0) * mask
    sy = jnp.where(live, lines / safe, 0.0) * mask
    return sx.astype(jnp.bfloat16), sy.astype(jnp.bfloat16)


def stacked(modes_ref, x, picks):
    parts = [modes_ref[x, s, k].astype(jnp.float32) for s, k in picks]
    used = sum(p.shape[0] for p in parts)
    parts.append(jnp.zeros((LANES - used, parts[0].shape[1]), jnp.float32))
    return jnp.concatenate(parts, axis=0).astype(jnp.bfloat16)


def kernel_moments(
    sub_rows, sub_cols, frames, x_hbm, off_hbm, mask_hbm, modes_hbm,
    pm_ref, edge_ref, em_ref, count_ref, halo_ref,
    buf, w_ref, r_ref, p_ref, geo_ref, off_ref, mask_ref, modes_ref, sem, side_sem,
):
    sensors = x_hbm.shape[0]
    block = SIDE * frames
    last = sub_rows - 1

    def copy(s, i):
        return pltpu.make_async_copy(
            x_hbm.at[s, pl.ds(i * block, block)], buf.at[s, i], sem.at[s, i]
        )

    off_copy = pltpu.make_async_copy(off_hbm, off_ref, side_sem.at[0])
    mask_copy = pltpu.make_async_copy(mask_hbm, mask_ref, side_sem.at[1])
    modes_copy = pltpu.make_async_copy(modes_hbm, modes_ref, side_sem.at[2])
    off_copy.start()
    for s in range(sensors):
        for i in range(sub_rows):
            copy(s, i).start()
    mask_copy.start()
    modes_copy.start()
    off_copy.wait()
    geometry(geo_ref, off_ref, sensors, sub_rows, sub_cols)
    build_weights(geo_ref[0, 0], w_ref.at[0])

    def step(s, carry):
        for i in range(sub_rows):
            copy(s, i).wait()
            if i < last:
                build_weights(geo_ref[s, i + 1], w_ref.at[i + 1])
            else:
                build_weights(geo_ref[jnp.minimum(s + 1, sensors - 1), 0], w_ref.at[0])
            r_ref[i] = jnp.dot(buf[s, i], w_ref[i], preferred_element_type=jnp.float32)
            if i > 0:
                row_sums(geo_ref[s, i - 1], r_ref.at[i - 1], p_ref.at[s, i - 1], frames)
        row_sums(geo_ref[s, last], r_ref.at[last], p_ref.at[s, last], frames)
        return carry

    lax.fori_loop(0, sensors, step, 0)
    lane = lane_iota()

    def strip_total(s, k, m):
        total = None
        for i in (k - 1, k, k + 1):
            if 0 <= i <= last:
                v = p_ref[s, i, m]
                total = v if total is None else total + v
        return total

    for m in range(3):
        down = [None] * 3
        up = [None] * 3
        for s in range(sensors):
            down[slot_of(-1, s)] = p_ref[s, 0, m]
            up[slot_of(sub_rows, s)] = p_ref[s, last, m]
        halo_ref[0, m] = by_slot(lane, sub_cols, up)
        halo_ref[1, m] = by_slot(lane, sub_cols, down)
    mask_copy.wait()
    modes_copy.wait()
    masks = {}
    for s in range(sensors):
        for k in range(sub_rows):
            masks[s, k] = mask_ref[s, k].astype(jnp.float32)
    count = None
    for e, k in enumerate((0, last)):
        order = [None] * 3
        for s in range(sensors):
            order[slot_of(k, s)] = s
        m = side_by_side(*[masks[s, k] for s in order])
        em_ref[e] = m
        count = m if count is None else count + m
        for mom in range(3):
            edge_ref[e, mom] = by_slot(lane, sub_cols, [strip_total(s, k, mom) for s in order])
    modes = jnp.zeros((frames, modes_ref.shape[-1]), jnp.float32)
    for s in range(sensors):
        for g in range(1, last, 3):
            strips = list(range(g, min(g + 3, last)))
            order = sorted(strips, key=lambda k: slot_of(k, s))
            mask = side_by_side(*[masks[s, k] for k in order])
            count = count + mask
            mom = [
                by_slot(lane, sub_cols, [strip_total(s, k, m) for k in order]) for m in range(3)
            ]
            pair = slope_pair(mom[0], mom[1], mom[2], mask)
            for x in range(2):
                modes = modes + jnp.dot(
                    pair[x],
                    stacked(modes_ref, x, [(s, k) for k in order]),
                    preferred_element_type=jnp.float32,
                )
    pm_ref[...] = modes
    count_ref[...] = jnp.broadcast_to(jnp.sum(count, axis=1, keepdims=True), count_ref.shape)


def kernel_join(
    sub_rows, sub_cols, frames, tiles,
    live_ref, halo_ref, pm_ref, edge_ref, em_ref, count_ref, modes_ref, gain_ref, out_ref,
):
    sensors = modes_ref.shape[1]
    last = sub_rows - 1
    modes = pm_ref[...]
    tile = lax.axis_index("tile")
    for e, k in enumerate((0, last)):
        halo_strip = (sub_rows, -1)[e]
        near = (jnp.maximum(tile - 1, 0), jnp.minimum(tile + 1, tiles - 1))[e]
        there = (tile > 0, tile < tiles - 1)[e]
        turn = (slot_of(k, 0) - slot_of(halo_strip, 0)) % 3
        order = [None] * 3
        for s in range(sensors):
            order[slot_of(k, s)] = s
        mom = [
            edge_ref[e, m] + rotate(jnp.where(there, halo_ref[near, e, m], 0.0), turn, sub_cols)
            for m in range(3)
        ]
        pair = slope_pair(mom[0], mom[1], mom[2], em_ref[e])
        for x in range(2):
            modes = modes + jnp.dot(
                pair[x],
                stacked(modes_ref, x, [(s, k) for s in order]),
                preferred_element_type=jnp.float32,
            )
    frame = lax.broadcasted_iota(jnp.int32, (frames, 1), 0)
    live = (frame < live_ref[0]).astype(jnp.float32)
    out_ref[0:frames, :] = gain_ref[...] * modes * live
    lane = lane_iota(frames)
    own = lane == lax.broadcasted_iota(jnp.int32, (frames, LANES), 0)
    count_row = jnp.sum(jnp.where(own, count_ref[...] * live, 0.0), axis=0, keepdims=True)
    out_ref[frames : frames + 8, :] = jnp.zeros((8, modes.shape[1]), jnp.float32)
    out_ref[frames : frames + 1, 0:LANES] = count_row


def shifted(x, by, fill, back):
    rows = x.shape[0]
    if by % 8 == 0:
        pad = jnp.full((by, x.shape[1]), fill, x.dtype)
        if back:
            return jnp.concatenate([x[by:], pad], axis=0)
        return jnp.concatenate([pad, x[: rows - by]], axis=0)
    row = lax.broadcasted_iota(jnp.int32, (rows, 1), 0)
    if back:
        return jnp.where(row < rows - by, pltpu.roll(x, rows - by, axis=0), fill)
    return jnp.where(row >= by, pltpu.roll(x, by, axis=0), fill)


def kernel_smooth(tiles, blocks, frames, total_subaps, in_ref, noise_ref, gain_ref, mean_ref, var_ref, mean_scr, var_scr):
    share = mean_ref.shape[1]
    total = blocks * frames
    tile = lax.axis_index("tile")
    time = lax.axis_index("tm")
    def own_modes(v):
        out = v[:, 0:share]
        for t in range(1, tiles):
            out = jnp.where(tile == t, v[:, t * share : (t + 1) * share], out)
        return out

    q = own_modes(noise_ref[...])
    gain = own_modes(gain_ref[...])
    own = lane_iota(frames) == lax.broadcasted_iota(jnp.int32, (frames, LANES), 0)
    summed = []
    counts = []
    for b in range(blocks):
        v = in_ref[b]
        for t in range(1, tiles):
            v = v + in_ref[t * blocks + b]
        summed.append(v[0:frames])
        count_row = v[frames : frames + 1, 0:LANES]
        counts.append(jnp.sum(jnp.where(own, count_row, 0.0), axis=1, keepdims=True))
    info_mean = own_modes(jnp.concatenate(summed, axis=0))
    prec = gain * jnp.concatenate(counts, axis=0) / total_subaps
    row = lax.broadcasted_iota(jnp.int32, (total, 1), 0)
    first = row == 0
    retain = 1.0 / (1.0 + q * prec)
    a = jnp.where(first, 0.0, retain)
    c = jnp.where(first, 1.0 / (1.0 + prec), q * retain)
    b = c * info_mean
    e = a * info_mean
    j = a * prec
    by = 1
    while by < total:
        a1 = shifted(a, by, 1.0, False)
        b1 = shifted(b, by, 0.0, False)
        c1 = shifted(c, by, 0.0, False)
        e1 = shifted(e, by, 0.0, False)
        j1 = shifted(j, by, 0.0, False)
        damp = 1.0 / (1.0 + c1 * j)
        left = a * damp
        right = a1 * damp
        b = left * (b1 + c1 * e) + b
        c = left * a * c1 + c
        e, j = right * (e - j * b1) + e1, right * a1 * j + j1
        a = left * a1
        by *= 2
    g = jnp.where(row == total - 1, 0.0, c / (c + q))
    m = (1.0 - g) * b
    v = c * (1.0 - g)
    by = 1
    while by < total:
        g1 = shifted(g, by, 1.0, True)
        m1 = shifted(m, by, 0.0, True)
        v1 = shifted(v, by, 0.0, True)
        m = g * m1 + m
        v = g * g * v1 + v
        g = g * g1
        by *= 2
    mean_scr[...] = m
    var_scr[...] = v
    start = pl.multiple_of(time * frames, 8)
    mean_ref[...] = mean_scr[pl.ds(start, frames), :]
    var_ref[...] = var_scr[pl.ds(start, frames), :]


def body(pixels, offsets, mask, frame_count, slope_to_modes, process_noise, mode_gain):
    sensors, frames, lines, width = pixels.shape
    sub_rows, sub_cols = mask.shape[2], mask.shape[3]
    modes = process_noise.shape[0]
    tiles = lax.axis_size("tile")
    blocks = lax.axis_size("tm")
    share = modes // tiles
    total_subaps = sensors * sub_rows * tiles * sub_cols
    f32 = jnp.float32
    x = jnp.transpose(pixels, (0, 2, 1, 3)).reshape(sensors, lines * frames, width)
    off = jnp.transpose(offsets, (0, 1, 3, 2))
    msk = jnp.transpose(mask, (0, 2, 1, 3))
    block = SIDE * frames
    params = pltpu.CompilerParams(vmem_limit_bytes=VMEM_LIMIT)

    def cost(chunks):
        return pl.CostEstimate(
            flops=2 * chunks * block * width * 256, bytes_accessed=chunks * block * width * 2, transcendentals=0
        )

    bf16 = jnp.bfloat16
    partial_modes, edge, edge_mask, count, halo = pl.pallas_call(
        functools.partial(kernel_moments, sub_rows, sub_cols, frames),
        out_shape=(
            jax.ShapeDtypeStruct((frames, modes), f32),
            jax.ShapeDtypeStruct((2, 3, frames, LANES), f32),
            jax.ShapeDtypeStruct((2, frames, LANES), f32),
            jax.ShapeDtypeStruct((frames, LANES), f32),
            jax.ShapeDtypeStruct((2, 3, frames, LANES), f32),
        ),
        in_specs=[HBM] * 4,
        out_specs=(VMEM,) * 5,
        scratch_shapes=[
            pltpu.VMEM((sensors, sub_rows, block, width), bf16),
            pltpu.VMEM((sub_rows, width, 2 * LANES), bf16),
            pltpu.VMEM((sub_rows, block, 2 * LANES), f32),
            pltpu.VMEM((sensors, sub_rows, 3, frames, LANES), f32),
            pltpu.VMEM((sensors, sub_rows, 8, LANES), f32),
            pltpu.VMEM(off.shape, off.dtype),
            pltpu.VMEM(msk.shape, msk.dtype),
            pltpu.VMEM(slope_to_modes.shape, bf16),
            pltpu.SemaphoreType.DMA((sensors, sub_rows)),
            pltpu.SemaphoreType.DMA((3,)),
        ],
        compiler_params=params,
        cost_estimate=cost(sensors * sub_rows),
        name="moments",
    )(x, off, msk, slope_to_modes)
    halos = lax.all_gather(halo, "tile")
    gain = mode_gain.reshape(1, modes)
    payload = pl.pallas_call(
        functools.partial(kernel_join, sub_rows, sub_cols, frames, tiles),
        out_shape=jax.ShapeDtypeStruct((frames + 8, modes), f32),
        in_specs=[pl.BlockSpec(memory_space=pltpu.SMEM)] + [VMEM] * 7,
        out_specs=VMEM,
        compiler_params=params,
        name="join_halo",
    )(frame_count, halos, partial_modes, edge, edge_mask, count, slope_to_modes, gain)
    info = lax.all_gather(payload, ("tile", "tm"))
    return pl.pallas_call(
        functools.partial(kernel_smooth, tiles, blocks, frames, float(total_subaps)),
        out_shape=(
            jax.ShapeDtypeStruct((frames, share), f32),
            jax.ShapeDtypeStruct((frames, share), f32),
        ),
        in_specs=[VMEM] * 3,
        out_specs=(VMEM, VMEM),
        scratch_shapes=[
            pltpu.VMEM((blocks * frames, share), f32),
            pltpu.VMEM((blocks * frames, share), f32),
        ],
        compiler_params=params,
        name="smooth",
    )(info, process_noise.reshape(1, modes), gain)


def solution(mesh):
    return jax.shard_map(
        body,
        mesh=mesh,
        in_specs=(
            P("grp", "tm", "tile", None),
            P("grp", None, None, None),
            P("grp", "tm", "tile", None),
            P(("grp", "tm")),
            P(None, None, "tile", None, None),
            P(),
            P(),
        ),
        out_specs=(P(("grp", "tm"), "tile"), P(("grp", "tm"), "tile")),
        check_vma=False,
    )
```

```python
import functools

import jax
import jax.numpy as jnp
from jax import lax
from jax.experimental import pallas as pl
from jax.experimental.pallas import tpu as pltpu
from jax.sharding import PartitionSpec as P

SIDE = 20
SHIFT = 6
CENTRE = (SIDE - 1) / 2.0
LANES = 128
HALF = LANES // 2
VMEM_LIMIT = 24 * 1024 * 1024
VMEM = pl.BlockSpec(memory_space=pltpu.VMEM)
HBM = pl.BlockSpec(memory_space=pl.ANY)


def slot_of(strip, sensor):
    return (strip + 1 + sensor) % 3


def half_columns(half, sub_cols, width):
    cols = sub_cols // 2
    first = max(0, half * cols * SIDE - SHIFT) // LANES * LANES
    end = min(width, -(-((half + 1) * cols * SIDE + SHIFT) // 16) * 16)
    return first, end - first


def lane_iota(rows=1):
    return lax.broadcasted_iota(jnp.int32, (rows, LANES), 1)


def half_lane(rows=1):
    lane = lane_iota(rows)
    return jnp.where(lane >= HALF, lane - HALF, lane)


def by_slot(values, cols):
    lane = half_lane()
    out = jnp.zeros_like(values[0])
    for q, v in enumerate(values):
        if v is not None:
            out = jnp.where((lane >= q * cols) & (lane < (q + 1) * cols), v, out)
    return out


def side_by_side(pieces):
    rows, cols = pieces[0].shape
    pad = jnp.zeros((rows, HALF - 3 * cols), pieces[0].dtype)
    return jnp.concatenate([*pieces, pad, *pieces, pad], axis=1)


def rotate(x, slots, cols):
    shift = slots * cols
    if shift == 0:
        return x
    near = pltpu.roll(x, shift, axis=1)
    far = pltpu.roll(x, LANES - 3 * cols + shift, axis=1)
    return jnp.where(half_lane() >= shift, near, far)


def geometry(geo_ref, off_ref, sensors, sub_rows, sub_cols, width):
    cols = sub_cols // 2
    lane = half_lane()
    index = lane - cols * (lane >= cols).astype(jnp.int32)
    index = index - cols * (lane >= 2 * cols).astype(jnp.int32)
    used = lane < 3 * cols
    tile = lax.axis_index("tile")
    total_rows = off_ref.shape[1]
    for s in range(sensors):
        spread_rows = []
        for k in range(-1, sub_rows + 1):
            row = jnp.clip(tile * sub_rows + k, 0, total_rows - 1)
            v = off_ref[s, row].astype(jnp.float32)
            spread_rows.append([side_by_side([v[:, h * cols : (h + 1) * cols]] * 3) for h in range(2)])
        for i in range(sub_rows):
            for h in range(2):
                first, _ = half_columns(h, sub_cols, width)
                col_base = (SIDE * (index + h * cols) - first).astype(jnp.float32) + CENTRE
                cs = [None] * 3
                rs = [None] * 3
                for k in (i - 1, i, i + 1):
                    q = slot_of(k, s)
                    v = spread_rows[k + 1][h]
                    cs[q] = v[1:2] + col_base
                    rs[q] = v[0:1] + (SIDE * (k - i) + CENTRE)
                geo_ref[s, i, 2 * h : 2 * h + 1, :] = jnp.where(used, by_slot(cs, cols), -1000.0)
                geo_ref[s, i, 2 * h + 1 : 2 * h + 2, :] = jnp.where(used, by_slot(rs, cols), -1000.0)


def build_weights(col_pos, w_ref):
    base = lax.broadcasted_iota(jnp.int32, (16, LANES), 0).astype(jnp.float32) - col_pos
    left = lane_iota(16) < HALF
    for t in range(w_ref.shape[0] // 16):
        d = base + float(16 * t)
        value = jnp.where(left, 1.0, d)
        w_ref[16 * t : 16 * t + 16, :] = jnp.where(jnp.abs(d) < 10.0, value, 0.0).astype(jnp.bfloat16)


def row_sums(row_pos, r, frames):
    plain = jnp.zeros((frames, LANES), jnp.float32)
    lines = jnp.zeros((frames, LANES), jnp.float32)
    for y in range(r.shape[0] // frames):
        d = float(y) - row_pos
        inside = jnp.abs(d) < 10.0
        one = jnp.where(inside, 1.0, 0.0)
        centred = jnp.where(inside, d, 0.0)
        piece = r[y * frames : (y + 1) * frames, :]
        plain = plain + one * piece
        lines = lines + centred * piece
    return plain, lines


def block_moments(x_ref, geo_ref, w_ref, p_ref, sub_cols, frames):
    count = len(x_ref)
    for n in range(count):
        for h in range(2):
            build_weights(geo_ref[n][2 * h : 2 * h + 1, :], w_ref.at[n, h])
    for n in range(count):
        for h in range(2):
            first, size = half_columns(h, sub_cols, x_ref[n].shape[1])
            r = jnp.dot(
                x_ref[n][:, first : first + size],
                w_ref[n, h, 0:size, :],
                preferred_element_type=jnp.float32,
            )
            plain, lines = row_sums(geo_ref[n][2 * h + 1 : 2 * h + 2, :], r, frames)
            p_ref[n][h, 0] = plain
            p_ref[n][h, 1] = lines


def kernel_edge(
    sub_rows, sub_cols, frames, x_hbm, off_hbm, mask_hbm, modes_hbm,
    up_ref, down_ref, p_ref, geo_ref, buf, mask_ref, modes_ref,
    w_ref, off_ref, sem, side_sem,
):
    sensors = x_hbm.shape[0]
    block = SIDE * frames
    last = sub_rows - 1
    cols = sub_cols // 2

    def copy(s, i):
        return pltpu.make_async_copy(
            x_hbm.at[s, pl.ds(i * block, block)], buf.at[s, i], sem.at[s, i]
        )

    off_copy = pltpu.make_async_copy(off_hbm, off_ref, side_sem.at[0])
    mask_copy = pltpu.make_async_copy(mask_hbm, mask_ref, side_sem.at[1])
    modes_copy = pltpu.make_async_copy(modes_hbm, modes_ref, side_sem.at[2])
    off_copy.start()
    for s in range(sensors):
        for i in (0, last):
            copy(s, i).start()
    for s in range(sensors):
        for i in range(1, last):
            copy(s, i).start()
    mask_copy.start()
    modes_copy.start()
    off_copy.wait()
    geometry(geo_ref, off_ref, sensors, sub_rows, sub_cols, x_hbm.shape[2])

    def step(s, carry):
        copy(s, 0).wait()
        copy(s, last).wait()
        block_moments(
            [buf.at[s, 0], buf.at[s, last]],
            [geo_ref.at[s, 0], geo_ref.at[s, last]],
            w_ref,
            [p_ref.at[s, 0], p_ref.at[s, 1]],
            sub_cols,
            frames,
        )
        return carry

    lax.fori_loop(0, sensors, step, 0)
    left = lane_iota() < HALF
    for ref, e, strip in ((down_ref, 0, -1), (up_ref, 1, sub_rows)):
        pair = []
        for h in range(2):
            both = []
            for a in range(2):
                order = [None] * 3
                for s in range(sensors):
                    order[slot_of(strip, s)] = p_ref[s, e, h, a]
                both.append(by_slot(order, cols))
            ref[h] = both[0]
            pair.append(both[1])
        ref[2] = jnp.where(left, pair[0], pltpu.roll(pair[1], HALF, axis=1))
    for s in range(sensors):
        for i in range(1, last):
            copy(s, i).wait()
    mask_copy.wait()
    modes_copy.wait()


def slope_terms(plain, lines, mask):
    left = lane_iota() < HALF
    live = mask > 0.0
    flux = jnp.where(left, plain, pltpu.roll(plain, HALF, axis=1))
    moment = jnp.where(left, lines, plain)
    return jnp.where(live, moment / jnp.where(live, flux, 1.0) * mask, 0.0).astype(jnp.bfloat16)


def stacked(modes_ref, picks, half, cols):
    parts = []
    for x in (1, 0):
        used = 0
        for pick in picks:
            if pick is None:
                parts.append(jnp.zeros((cols, modes_ref.shape[-1]), jnp.float32))
            else:
                s, k = pick
                rows = modes_ref[x, s, k].astype(jnp.float32)
                parts.append(rows[half * cols : (half + 1) * cols])
            used += cols
        parts.append(jnp.zeros((HALF - used, modes_ref.shape[-1]), jnp.float32))
    return jnp.concatenate(parts, axis=0).astype(jnp.bfloat16)


def kernel_inner(
    sub_rows, sub_cols, frames, x_ref, geo_ref, pe_ref, mask_ref, modes_ref,
    pm_ref, edge_ref, em_ref, count_ref, w_ref, p_ref,
):
    sensors = x_ref.shape[0]
    last = sub_rows - 1
    cols = sub_cols // 2

    def step(s, carry):
        block_moments(
            [x_ref.at[s, i] for i in range(1, last)],
            [geo_ref.at[s, i] for i in range(1, last)],
            w_ref,
            [p_ref.at[s, i - 1] for i in range(1, last)],
            sub_cols,
            frames,
        )
        return carry

    lax.fori_loop(0, sensors, step, 0)

    def partial(s, i, h, a):
        if i == 0:
            return pe_ref[s, 0, h, a]
        if i == last:
            return pe_ref[s, 1, h, a]
        return p_ref[s, i - 1, h, a]

    def strip_total(s, k, h, a):
        total = None
        for i in (k - 1, k, k + 1):
            if 0 <= i <= last:
                v = partial(s, i, h, a)
                total = v if total is None else total + v
        return total

    def mask_of(s, k, h):
        return mask_ref[s, k].astype(jnp.float32)[:, h * cols : (h + 1) * cols]

    count = jnp.zeros((frames, LANES), jnp.float32)
    for e, k in enumerate((0, last)):
        order = [None] * 3
        for s in range(sensors):
            order[slot_of(k, s)] = s
        for h in range(2):
            m = side_by_side([mask_of(s, k, h) for s in order])
            em_ref[e, h] = m
            count = count + m
            for a in range(2):
                edge_ref[e, h, a] = by_slot([strip_total(s, k, h, a) for s in order], cols)
    modes = jnp.zeros((frames, modes_ref.shape[-1]), jnp.float32)
    for s in range(sensors):
        for g in range(1, last, 3):
            order = [None] * 3
            for k in range(g, min(g + 3, last)):
                order[slot_of(k, s)] = k
            for h in range(2):
                none = jnp.zeros((frames, cols), jnp.float32)
                mask = side_by_side([none if k is None else mask_of(s, k, h) for k in order])
                count = count + mask
                plain, lines = (
                    by_slot([None if k is None else strip_total(s, k, h, a) for k in order], cols)
                    for a in range(2)
                )
                modes = modes + jnp.dot(
                    slope_terms(plain, lines, mask),
                    stacked(modes_ref, [None if k is None else (s, k) for k in order], h, cols),
                    preferred_element_type=jnp.float32,
                )
    pm_ref[...] = modes
    count_ref[...] = jnp.broadcast_to(0.5 * jnp.sum(count, axis=1, keepdims=True), count_ref.shape)


def kernel_join(
    sub_rows, sub_cols, frames, tiles, blocks,
    live_ref, before_ref, after_ref, pm_ref, edge_ref, em_ref, count_ref, modes_ref, gain_ref, out_ref,
):
    sensors = modes_ref.shape[1]
    last = sub_rows - 1
    cols = sub_cols // 2
    modes = pm_ref[...]
    for e, k in enumerate((0, last)):
        halo_ref = (before_ref, after_ref)[e]
        halo_strip = (sub_rows, -1)[e]
        turn = (slot_of(k, 0) - slot_of(halo_strip, 0)) % 3
        order = [None] * 3
        for s in range(sensors):
            order[slot_of(k, s)] = s
        both = halo_ref[2]
        for h in range(2):
            lines = both if h == 0 else pltpu.roll(both, HALF, axis=1)
            plain = edge_ref[e, h, 0] + rotate(halo_ref[h], turn, cols)
            lines = edge_ref[e, h, 1] + rotate(lines, turn, cols)
            modes = modes + jnp.dot(
                slope_terms(plain, lines, em_ref[e, h]),
                stacked(modes_ref, [None if s is None else (s, k) for s in order], h, cols),
                preferred_element_type=jnp.float32,
            )
    frame = lax.broadcasted_iota(jnp.int32, (frames, 1), 0)
    live = (frame < live_ref[0]).astype(jnp.float32)
    info = gain_ref[...] * modes * live
    own = lane_iota(frames) == lax.broadcasted_iota(jnp.int32, (frames, LANES), 0)
    counts = jnp.sum(jnp.where(own, count_ref[...] * live, 0.0), axis=0, keepdims=True)
    share = modes.shape[1] // tiles
    pack = LANES // share
    rows = frames // pack
    pad = jnp.zeros((out_ref.shape[1] - rows - 1, LANES), jnp.float32)
    for t in range(tiles):
        piece = jnp.concatenate(
            [info[g * rows : (g + 1) * rows, t * share : (t + 1) * share] for g in range(pack)], axis=1
        )
        piece = jnp.concatenate([piece, counts, pad], axis=0)
        for b in range(blocks):
            out_ref[t * blocks + b] = piece


def shifted(x, by, fill, back):
    rows = x.shape[0]
    if by % 8 == 0:
        pad = jnp.full((by, x.shape[1]), fill, x.dtype)
        if back:
            return jnp.concatenate([x[by:], pad], axis=0)
        return jnp.concatenate([pad, x[: rows - by]], axis=0)
    row = lax.broadcasted_iota(jnp.int32, (rows, 1), 0)
    if back:
        return jnp.where(row < rows - by, pltpu.roll(x, rows - by, axis=0), fill)
    return jnp.where(row >= by, pltpu.roll(x, by, axis=0), fill)


def kernel_smooth(
    tiles, blocks, frames, total_subaps, in_ref, noise_ref, gain_ref, mean_ref, var_ref, mean_scr, var_scr
):
    share = mean_ref.shape[1]
    total = blocks * frames
    tile = lax.axis_index("tile")
    time = lax.axis_index("tm")
    pack = LANES // share
    rows = frames // pack

    def own_modes(v):
        out = v[:, 0:share]
        for t in range(1, tiles):
            out = jnp.where(tile == t, v[:, t * share : (t + 1) * share], out)
        return out

    q = own_modes(noise_ref[...])
    gain = own_modes(gain_ref[...])
    own = lane_iota(frames) == lax.broadcasted_iota(jnp.int32, (frames, LANES), 0)
    infos = []
    counts = []
    for b in range(blocks):
        v = in_ref[b]
        for t in range(1, tiles):
            v = v + in_ref[t * blocks + b]
        for g in range(pack):
            infos.append(v[0:rows, g * share : (g + 1) * share])
        counts.append(jnp.sum(jnp.where(own, v[rows : rows + 1], 0.0), axis=1, keepdims=True))
    info_mean = jnp.concatenate(infos, axis=0)
    prec = gain * jnp.concatenate(counts, axis=0) / total_subaps
    row = lax.broadcasted_iota(jnp.int32, (total, 1), 0)
    first = row == 0
    retain = 1.0 / (1.0 + q * prec)
    a = jnp.where(first, 0.0, retain)
    c = jnp.where(first, 1.0 / (1.0 + prec), q * retain)
    b = c * info_mean
    e = a * info_mean
    j = a * prec
    by = 1
    while by < total:
        a1 = shifted(a, by, 1.0, False)
        b1 = shifted(b, by, 0.0, False)
        c1 = shifted(c, by, 0.0, False)
        e1 = shifted(e, by, 0.0, False)
        j1 = shifted(j, by, 0.0, False)
        damp = 1.0 / (1.0 + c1 * j)
        left = a * damp
        right = a1 * damp
        b = left * (b1 + c1 * e) + b
        c = left * a * c1 + c
        e, j = right * (e - j * b1) + e1, right * a1 * j + j1
        a = left * a1
        by *= 2
    g = jnp.where(row == total - 1, 0.0, c / (c + q))
    m = (1.0 - g) * b
    v = c * (1.0 - g)
    by = 1
    while by < total:
        g1 = shifted(g, by, 1.0, True)
        m1 = shifted(m, by, 0.0, True)
        v1 = shifted(v, by, 0.0, True)
        m = g * m1 + m
        v = g * g * v1 + v
        g = g * g1
        by *= 2
    mean_scr[...] = m
    var_scr[...] = v
    start = pl.multiple_of(time * frames, 8)
    mean_ref[...] = mean_scr[pl.ds(start, frames), :]
    var_ref[...] = var_scr[pl.ds(start, frames), :]


def body(pixels, offsets, mask, frame_count, slope_to_modes, process_noise, mode_gain):
    sensors, frames, lines, width = pixels.shape
    sub_rows, sub_cols = mask.shape[2], mask.shape[3]
    modes = process_noise.shape[0]
    tiles = lax.axis_size("tile")
    blocks = lax.axis_size("tm")
    share = modes // tiles
    total_subaps = sensors * sub_rows * tiles * sub_cols
    f32 = jnp.float32
    bf16 = jnp.bfloat16
    x = jnp.transpose(pixels, (0, 2, 1, 3)).reshape(sensors, lines * frames, width)
    off = jnp.transpose(offsets, (0, 1, 3, 2))
    msk = jnp.transpose(mask, (0, 2, 1, 3))
    x, off, msk, slope_to_modes = (
        pltpu.with_memory_space_constraint(v, pltpu.HBM) for v in (x, off, msk, slope_to_modes)
    )
    block = SIDE * frames
    inner = sub_rows - 2
    depth = max(half_columns(h, sub_cols, width)[1] for h in range(2))
    params = pltpu.CompilerParams(vmem_limit_bytes=VMEM_LIMIT)

    def cost(chunks):
        return pl.CostEstimate(
            flops=2 * chunks * block * width * 256, bytes_accessed=chunks * block * width * 2, transcendentals=0
        )

    up, down, parts, geo, buf, mask_v, modes_v = pl.pallas_call(
        functools.partial(kernel_edge, sub_rows, sub_cols, frames),
        out_shape=(
            jax.ShapeDtypeStruct((3, frames, LANES), f32),
            jax.ShapeDtypeStruct((3, frames, LANES), f32),
            pltpu.VMEM((sensors, 2, 2, 2, frames, LANES), f32),
            pltpu.VMEM((sensors, sub_rows, 8, LANES), f32),
            pltpu.VMEM((sensors, sub_rows, block, width), bf16),
            pltpu.VMEM(msk.shape, msk.dtype),
            pltpu.VMEM(slope_to_modes.shape, bf16),
        ),
        in_specs=[HBM] * 4,
        out_specs=(VMEM,) * 7,
        scratch_shapes=[
            pltpu.VMEM((2, 2, depth, LANES), bf16),
            pltpu.VMEM(off.shape, off.dtype),
            pltpu.SemaphoreType.DMA((sensors, sub_rows)),
            pltpu.SemaphoreType.DMA((3,)),
        ],
        compiler_params=params,
        cost_estimate=cost(2 * sensors),
        name="edge_moments",
    )(x, off, msk, slope_to_modes)
    onward = [(i, i + 1) for i in range(tiles - 1)]
    backward = [(j, i) for i, j in onward]
    from_before = lax.ppermute(up, "tile", onward)
    from_after = lax.ppermute(down, "tile", backward)
    partial_modes, edge, edge_mask, count = pl.pallas_call(
        functools.partial(kernel_inner, sub_rows, sub_cols, frames),
        out_shape=(
            pltpu.VMEM((frames, modes), f32),
            pltpu.VMEM((2, 2, 2, frames, LANES), f32),
            pltpu.VMEM((2, 2, frames, LANES), f32),
            pltpu.VMEM((frames, LANES), f32),
        ),
        in_specs=[VMEM] * 5,
        out_specs=(VMEM,) * 4,
        scratch_shapes=[
            pltpu.VMEM((inner, 2, depth, LANES), bf16),
            pltpu.VMEM((sensors, inner, 2, 2, frames, LANES), f32),
        ],
        compiler_params=params,
        cost_estimate=cost(inner * sensors),
        name="inner_moments",
    )(buf, geo, parts, mask_v, modes_v)
    gain = mode_gain.reshape(1, modes)
    packed = -(-(frames * share // LANES + 1) // 8) * 8
    payload = pl.pallas_call(
        functools.partial(kernel_join, sub_rows, sub_cols, frames, tiles, blocks),
        out_shape=jax.ShapeDtypeStruct((tiles * blocks, packed, LANES), f32),
        in_specs=[pl.BlockSpec(memory_space=pltpu.SMEM)] + [VMEM] * 8,
        out_specs=VMEM,
        compiler_params=params,
        name="join_halo",
    )(frame_count, from_before, from_after, partial_modes, edge, edge_mask, count, modes_v, gain)
    info = lax.all_to_all(payload, ("tile", "tm"), 0, 0)
    return pl.pallas_call(
        functools.partial(kernel_smooth, tiles, blocks, frames, float(total_subaps)),
        out_shape=(
            jax.ShapeDtypeStruct((frames, share), f32),
            jax.ShapeDtypeStruct((frames, share), f32),
        ),
        in_specs=[VMEM] * 3,
        out_specs=(VMEM, VMEM),
        scratch_shapes=[
            pltpu.VMEM((blocks * frames, share), f32),
            pltpu.VMEM((blocks * frames, share), f32),
        ],
        compiler_params=params,
        name="smooth",
    )(info, process_noise.reshape(1, modes), gain)


def solution(mesh):
    return jax.shard_map(
        body,
        mesh=mesh,
        in_specs=(
            P("grp", "tm", "tile", None),
            P("grp", None, None, None),
            P("grp", "tm", "tile", None),
            P(("grp", "tm")),
            P(None, None, "tile", None, None),
            P(),
            P(),
        ),
        out_specs=(P(("grp", "tm"), "tile"), P(("grp", "tm"), "tile")),
        check_vma=False,
    )
```

```python
import functools

import jax
import jax.numpy as jnp
from jax import lax
from jax.experimental import pallas as pl
from jax.experimental.pallas import tpu as pltpu
from jax.sharding import PartitionSpec as P

SIDE = 20
SHIFT = 6
CENTRE = (SIDE - 1) / 2.0
LANES = 128
HALF = LANES // 2
VMEM_LIMIT = 24 * 1024 * 1024
VMEM = pl.BlockSpec(memory_space=pltpu.VMEM)
HBM = pl.BlockSpec(memory_space=pl.ANY)


def slot_of(strip, sensor):
    return (strip + 1 + sensor) % 3


def half_columns(half, sub_cols, width):
    cols = sub_cols // 2
    first = max(0, half * cols * SIDE - SHIFT) // LANES * LANES
    end = min(width, -(-((half + 1) * cols * SIDE + SHIFT) // 16) * 16)
    return first, end - first


def lane_iota(rows=1):
    return lax.broadcasted_iota(jnp.int32, (rows, LANES), 1)


def half_lane(rows=1):
    lane = lane_iota(rows)
    return jnp.where(lane >= HALF, lane - HALF, lane)


def by_slot(values, cols):
    lane = half_lane()
    out = jnp.zeros_like(values[0])
    for q, v in enumerate(values):
        if v is not None:
            out = jnp.where((lane >= q * cols) & (lane < (q + 1) * cols), v, out)
    return out


def side_by_side(pieces):
    rows, cols = pieces[0].shape
    pad = jnp.zeros((rows, HALF - 3 * cols), pieces[0].dtype)
    return jnp.concatenate([*pieces, pad, *pieces, pad], axis=1)


def rotate(x, slots, cols):
    shift = slots * cols
    if shift == 0:
        return x
    near = pltpu.roll(x, shift, axis=1)
    far = pltpu.roll(x, LANES - 3 * cols + shift, axis=1)
    return jnp.where(half_lane() >= shift, near, far)


def geometry(geo_ref, off_ref, sensors, sub_rows, sub_cols, width):
    cols = sub_cols // 2
    lane = half_lane()
    index = lane - cols * (lane >= cols).astype(jnp.int32)
    index = index - cols * (lane >= 2 * cols).astype(jnp.int32)
    used = lane < 3 * cols
    tile = lax.axis_index("tile")
    total_rows = off_ref.shape[1]
    for s in range(sensors):
        spread_rows = []
        for k in range(-1, sub_rows + 1):
            row = jnp.clip(tile * sub_rows + k, 0, total_rows - 1)
            v = off_ref[s, row].astype(jnp.float32)
            spread_rows.append([side_by_side([v[:, h * cols : (h + 1) * cols]] * 3) for h in range(2)])
        for i in range(sub_rows):
            for h in range(2):
                first, _ = half_columns(h, sub_cols, width)
                col_base = (SIDE * (index + h * cols) - first).astype(jnp.float32) + CENTRE
                cs = [None] * 3
                rs = [None] * 3
                for k in (i - 1, i, i + 1):
                    q = slot_of(k, s)
                    v = spread_rows[k + 1][h]
                    cs[q] = v[1:2] + col_base
                    rs[q] = v[0:1] + (SIDE * (k - i) + CENTRE)
                geo_ref[s, i, 2 * h : 2 * h + 1, :] = jnp.where(used, by_slot(cs, cols), -1000.0)
                geo_ref[s, i, 2 * h + 1 : 2 * h + 2, :] = jnp.where(used, by_slot(rs, cols), -1000.0)


def build_weights(col_pos, w_ref):
    base = lax.broadcasted_iota(jnp.int32, (16, LANES), 0).astype(jnp.float32) - col_pos
    left = lane_iota(16) < HALF
    for t in range(w_ref.shape[0] // 16):
        d = base + float(16 * t)
        value = jnp.where(left, 1.0, d)
        w_ref[16 * t : 16 * t + 16, :] = jnp.where(jnp.abs(d) < 10.0, value, 0.0).astype(jnp.bfloat16)


def row_sums(row_pos, r, frames):
    plain = jnp.zeros((frames, LANES), jnp.float32)
    lines = jnp.zeros((frames, LANES), jnp.float32)
    for y in range(r.shape[0] // frames):
        d = float(y) - row_pos
        inside = jnp.abs(d) < 10.0
        one = jnp.where(inside, 1.0, 0.0)
        centred = jnp.where(inside, d, 0.0)
        piece = r[y * frames : (y + 1) * frames, :]
        plain = plain + one * piece
        lines = lines + centred * piece
    return plain, lines


def block_moments(x_ref, geo_ref, w_ref, p_ref, sub_cols, frames):
    count = len(x_ref)
    for n in range(count):
        for h in range(2):
            build_weights(geo_ref[n][2 * h : 2 * h + 1, :], w_ref.at[n, h])
    for n in range(count):
        for h in range(2):
            first, size = half_columns(h, sub_cols, x_ref[n].shape[1])
            r = jnp.dot(
                x_ref[n][:, first : first + size],
                w_ref[n, h, 0:size, :],
                preferred_element_type=jnp.float32,
            )
            plain, lines = row_sums(geo_ref[n][2 * h + 1 : 2 * h + 2, :], r, frames)
            p_ref[n][h, 0] = plain
            p_ref[n][h, 1] = lines


def kernel_edge(
    sub_rows, sub_cols, frames, x_hbm, off_hbm, mask_hbm, frames_ref, modes_hbm,
    up_ref, down_ref, p_ref, geo_ref, mask_ref, live_ref, modes_ref, ahead_ref,
    buf, w_ref, off_ref, sem, side_sem,
):
    sensors = x_hbm.shape[0]
    block = SIDE * frames
    last = sub_rows - 1
    cols = sub_cols // 2

    def copy(s, e):
        return pltpu.make_async_copy(
            x_hbm.at[s, pl.ds(e * last * block, block)], buf.at[s, e], sem.at[s, e]
        )

    off_copy = pltpu.make_async_copy(off_hbm, off_ref, side_sem.at[0])
    mask_copy = pltpu.make_async_copy(mask_hbm, mask_ref, side_sem.at[1])
    modes_copy = pltpu.make_async_copy(modes_hbm, modes_ref, side_sem.at[2])
    ahead_copy = pltpu.make_async_copy(
        x_hbm.at[0, pl.ds(block, ahead_ref.shape[0])], ahead_ref, side_sem.at[3]
    )
    off_copy.start()
    for s in range(sensors):
        for e in range(2):
            copy(s, e).start()
    ahead_copy.start()
    mask_copy.start()
    modes_copy.start()
    off_copy.wait()
    geometry(geo_ref, off_ref, sensors, sub_rows, sub_cols, x_hbm.shape[2])

    def step(s, carry):
        copy(s, 0).wait()
        copy(s, 1).wait()
        block_moments(
            [buf.at[s, 0], buf.at[s, 1]],
            [geo_ref.at[s, 0], geo_ref.at[s, last]],
            w_ref,
            [p_ref.at[s, 0], p_ref.at[s, 1]],
            sub_cols,
            frames,
        )
        return carry

    lax.fori_loop(0, sensors, step, 0)
    left = lane_iota() < HALF
    for ref, e, strip in ((down_ref, 0, -1), (up_ref, 1, sub_rows)):
        pair = []
        for h in range(2):
            both = []
            for a in range(2):
                order = [None] * 3
                for s in range(sensors):
                    order[slot_of(strip, s)] = p_ref[s, e, h, a]
                both.append(by_slot(order, cols))
            ref[h] = both[0]
            pair.append(both[1])
        ref[2] = jnp.where(left, pair[0], pltpu.roll(pair[1], HALF, axis=1))
    frame = lax.broadcasted_iota(jnp.int32, (frames, LANES), 0)
    live_ref[...] = (frame < frames_ref[0]).astype(jnp.float32)
    ahead_copy.wait()
    mask_copy.wait()
    modes_copy.wait()


def slope_terms(plain, lines, mask):
    left = lane_iota() < HALF
    live = mask > 0.0
    flux = jnp.where(left, plain, pltpu.roll(plain, HALF, axis=1))
    moment = jnp.where(left, lines, plain)
    return jnp.where(live, moment / jnp.where(live, flux, 1.0) * mask, 0.0).astype(jnp.bfloat16)


def stacked(modes_ref, picks, half, cols):
    parts = []
    for x in (1, 0):
        used = 0
        for pick in picks:
            if pick is None:
                parts.append(jnp.zeros((cols, modes_ref.shape[-1]), jnp.float32))
            else:
                s, k = pick
                rows = modes_ref[x, s, k].astype(jnp.float32)
                parts.append(rows[half * cols : (half + 1) * cols])
            used += cols
        parts.append(jnp.zeros((HALF - used, modes_ref.shape[-1]), jnp.float32))
    return jnp.concatenate(parts, axis=0).astype(jnp.bfloat16)


def kernel_inner(
    sub_rows, sub_cols, frames, ahead, x_hbm, ahead_ref, geo_ref, pe_ref, mask_ref, modes_ref,
    pm_ref, edge_ref, em_ref, count_ref, buf, w_ref, p_ref, sem,
):
    sensors = x_hbm.shape[0]
    block = SIDE * frames
    last = sub_rows - 1
    cols = sub_cols // 2

    def copy(s, i):
        return pltpu.make_async_copy(
            x_hbm.at[s, pl.ds(i * block, block)], buf.at[s, i - 1], sem.at[s, i - 1]
        )

    def done(s, i):
        return s == 0 and i <= ahead

    for s in range(sensors):
        for i in range(1, last):
            if not done(s, i):
                copy(s, i).start()
    for s in range(sensors):
        for i in range(1, last):
            if done(s, i):
                pixels = ahead_ref.at[(i - 1) * block : i * block]
            else:
                copy(s, i).wait()
                pixels = buf.at[s, i - 1]
            block_moments(
                [pixels], [geo_ref.at[s, i]], w_ref.at[pl.ds(i - 1, 1)], [p_ref.at[s, i - 1]], sub_cols, frames
            )

    def partial(s, i, h, a):
        if i == 0:
            return pe_ref[s, 0, h, a]
        if i == last:
            return pe_ref[s, 1, h, a]
        return p_ref[s, i - 1, h, a]

    def strip_total(s, k, h, a):
        total = None
        for i in (k - 1, k, k + 1):
            if 0 <= i <= last:
                v = partial(s, i, h, a)
                total = v if total is None else total + v
        return total

    def mask_of(s, k, h):
        return mask_ref[s, k].astype(jnp.float32)[:, h * cols : (h + 1) * cols]

    count = jnp.zeros((frames, LANES), jnp.float32)
    for e, k in enumerate((0, last)):
        order = [None] * 3
        for s in range(sensors):
            order[slot_of(k, s)] = s
        for h in range(2):
            m = side_by_side([mask_of(s, k, h) for s in order])
            em_ref[e, h] = m
            count = count + m
            for a in range(2):
                edge_ref[e, h, a] = by_slot([strip_total(s, k, h, a) for s in order], cols)
    modes = jnp.zeros((frames, modes_ref.shape[-1]), jnp.float32)
    for s in range(sensors):
        for g in range(1, last, 3):
            order = [None] * 3
            for k in range(g, min(g + 3, last)):
                order[slot_of(k, s)] = k
            for h in range(2):
                none = jnp.zeros((frames, cols), jnp.float32)
                mask = side_by_side([none if k is None else mask_of(s, k, h) for k in order])
                count = count + mask
                plain, lines = (
                    by_slot([None if k is None else strip_total(s, k, h, a) for k in order], cols)
                    for a in range(2)
                )
                modes = modes + jnp.dot(
                    slope_terms(plain, lines, mask),
                    stacked(modes_ref, [None if k is None else (s, k) for k in order], h, cols),
                    preferred_element_type=jnp.float32,
                )
    pm_ref[...] = modes
    count_ref[...] = jnp.broadcast_to(0.5 * jnp.sum(count, axis=1, keepdims=True), count_ref.shape)


def kernel_join(
    sub_rows, sub_cols, frames, tiles,
    live_ref, before_ref, after_ref, pm_ref, edge_ref, em_ref, count_ref, modes_ref, gain_ref, out_ref,
):
    sensors = modes_ref.shape[1]
    last = sub_rows - 1
    cols = sub_cols // 2
    modes = pm_ref[...]
    for e, k in enumerate((0, last)):
        halo_ref = (before_ref, after_ref)[e]
        halo_strip = (sub_rows, -1)[e]
        turn = (slot_of(k, 0) - slot_of(halo_strip, 0)) % 3
        order = [None] * 3
        for s in range(sensors):
            order[slot_of(k, s)] = s
        both = halo_ref[2]
        for h in range(2):
            lines = both if h == 0 else pltpu.roll(both, HALF, axis=1)
            plain = edge_ref[e, h, 0] + rotate(halo_ref[h], turn, cols)
            lines = edge_ref[e, h, 1] + rotate(lines, turn, cols)
            modes = modes + jnp.dot(
                slope_terms(plain, lines, em_ref[e, h]),
                stacked(modes_ref, [None if s is None else (s, k) for s in order], h, cols),
                preferred_element_type=jnp.float32,
            )
    live = live_ref[...]
    info = gain_ref[...] * modes * jnp.concatenate([live] * (modes.shape[1] // LANES), axis=1)
    own = lane_iota(frames) == lax.broadcasted_iota(jnp.int32, (frames, LANES), 0)
    counts = jnp.sum(jnp.where(own, count_ref[...] * live, 0.0), axis=0, keepdims=True)
    share = modes.shape[1] // tiles
    pack = LANES // share
    rows = frames // pack
    pad = jnp.zeros((out_ref.shape[1] - rows - 1, LANES), jnp.float32)
    for t in range(tiles):
        piece = jnp.concatenate(
            [info[g * rows : (g + 1) * rows, t * share : (t + 1) * share] for g in range(pack)], axis=1
        )
        piece = jnp.concatenate([piece, counts, pad], axis=0)
        out_ref[t] = piece


def kernel_sum(blocks, in_ref, out_ref):
    total = in_ref[0]
    for t in range(1, in_ref.shape[0]):
        total = total + in_ref[t]
    for b in range(blocks):
        out_ref[b] = total


def shifted(x, by, fill, back):
    rows = x.shape[0]
    if by % 8 == 0:
        pad = jnp.full((by, x.shape[1]), fill, x.dtype)
        if back:
            return jnp.concatenate([x[by:], pad], axis=0)
        return jnp.concatenate([pad, x[: rows - by]], axis=0)
    row = lax.broadcasted_iota(jnp.int32, (rows, 1), 0)
    if back:
        return jnp.where(row < rows - by, pltpu.roll(x, rows - by, axis=0), fill)
    return jnp.where(row >= by, pltpu.roll(x, by, axis=0), fill)


def kernel_smooth(
    tiles, blocks, frames, total_subaps, in_ref, noise_ref, gain_ref, mean_ref, var_ref, mean_scr, var_scr
):
    share = mean_ref.shape[1]
    total = blocks * frames
    tile = lax.axis_index("tile")
    time = lax.axis_index("tm")
    pack = LANES // share
    rows = frames // pack

    def own_modes(v):
        out = v[:, 0:share]
        for t in range(1, tiles):
            out = jnp.where(tile == t, v[:, t * share : (t + 1) * share], out)
        return out

    q = own_modes(noise_ref[...])
    gain = own_modes(gain_ref[...])
    own = lane_iota(frames) == lax.broadcasted_iota(jnp.int32, (frames, LANES), 0)
    infos = []
    counts = []
    for b in range(blocks):
        v = in_ref[b]
        for g in range(pack):
            infos.append(v[0:rows, g * share : (g + 1) * share])
        counts.append(jnp.sum(jnp.where(own, v[rows : rows + 1], 0.0), axis=1, keepdims=True))
    info_mean = jnp.concatenate(infos, axis=0)
    prec = gain * jnp.concatenate(counts, axis=0) / total_subaps
    row = lax.broadcasted_iota(jnp.int32, (total, 1), 0)
    first = row == 0
    retain = 1.0 / (1.0 + q * prec)
    a = jnp.where(first, 0.0, retain)
    c = jnp.where(first, 1.0 / (1.0 + prec), q * retain)
    b = c * info_mean
    e = a * info_mean
    j = a * prec
    by = 1
    while by < total:
        a1 = shifted(a, by, 1.0, False)
        b1 = shifted(b, by, 0.0, False)
        c1 = shifted(c, by, 0.0, False)
        e1 = shifted(e, by, 0.0, False)
        j1 = shifted(j, by, 0.0, False)
        damp = 1.0 / (1.0 + c1 * j)
        left = a * damp
        right = a1 * damp
        b = left * (b1 + c1 * e) + b
        c = left * a * c1 + c
        e, j = right * (e - j * b1) + e1, right * a1 * j + j1
        a = left * a1
        by *= 2
    g = jnp.where(row == total - 1, 0.0, c / (c + q))
    m = (1.0 - g) * b
    v = c * (1.0 - g)
    by = 1
    while by < total:
        g1 = shifted(g, by, 1.0, True)
        m1 = shifted(m, by, 0.0, True)
        v1 = shifted(v, by, 0.0, True)
        m = g * m1 + m
        v = g * g * v1 + v
        g = g * g1
        by *= 2
    mean_scr[...] = m
    var_scr[...] = v
    start = pl.multiple_of(time * frames, 8)
    mean_ref[...] = mean_scr[pl.ds(start, frames), :]
    var_ref[...] = var_scr[pl.ds(start, frames), :]


def body(pixels, offsets, mask, frame_count, slope_to_modes, process_noise, mode_gain):
    sensors, frames, lines, width = pixels.shape
    sub_rows, sub_cols = mask.shape[2], mask.shape[3]
    modes = process_noise.shape[0]
    tiles = lax.axis_size("tile")
    blocks = lax.axis_size("tm")
    share = modes // tiles
    total_subaps = sensors * sub_rows * tiles * sub_cols
    f32 = jnp.float32
    bf16 = jnp.bfloat16
    x = jnp.transpose(pixels, (0, 2, 1, 3)).reshape(sensors, lines * frames, width)
    off = jnp.transpose(offsets, (0, 1, 3, 2))
    msk = jnp.transpose(mask, (0, 2, 1, 3))
    block = SIDE * frames
    x, off, msk, slope_to_modes = (
        pltpu.with_memory_space_constraint(v, pltpu.HBM) for v in (x, off, msk, slope_to_modes)
    )
    inner = sub_rows - 2
    ahead = min(2, inner)
    depth = max(half_columns(h, sub_cols, width)[1] for h in range(2))
    params = pltpu.CompilerParams(vmem_limit_bytes=VMEM_LIMIT)

    def cost(chunks):
        return pl.CostEstimate(
            flops=2 * chunks * block * width * 256, bytes_accessed=chunks * block * width * 2, transcendentals=0
        )

    up, down, parts, geo, mask_v, live, modes_v, pixels_ahead = pl.pallas_call(
        functools.partial(kernel_edge, sub_rows, sub_cols, frames),
        out_shape=(
            jax.ShapeDtypeStruct((3, frames, LANES), f32),
            jax.ShapeDtypeStruct((3, frames, LANES), f32),
            pltpu.VMEM((sensors, 2, 2, 2, frames, LANES), f32),
            pltpu.VMEM((sensors, sub_rows, 8, LANES), f32),
            pltpu.VMEM(msk.shape, msk.dtype),
            pltpu.VMEM((frames, LANES), f32),
            pltpu.VMEM(slope_to_modes.shape, bf16),
            pltpu.VMEM((ahead * block, width), bf16),
        ),
        in_specs=[HBM, HBM, HBM, pl.BlockSpec(memory_space=pltpu.SMEM), HBM],
        out_specs=(VMEM,) * 8,
        scratch_shapes=[
            pltpu.VMEM((sensors, 2, block, width), bf16),
            pltpu.VMEM((2, 2, depth, LANES), bf16),
            pltpu.VMEM(off.shape, off.dtype),
            pltpu.SemaphoreType.DMA((sensors, 2)),
            pltpu.SemaphoreType.DMA((4,)),
        ],
        compiler_params=params,
        cost_estimate=cost(2 * sensors),
        name="edge_moments",
    )(x, off, msk, frame_count, slope_to_modes)
    onward = [(i, i + 1) for i in range(tiles - 1)]
    backward = [(j, i) for i, j in onward]
    from_before = lax.ppermute(up, "tile", onward)
    from_after = lax.ppermute(down, "tile", backward)
    partial_modes, edge, edge_mask, count = pl.pallas_call(
        functools.partial(kernel_inner, sub_rows, sub_cols, frames, ahead),
        out_shape=(
            pltpu.VMEM((frames, modes), f32),
            pltpu.VMEM((2, 2, 2, frames, LANES), f32),
            pltpu.VMEM((2, 2, frames, LANES), f32),
            pltpu.VMEM((frames, LANES), f32),
        ),
        in_specs=[HBM] + [VMEM] * 5,
        out_specs=(VMEM,) * 4,
        scratch_shapes=[
            pltpu.VMEM((sensors, inner, block, width), bf16),
            pltpu.VMEM((inner, 2, depth, LANES), bf16),
            pltpu.VMEM((sensors, inner, 2, 2, frames, LANES), f32),
            pltpu.SemaphoreType.DMA((sensors, inner)),
        ],
        compiler_params=params,
        cost_estimate=cost(inner * sensors),
        name="inner_moments",
    )(x, pixels_ahead, geo, parts, mask_v, modes_v)
    gain = mode_gain.reshape(1, modes)
    packed = -(-(frames * share // LANES + 1) // 8) * 8
    payload = pl.pallas_call(
        functools.partial(kernel_join, sub_rows, sub_cols, frames, tiles),
        out_shape=jax.ShapeDtypeStruct((tiles, packed, LANES), f32),
        in_specs=[VMEM] * 9,
        out_specs=VMEM,
        compiler_params=params,
        name="join_halo",
    )(live, from_before, from_after, partial_modes, edge, edge_mask, count, modes_v, gain)
    own_share = lax.all_to_all(payload, "tile", 0, 0)
    summed = pl.pallas_call(
        functools.partial(kernel_sum, blocks),
        out_shape=jax.ShapeDtypeStruct((blocks, packed, LANES), f32),
        in_specs=[VMEM],
        out_specs=VMEM,
        compiler_params=params,
        name="sum_tiles",
    )(own_share)
    info = lax.all_to_all(summed, "tm", 0, 0)
    return pl.pallas_call(
        functools.partial(kernel_smooth, tiles, blocks, frames, float(total_subaps)),
        out_shape=(
            jax.ShapeDtypeStruct((frames, share), f32),
            jax.ShapeDtypeStruct((frames, share), f32),
        ),
        in_specs=[VMEM] * 3,
        out_specs=(VMEM, VMEM),
        scratch_shapes=[
            pltpu.VMEM((blocks * frames, share), f32),
            pltpu.VMEM((blocks * frames, share), f32),
        ],
        compiler_params=params,
        name="smooth",
    )(info, process_noise.reshape(1, modes), gain)


def solution(mesh):
    return jax.shard_map(
        body,
        mesh=mesh,
        in_specs=(
            P("grp", "tm", "tile", None),
            P("grp", None, None, None),
            P("grp", "tm", "tile", None),
            P(("grp", "tm")),
            P(None, None, "tile", None, None),
            P(),
            P(),
        ),
        out_specs=(P(("grp", "tm"), "tile"), P(("grp", "tm"), "tile")),
        check_vma=False,
    )
```

```python
import functools

import jax
import jax.numpy as jnp
from jax import lax
from jax.experimental import pallas as pl
from jax.experimental.pallas import tpu as pltpu
from jax.sharding import PartitionSpec as P

SIDE = 20
SHIFT = 6
CENTRE = (SIDE - 1) / 2.0
LANES = 128
HALF = LANES // 2
VMEM_LIMIT = 24 * 1024 * 1024
VMEM = pl.BlockSpec(memory_space=pltpu.VMEM)
HBM = pl.BlockSpec(memory_space=pl.ANY)


def slot_of(strip, sensor):
    return (strip + 1 + sensor) % 3


def half_columns(half, sub_cols, width):
    cols = sub_cols // 2
    first = max(0, half * cols * SIDE - SHIFT) // LANES * LANES
    end = min(width, -(-((half + 1) * cols * SIDE + SHIFT) // 16) * 16)
    return first, end - first


def lane_iota(rows=1):
    return lax.broadcasted_iota(jnp.int32, (rows, LANES), 1)


def half_lane(rows=1):
    lane = lane_iota(rows)
    return jnp.where(lane >= HALF, lane - HALF, lane)


def by_slot(values, cols):
    lane = half_lane()
    out = jnp.zeros_like(values[0])
    for q, v in enumerate(values):
        if v is not None:
            out = jnp.where((lane >= q * cols) & (lane < (q + 1) * cols), v, out)
    return out


def side_by_side(pieces):
    rows, cols = pieces[0].shape
    pad = jnp.zeros((rows, HALF - 3 * cols), pieces[0].dtype)
    return jnp.concatenate([*pieces, pad, *pieces, pad], axis=1)


def rotate(x, slots, cols):
    shift = slots * cols
    if shift == 0:
        return x
    near = pltpu.roll(x, shift, axis=1)
    far = pltpu.roll(x, LANES - 3 * cols + shift, axis=1)
    return jnp.where(half_lane() >= shift, near, far)


def geometry(geo_ref, off_ref, sensors, sub_rows, sub_cols, width):
    cols = sub_cols // 2
    lane = half_lane()
    index = lane - cols * (lane >= cols).astype(jnp.int32)
    index = index - cols * (lane >= 2 * cols).astype(jnp.int32)
    used = lane < 3 * cols
    tile = lax.axis_index("tile")
    total_rows = off_ref.shape[1]
    for s in range(sensors):
        spread_rows = []
        for k in range(-1, sub_rows + 1):
            row = jnp.clip(tile * sub_rows + k, 0, total_rows - 1)
            v = off_ref[s, row].astype(jnp.float32)
            spread_rows.append([side_by_side([v[:, h * cols : (h + 1) * cols]] * 3) for h in range(2)])
        for i in range(sub_rows):
            for h in range(2):
                first, _ = half_columns(h, sub_cols, width)
                col_base = (SIDE * (index + h * cols) - first).astype(jnp.float32) + CENTRE
                cs = [None] * 3
                rs = [None] * 3
                for k in (i - 1, i, i + 1):
                    q = slot_of(k, s)
                    v = spread_rows[k + 1][h]
                    cs[q] = v[1:2] + col_base
                    rs[q] = v[0:1] + (SIDE * (k - i) + CENTRE)
                geo_ref[s, i, 2 * h : 2 * h + 1, :] = jnp.where(used, by_slot(cs, cols), -1000.0)
                geo_ref[s, i, 2 * h + 1 : 2 * h + 2, :] = jnp.where(used, by_slot(rs, cols), -1000.0)


def build_weights(col_pos, w_ref):
    base = lax.broadcasted_iota(jnp.int32, (16, LANES), 0).astype(jnp.float32) - col_pos
    left = lane_iota(16) < HALF
    for t in range(w_ref.shape[0] // 16):
        d = base + float(16 * t)
        value = jnp.where(left, 1.0, d)
        w_ref[16 * t : 16 * t + 16, :] = jnp.where(jnp.abs(d) < 10.0, value, 0.0).astype(jnp.bfloat16)


def row_sums(row_pos, r, frames):
    plain = jnp.zeros((frames, LANES), jnp.float32)
    lines = jnp.zeros((frames, LANES), jnp.float32)
    for y in range(r.shape[0] // frames):
        d = float(y) - row_pos
        inside = jnp.abs(d) < 10.0
        one = jnp.where(inside, 1.0, 0.0)
        centred = jnp.where(inside, d, 0.0)
        piece = r[y * frames : (y + 1) * frames, :]
        plain = plain + one * piece
        lines = lines + centred * piece
    return plain, lines


def block_moments(pixels, row_pos, w_ref, p_ref, sub_cols, frames):
    for h in range(2):
        first, size = half_columns(h, sub_cols, pixels.shape[1])
        r = jnp.dot(
            pixels[:, first : first + size], w_ref[h, 0:size, :], preferred_element_type=jnp.float32
        )
        plain, lines = row_sums(row_pos[h], r, frames)
        p_ref[h, 0] = plain
        p_ref[h, 1] = lines


def block_weights(geo_ref, w_ref):
    for h in range(2):
        build_weights(geo_ref[2 * h : 2 * h + 1, :], w_ref.at[h])


def row_positions(geo_ref):
    return [geo_ref[2 * h + 1 : 2 * h + 2, :] for h in range(2)]


def strip_total(p_ref, s, k, h, a):
    total = None
    for i in (k - 1, k, k + 1):
        if 0 <= i < p_ref.shape[1]:
            v = p_ref[s, i, h, a]
            total = v if total is None else total + v
    return total


def mask_of(mask_ref, s, k, h):
    cols = mask_ref.shape[3] // 2
    return mask_ref[s, k].astype(jnp.float32)[:, h * cols : (h + 1) * cols]


def inner_projection(p_ref, mask_ref, modes_ref, s):
    last = p_ref.shape[1] - 1
    frames, sub_cols = mask_ref.shape[2:]
    cols = sub_cols // 2
    modes = jnp.zeros((frames, modes_ref.shape[-1]), jnp.float32)
    count = jnp.zeros((frames, LANES), jnp.float32)
    none = jnp.zeros((frames, cols), jnp.float32)
    for g in range(1, last, 3):
        order = [None] * 3
        for k in range(g, min(g + 3, last)):
            order[slot_of(k, s)] = k
        for h in range(2):
            mask = side_by_side([none if k is None else mask_of(mask_ref, s, k, h) for k in order])
            count = count + mask
            plain, lines = (
                by_slot([None if k is None else strip_total(p_ref, s, k, h, a) for k in order], cols)
                for a in range(2)
            )
            modes = modes + jnp.dot(
                slope_terms(plain, lines, mask),
                stacked(modes_ref, [None if k is None else (s, k) for k in order], h, cols),
                preferred_element_type=jnp.float32,
            )
    return modes, count


def kernel_first(
    sub_rows, sub_cols, frames, x_hbm, off_hbm, mask_hbm, modes_hbm,
    up_ref, down_ref, p_ref, geo_ref, mask_ref, modes_ref, ahead_ref, pm_ref, count_ref,
    buf, edge_buf, w_ref, off_ref, sem, side_sem,
):
    sensors = x_hbm.shape[0]
    block = SIDE * frames
    piece = block // 2
    last = sub_rows - 1
    cols = sub_cols // 2
    final = sensors - 1
    order = (0, last, *range(1, last))

    def place(s, i):
        if isinstance(s, int) and s == final:
            return ahead_ref.at[i - 1] if 0 < i < last else edge_buf.at[min(i, 1)]
        return buf.at[s, i]

    def copies(s, i):
        return [
            pltpu.make_async_copy(
                x_hbm.at[s, pl.ds(i * block + z * piece, piece)],
                place(s, i).at[pl.ds(z * piece, piece)],
                sem.at[s, i, z],
            )
            for z in range(2)
        ]

    def wait(s, i):
        for c in copies(s, i):
            c.wait()

    off_copy = pltpu.make_async_copy(off_hbm, off_ref, side_sem.at[0])
    mask_copy = pltpu.make_async_copy(mask_hbm, mask_ref, side_sem.at[1])
    modes_copy = pltpu.make_async_copy(modes_hbm, modes_ref, side_sem.at[2])
    off_copy.start()
    for s in range(sensors):
        for i in order:
            for c in copies(s, i):
                c.start()
        if s == 0:
            mask_copy.start()
            modes_copy.start()
    off_copy.wait()
    geometry(geo_ref, off_ref, sensors, sub_rows, sub_cols, x_hbm.shape[2])
    block_weights(geo_ref.at[0, order[0]], w_ref.at[0])

    def step(s, carry):
        for n, i in enumerate(order):
            wait(s, i)
            after = (s, order[n + 1]) if n + 1 < sub_rows else (s + 1, order[0])
            block_weights(geo_ref.at[after], w_ref.at[(n + 1) % sub_rows])
            block_moments(
                buf.at[s, i], row_positions(geo_ref.at[s, i]), w_ref.at[n], p_ref.at[s, i], sub_cols, frames
            )
        return carry

    lax.fori_loop(0, final, step, 0)
    mask_copy.wait()
    modes_copy.wait()
    modes = jnp.zeros(pm_ref.shape, jnp.float32)
    count = jnp.zeros(count_ref.shape, jnp.float32)
    for s in range(final):
        part, number = inner_projection(p_ref, mask_ref, modes_ref, s)
        modes = modes + part
        count = count + number
    pm_ref[...] = modes
    count_ref[...] = count
    block_weights(geo_ref.at[final, last], w_ref.at[1])
    for n, i in enumerate((0, last)):
        wait(final, i)
        block_moments(
            place(final, i), row_positions(geo_ref.at[final, i]), w_ref.at[n], p_ref.at[final, i], sub_cols, frames
        )
    left = lane_iota() < HALF
    for ref, i, strip in ((down_ref, 0, -1), (up_ref, last, sub_rows)):
        pair = []
        for h in range(2):
            both = []
            for a in range(2):
                pieces = [None] * 3
                for s in range(sensors):
                    pieces[slot_of(strip, s)] = p_ref[s, i, h, a]
                both.append(by_slot(pieces, cols))
            ref[h] = both[0]
            pair.append(both[1])
        ref[2] = jnp.where(left, pair[0], pltpu.roll(pair[1], HALF, axis=1))
    for i in range(1, last):
        wait(final, i)


def slope_terms(plain, lines, mask):
    left = lane_iota() < HALF
    live = mask > 0.0
    flux = jnp.where(left, plain, pltpu.roll(plain, HALF, axis=1))
    moment = jnp.where(left, lines, plain)
    return jnp.where(live, moment / jnp.where(live, flux, 1.0) * mask, 0.0).astype(jnp.bfloat16)


def stacked(modes_ref, picks, half, cols):
    parts = []
    for x in (1, 0):
        used = 0
        for pick in picks:
            if pick is None:
                parts.append(jnp.zeros((cols, modes_ref.shape[-1]), jnp.float32))
            else:
                s, k = pick
                rows = modes_ref[x, s, k].astype(jnp.float32)
                parts.append(rows[half * cols : (half + 1) * cols])
            used += cols
        parts.append(jnp.zeros((HALF - used, modes_ref.shape[-1]), jnp.float32))
    return jnp.concatenate(parts, axis=0).astype(jnp.bfloat16)


class OneSensor:
    def __init__(self, ref):
        self.ref = ref
        self.shape = ref.shape

    def __getitem__(self, at):
        return self.ref[0, at[1], at[2], at[3]]


def kernel_second(
    sub_rows, sub_cols, frames, ahead_ref, geo_ref, pf_ref, mask_ref, modes_ref, pm_in_ref, count_in_ref,
    pm_ref, edge_ref, em_ref, count_ref, w_ref, p_ref,
):
    sensors = pf_ref.shape[0]
    last = sub_rows - 1
    cols = sub_cols // 2
    final = sensors - 1
    for i in range(1, last):
        block_weights(geo_ref.at[final, i], w_ref.at[i - 1])
    for i in range(1, last):
        block_moments(
            ahead_ref.at[i - 1], row_positions(geo_ref.at[final, i]), w_ref.at[i - 1], p_ref.at[0, i], sub_cols, frames
        )
    for i in (0, last):
        p_ref[0, i] = pf_ref[final, i]
    modes, count = inner_projection(OneSensor(p_ref), mask_ref, modes_ref, final)
    count = count + count_in_ref[...]
    for e, k in enumerate((0, last)):
        order = [None] * 3
        for s in range(sensors):
            order[slot_of(k, s)] = s
        for h in range(2):
            m = side_by_side([mask_of(mask_ref, s, k, h) for s in order])
            em_ref[e, h] = m
            count = count + m
            for a in range(2):
                edge_ref[e, h, a] = by_slot(
                    [strip_total(OneSensor(p_ref) if s == final else pf_ref, s, k, h, a) for s in order], cols
                )
    pm_ref[...] = pm_in_ref[...] + modes
    count_ref[...] = jnp.broadcast_to(0.5 * jnp.sum(count, axis=1, keepdims=True), count_ref.shape)


def kernel_join(
    sub_rows, sub_cols, frames, tiles, blocks,
    live_ref, after_ref, before_ref, pm_ref, edge_ref, em_ref, count_ref, modes_ref, gain_ref, out_ref,
):
    sensors = modes_ref.shape[1]
    last = sub_rows - 1
    cols = sub_cols // 2
    modes = pm_ref[...]
    for e, k in enumerate((0, last)):
        halo_ref = (before_ref, after_ref)[e]
        halo_strip = (sub_rows, -1)[e]
        turn = (slot_of(k, 0) - slot_of(halo_strip, 0)) % 3
        order = [None] * 3
        for s in range(sensors):
            order[slot_of(k, s)] = s
        both = halo_ref[2]
        for h in range(2):
            lines = both if h == 0 else pltpu.roll(both, HALF, axis=1)
            plain = edge_ref[e, h, 0] + rotate(halo_ref[h], turn, cols)
            lines = edge_ref[e, h, 1] + rotate(lines, turn, cols)
            modes = modes + jnp.dot(
                slope_terms(plain, lines, em_ref[e, h]),
                stacked(modes_ref, [None if s is None else (s, k) for s in order], h, cols),
                preferred_element_type=jnp.float32,
            )
    live = (lax.broadcasted_iota(jnp.int32, (frames, LANES), 0) < live_ref[0]).astype(jnp.float32)
    info = gain_ref[...] * modes * jnp.concatenate([live] * (modes.shape[1] // LANES), axis=1)
    own = lane_iota(frames) == lax.broadcasted_iota(jnp.int32, (frames, LANES), 0)
    counts = jnp.sum(jnp.where(own, count_ref[...] * live, 0.0), axis=0, keepdims=True)
    share = modes.shape[1] // tiles
    pack = LANES // share
    rows = frames // pack
    pad = jnp.zeros((out_ref.shape[1] - rows - 1, LANES), jnp.float32)
    for t in range(tiles):
        piece = jnp.concatenate(
            [info[g * rows : (g + 1) * rows, t * share : (t + 1) * share] for g in range(pack)], axis=1
        )
        piece = jnp.concatenate([piece, counts, pad], axis=0)
        for b in range(blocks):
            out_ref[t * blocks + b] = piece


def shifted(x, by, fill, back):
    rows = x.shape[0]
    if by % 8 == 0:
        pad = jnp.full((by, x.shape[1]), fill, x.dtype)
        if back:
            return jnp.concatenate([x[by:], pad], axis=0)
        return jnp.concatenate([pad, x[: rows - by]], axis=0)
    row = lax.broadcasted_iota(jnp.int32, (rows, 1), 0)
    if back:
        return jnp.where(row < rows - by, pltpu.roll(x, rows - by, axis=0), fill)
    return jnp.where(row >= by, pltpu.roll(x, by, axis=0), fill)


def kernel_smooth(
    tiles, blocks, frames, total_subaps, in_ref, noise_ref, gain_ref, mean_ref, var_ref, mean_scr, var_scr
):
    share = mean_ref.shape[1]
    total = blocks * frames
    tile = lax.axis_index("tile")
    time = lax.axis_index("tm")
    pack = LANES // share
    rows = frames // pack

    def own_modes(v):
        out = v[:, 0:share]
        for t in range(1, tiles):
            out = jnp.where(tile == t, v[:, t * share : (t + 1) * share], out)
        return out

    q = own_modes(noise_ref[...])
    gain = own_modes(gain_ref[...])
    own = lane_iota(frames) == lax.broadcasted_iota(jnp.int32, (frames, LANES), 0)
    infos = []
    counts = []
    for b in range(blocks):
        v = in_ref[b]
        for t in range(1, tiles):
            v = v + in_ref[t * blocks + b]
        for g in range(pack):
            infos.append(v[0:rows, g * share : (g + 1) * share])
        counts.append(jnp.sum(jnp.where(own, v[rows : rows + 1], 0.0), axis=1, keepdims=True))
    info_mean = jnp.concatenate(infos, axis=0)
    prec = gain * jnp.concatenate(counts, axis=0) / total_subaps
    row = lax.broadcasted_iota(jnp.int32, (total, 1), 0)
    first = row == 0
    retain = 1.0 / (1.0 + q * prec)
    a = jnp.where(first, 0.0, retain)
    c = jnp.where(first, 1.0 / (1.0 + prec), q * retain)
    b = c * info_mean
    e = a * info_mean
    j = a * prec
    by = 1
    while by < total:
        a1 = shifted(a, by, 1.0, False)
        b1 = shifted(b, by, 0.0, False)
        c1 = shifted(c, by, 0.0, False)
        e1 = shifted(e, by, 0.0, False)
        j1 = shifted(j, by, 0.0, False)
        damp = 1.0 / (1.0 + c1 * j)
        left = a * damp
        right = a1 * damp
        b = left * (b1 + c1 * e) + b
        c = left * a * c1 + c
        e, j = right * (e - j * b1) + e1, right * a1 * j + j1
        a = left * a1
        by *= 2
    g = jnp.where(row == total - 1, 0.0, c / (c + q))
    m = (1.0 - g) * b
    v = c * (1.0 - g)
    by = 1
    while by < total:
        g1 = shifted(g, by, 1.0, True)
        m1 = shifted(m, by, 0.0, True)
        v1 = shifted(v, by, 0.0, True)
        m = g * m1 + m
        v = g * g * v1 + v
        g = g * g1
        by *= 2
    mean_scr[...] = m
    var_scr[...] = v
    start = pl.multiple_of(time * frames, 8)
    mean_ref[...] = mean_scr[pl.ds(start, frames), :]
    var_ref[...] = var_scr[pl.ds(start, frames), :]


def body(pixels, offsets, mask, frame_count, slope_to_modes, process_noise, mode_gain):
    sensors, frames, lines, width = pixels.shape
    sub_rows, sub_cols = mask.shape[2], mask.shape[3]
    modes = process_noise.shape[0]
    tiles = lax.axis_size("tile")
    blocks = lax.axis_size("tm")
    share = modes // tiles
    total_subaps = sensors * sub_rows * tiles * sub_cols
    f32 = jnp.float32
    bf16 = jnp.bfloat16
    x = jnp.transpose(pixels, (0, 2, 1, 3)).reshape(sensors, lines * frames, width)
    off = jnp.transpose(offsets, (0, 1, 3, 2))
    msk = jnp.transpose(mask, (0, 2, 1, 3))
    block = SIDE * frames
    x, off, msk, slope_to_modes = (
        pltpu.with_memory_space_constraint(v, pltpu.HBM) for v in (x, off, msk, slope_to_modes)
    )
    inner = sub_rows - 2
    depth = max(half_columns(h, sub_cols, width)[1] for h in range(2))
    params = pltpu.CompilerParams(vmem_limit_bytes=VMEM_LIMIT)

    def cost(chunks):
        return pl.CostEstimate(
            flops=2 * chunks * block * width * 256, bytes_accessed=chunks * block * width * 2, transcendentals=0
        )

    up, down, parts, geo, mask_v, modes_v, ahead, modes_first, count_first = pl.pallas_call(
        functools.partial(kernel_first, sub_rows, sub_cols, frames),
        out_shape=(
            jax.ShapeDtypeStruct((3, frames, LANES), f32),
            jax.ShapeDtypeStruct((3, frames, LANES), f32),
            pltpu.VMEM((sensors, sub_rows, 2, 2, frames, LANES), f32),
            pltpu.VMEM((sensors, sub_rows, 8, LANES), f32),
            pltpu.VMEM(msk.shape, msk.dtype),
            pltpu.VMEM(slope_to_modes.shape, bf16),
            pltpu.VMEM((inner, block, width), bf16),
            pltpu.VMEM((frames, modes), f32),
            pltpu.VMEM((frames, LANES), f32),
        ),
        in_specs=[HBM] * 4,
        out_specs=(VMEM,) * 9,
        scratch_shapes=[
            pltpu.VMEM((sensors - 1, sub_rows, block, width), bf16),
            pltpu.VMEM((2, block, width), bf16),
            pltpu.VMEM((sub_rows, 2, depth, LANES), bf16),
            pltpu.VMEM(off.shape, off.dtype),
            pltpu.SemaphoreType.DMA((sensors, sub_rows, 2)),
            pltpu.SemaphoreType.DMA((3,)),
        ],
        compiler_params=params,
        cost_estimate=cost(sensors * sub_rows - inner),
        name="first_moments",
    )(x, off, msk, slope_to_modes)
    onward = [(i, i + 1) for i in range(tiles - 1)]
    backward = [(j, i) for i, j in onward]
    from_after = lax.ppermute(down, "tile", backward)
    from_before = lax.ppermute(up, "tile", onward)
    partial_modes, edge, edge_mask, count = pl.pallas_call(
        functools.partial(kernel_second, sub_rows, sub_cols, frames),
        out_shape=(
            pltpu.VMEM((frames, modes), f32),
            pltpu.VMEM((2, 2, 2, frames, LANES), f32),
            pltpu.VMEM((2, 2, frames, LANES), f32),
            pltpu.VMEM((frames, LANES), f32),
        ),
        in_specs=[VMEM] * 7,
        out_specs=(VMEM,) * 4,
        scratch_shapes=[
            pltpu.VMEM((inner, 2, depth, LANES), bf16),
            pltpu.VMEM((1, sub_rows, 2, 2, frames, LANES), f32),
        ],
        compiler_params=params,
        cost_estimate=cost(inner),
        name="second_moments",
    )(ahead, geo, parts, mask_v, modes_v, modes_first, count_first)
    gain = mode_gain.reshape(1, modes)
    packed = -(-(frames * share // LANES + 1) // 8) * 8
    payload = pl.pallas_call(
        functools.partial(kernel_join, sub_rows, sub_cols, frames, tiles, blocks),
        out_shape=jax.ShapeDtypeStruct((tiles * blocks, packed, LANES), f32),
        in_specs=[pl.BlockSpec(memory_space=pltpu.SMEM)] + [VMEM] * 8,
        out_specs=VMEM,
        compiler_params=params,
        name="join_halo",
    )(frame_count, from_after, from_before, partial_modes, edge, edge_mask, count, modes_v, gain)
    info = lax.all_to_all(payload, ("tile", "tm"), 0, 0)
    return pl.pallas_call(
        functools.partial(kernel_smooth, tiles, blocks, frames, float(total_subaps)),
        out_shape=(
            jax.ShapeDtypeStruct((frames, share), f32),
            jax.ShapeDtypeStruct((frames, share), f32),
        ),
        in_specs=[VMEM] * 3,
        out_specs=(VMEM, VMEM),
        scratch_shapes=[
            pltpu.VMEM((blocks * frames, share), f32),
            pltpu.VMEM((blocks * frames, share), f32),
        ],
        compiler_params=params,
        name="smooth",
    )(info, process_noise.reshape(1, modes), gain)


def solution(mesh):
    return jax.shard_map(
        body,
        mesh=mesh,
        in_specs=(
            P("grp", "tm", "tile", None),
            P("grp", None, None, None),
            P("grp", "tm", "tile", None),
            P(("grp", "tm")),
            P(None, None, "tile", None, None),
            P(),
            P(),
        ),
        out_specs=(P(("grp", "tm"), "tile"), P(("grp", "tm"), "tile")),
        check_vma=False,
    )
```

```python
import functools

import jax
import jax.numpy as jnp
from jax import lax
from jax.experimental import pallas as pl
from jax.experimental.pallas import tpu as pltpu
from jax.sharding import PartitionSpec as P

SIDE = 20
SHIFT = 6
CENTRE = (SIDE - 1) / 2.0
LANES = 128
HALF = LANES // 2
VMEM_LIMIT = 24 * 1024 * 1024
VMEM = pl.BlockSpec(memory_space=pltpu.VMEM)
HBM = pl.BlockSpec(memory_space=pl.ANY)


def slot_of(strip, sensor):
    return (strip + 1 + sensor) % 3


def half_columns(half, sub_cols, width):
    cols = sub_cols // 2
    first = max(0, half * cols * SIDE - SHIFT) // LANES * LANES
    end = min(width, -(-((half + 1) * cols * SIDE + SHIFT) // 16) * 16)
    return first, end - first


def lane_iota(rows=1):
    return lax.broadcasted_iota(jnp.int32, (rows, LANES), 1)


def half_lane(rows=1):
    lane = lane_iota(rows)
    return jnp.where(lane >= HALF, lane - HALF, lane)


def by_slot(values, cols):
    lane = half_lane()
    out = jnp.zeros_like(values[0])
    for q, v in enumerate(values):
        if v is not None:
            out = jnp.where((lane >= q * cols) & (lane < (q + 1) * cols), v, out)
    return out


def side_by_side(pieces):
    rows, cols = pieces[0].shape
    pad = jnp.zeros((rows, HALF - 3 * cols), pieces[0].dtype)
    return jnp.concatenate([*pieces, pad, *pieces, pad], axis=1)


def rotate(x, slots, cols):
    shift = slots * cols
    if shift == 0:
        return x
    near = pltpu.roll(x, shift, axis=1)
    far = pltpu.roll(x, LANES - 3 * cols + shift, axis=1)
    return jnp.where(half_lane() >= shift, near, far)


def geometry(geo_ref, off_ref, sensors, sub_rows, sub_cols, width):
    cols = sub_cols // 2
    lane = half_lane()
    index = lane - cols * (lane >= cols).astype(jnp.int32)
    index = index - cols * (lane >= 2 * cols).astype(jnp.int32)
    used = lane < 3 * cols
    tile = lax.axis_index("tile")
    total_rows = off_ref.shape[1]
    for s in range(sensors):
        spread_rows = []
        for k in range(-1, sub_rows + 1):
            row = jnp.clip(tile * sub_rows + k, 0, total_rows - 1)
            v = off_ref[s, row].astype(jnp.float32)
            spread_rows.append([side_by_side([v[:, h * cols : (h + 1) * cols]] * 3) for h in range(2)])
        for i in range(sub_rows):
            for h in range(2):
                first, _ = half_columns(h, sub_cols, width)
                col_base = (SIDE * (index + h * cols) - first).astype(jnp.float32) + CENTRE
                cs = [None] * 3
                rs = [None] * 3
                for k in (i - 1, i, i + 1):
                    q = slot_of(k, s)
                    v = spread_rows[k + 1][h]
                    cs[q] = v[1:2] + col_base
                    rs[q] = v[0:1] + (SIDE * (k - i) + CENTRE)
                geo_ref[s, i, 2 * h : 2 * h + 1, :] = jnp.where(used, by_slot(cs, cols), -1000.0)
                geo_ref[s, i, 2 * h + 1 : 2 * h + 2, :] = jnp.where(used, by_slot(rs, cols), -1000.0)


def build_weights(col_pos, w_ref):
    base = lax.broadcasted_iota(jnp.int32, (16, LANES), 0).astype(jnp.float32) - col_pos
    left = lane_iota(16) < HALF
    for t in range(w_ref.shape[0] // 16):
        d = base + float(16 * t)
        value = jnp.where(left, 1.0, d)
        w_ref[16 * t : 16 * t + 16, :] = jnp.where(jnp.abs(d) < 10.0, value, 0.0).astype(jnp.bfloat16)


def row_sums(row_pos, r, frames):
    plain = jnp.zeros((frames, LANES), jnp.float32)
    lines = jnp.zeros((frames, LANES), jnp.float32)
    for y in range(r.shape[0] // frames):
        d = float(y) - row_pos
        inside = jnp.abs(d) < 10.0
        one = jnp.where(inside, 1.0, 0.0)
        centred = jnp.where(inside, d, 0.0)
        piece = r[y * frames : (y + 1) * frames, :]
        plain = plain + one * piece
        lines = lines + centred * piece
    return plain, lines


def block_moments(pixels, row_pos, w_ref, p_ref, sub_cols, frames):
    for h in range(2):
        first, size = half_columns(h, sub_cols, pixels.shape[1])
        r = jnp.dot(
            pixels[:, first : first + size], w_ref[h, 0:size, :], preferred_element_type=jnp.float32
        )
        plain, lines = row_sums(row_pos[h], r, frames)
        p_ref[h, 0] = plain
        p_ref[h, 1] = lines


def block_weights(geo_ref, w_ref):
    for h in range(2):
        build_weights(geo_ref[2 * h : 2 * h + 1, :], w_ref.at[h])


def row_positions(geo_ref):
    return [geo_ref[2 * h + 1 : 2 * h + 2, :] for h in range(2)]


def strip_total(p_ref, s, k, h, a):
    total = None
    for i in (k - 1, k, k + 1):
        if 0 <= i < p_ref.shape[1]:
            v = p_ref[s, i, h, a]
            total = v if total is None else total + v
    return total


def mask_of(mask_ref, s, k, h):
    cols = mask_ref.shape[3] // 2
    return mask_ref[s, k].astype(jnp.float32)[:, h * cols : (h + 1) * cols]


def inner_projection(p_ref, mask_ref, modes_ref, s):
    last = p_ref.shape[1] - 1
    frames, sub_cols = mask_ref.shape[2:]
    cols = sub_cols // 2
    modes = jnp.zeros((frames, modes_ref.shape[-1]), jnp.float32)
    count = jnp.zeros((frames, LANES), jnp.float32)
    none = jnp.zeros((frames, cols), jnp.float32)
    for g in range(1, last, 3):
        order = [None] * 3
        for k in range(g, min(g + 3, last)):
            order[slot_of(k, s)] = k
        for h in range(2):
            mask = side_by_side([none if k is None else mask_of(mask_ref, s, k, h) for k in order])
            count = count + mask
            plain, lines = (
                by_slot([None if k is None else strip_total(p_ref, s, k, h, a) for k in order], cols)
                for a in range(2)
            )
            modes = modes + jnp.dot(
                slope_terms(plain, lines, mask),
                stacked(modes_ref, [None if k is None else (s, k) for k in order], h, cols),
                preferred_element_type=jnp.float32,
            )
    return modes, count


def kernel_first(
    sub_rows, sub_cols, frames, x_hbm, off_hbm, mask_hbm, modes_hbm,
    up_ref, down_ref, p_ref, geo_ref, mask_ref, modes_ref, ahead_ref, pm_ref, count_ref,
    buf, edge_buf, w_ref, off_ref, sem, side_sem,
):
    sensors = x_hbm.shape[0]
    block = SIDE * frames
    last = sub_rows - 1
    cols = sub_cols // 2
    final = sensors - 1
    order = (0, last, *range(1, last))

    def place(s, i):
        if isinstance(s, int) and s == final:
            return ahead_ref.at[i - 1] if 0 < i < last else edge_buf.at[min(i, 1)]
        return buf.at[s, i]

    def copy(s, i):
        return pltpu.make_async_copy(x_hbm.at[s, pl.ds(i * block, block)], place(s, i), sem.at[s, i])

    off_copy = pltpu.make_async_copy(off_hbm, off_ref, side_sem.at[0])
    mask_copy = pltpu.make_async_copy(mask_hbm, mask_ref, side_sem.at[1])
    modes_copy = pltpu.make_async_copy(modes_hbm, modes_ref, side_sem.at[2])
    off_copy.start()
    for s in range(sensors):
        for i in order:
            copy(s, i).start()
        if s == 0:
            mask_copy.start()
            modes_copy.start()
    off_copy.wait()
    geometry(geo_ref, off_ref, sensors, sub_rows, sub_cols, x_hbm.shape[2])

    def blocks_of(s, which):
        for i in which:
            block_weights(geo_ref.at[s, i], w_ref.at[i])
        for i in which:
            copy(s, i).wait()
        for i in which:
            block_moments(
                place(s, i), row_positions(geo_ref.at[s, i]), w_ref.at[i], p_ref.at[s, i], sub_cols, frames
            )

    def step(s, carry):
        blocks_of(s, order)
        return carry

    lax.fori_loop(0, final, step, 0)
    mask_copy.wait()
    modes_copy.wait()
    modes = jnp.zeros(pm_ref.shape, jnp.float32)
    count = jnp.zeros(count_ref.shape, jnp.float32)
    for s in range(final):
        part, number = inner_projection(p_ref, mask_ref, modes_ref, s)
        modes = modes + part
        count = count + number
    pm_ref[...] = modes
    count_ref[...] = count
    blocks_of(final, (0, last))
    left = lane_iota() < HALF
    for ref, i, strip in ((down_ref, 0, -1), (up_ref, last, sub_rows)):
        pair = []
        for h in range(2):
            both = []
            for a in range(2):
                pieces = [None] * 3
                for s in range(sensors):
                    pieces[slot_of(strip, s)] = p_ref[s, i, h, a]
                both.append(by_slot(pieces, cols))
            ref[h] = both[0]
            pair.append(both[1])
        ref[2] = jnp.where(left, pair[0], pltpu.roll(pair[1], HALF, axis=1))
    for i in range(1, last):
        copy(final, i).wait()


def slope_terms(plain, lines, mask):
    left = lane_iota() < HALF
    live = mask > 0.0
    flux = jnp.where(left, plain, pltpu.roll(plain, HALF, axis=1))
    moment = jnp.where(left, lines, plain)
    return jnp.where(live, moment / jnp.where(live, flux, 1.0) * mask, 0.0).astype(jnp.bfloat16)


def stacked(modes_ref, picks, half, cols):
    parts = []
    for x in (1, 0):
        used = 0
        for pick in picks:
            if pick is None:
                parts.append(jnp.zeros((cols, modes_ref.shape[-1]), jnp.float32))
            else:
                s, k = pick
                rows = modes_ref[x, s, k].astype(jnp.float32)
                parts.append(rows[half * cols : (half + 1) * cols])
            used += cols
        parts.append(jnp.zeros((HALF - used, modes_ref.shape[-1]), jnp.float32))
    return jnp.concatenate(parts, axis=0).astype(jnp.bfloat16)


class OneSensor:
    def __init__(self, ref):
        self.ref = ref
        self.shape = ref.shape

    def __getitem__(self, at):
        return self.ref[0, at[1], at[2], at[3]]


def kernel_second(
    sub_rows, sub_cols, frames, ahead_ref, geo_ref, pf_ref, mask_ref, modes_ref, pm_in_ref, count_in_ref,
    pm_ref, edge_ref, em_ref, count_ref, w_ref, p_ref,
):
    sensors = pf_ref.shape[0]
    last = sub_rows - 1
    cols = sub_cols // 2
    final = sensors - 1
    for i in range(1, last):
        block_weights(geo_ref.at[final, i], w_ref.at[i - 1])
    for i in range(1, last):
        block_moments(
            ahead_ref.at[i - 1], row_positions(geo_ref.at[final, i]), w_ref.at[i - 1], p_ref.at[0, i], sub_cols, frames
        )
    for i in (0, last):
        p_ref[0, i] = pf_ref[final, i]
    modes, count = inner_projection(OneSensor(p_ref), mask_ref, modes_ref, final)
    count = count + count_in_ref[...]
    for e, k in enumerate((0, last)):
        order = [None] * 3
        for s in range(sensors):
            order[slot_of(k, s)] = s
        for h in range(2):
            m = side_by_side([mask_of(mask_ref, s, k, h) for s in order])
            em_ref[e, h] = m
            count = count + m
            for a in range(2):
                edge_ref[e, h, a] = by_slot(
                    [strip_total(OneSensor(p_ref) if s == final else pf_ref, s, k, h, a) for s in order], cols
                )
    pm_ref[...] = pm_in_ref[...] + modes
    count_ref[...] = jnp.broadcast_to(0.5 * jnp.sum(count, axis=1, keepdims=True), count_ref.shape)


def kernel_join(
    sub_rows, sub_cols, frames, tiles, blocks,
    live_ref, before_ref, after_ref, pm_ref, edge_ref, em_ref, count_ref, modes_ref, gain_ref, out_ref,
):
    sensors = modes_ref.shape[1]
    last = sub_rows - 1
    cols = sub_cols // 2
    modes = pm_ref[...]
    for e, k in enumerate((0, last)):
        halo_ref = (before_ref, after_ref)[e]
        halo_strip = (sub_rows, -1)[e]
        turn = (slot_of(k, 0) - slot_of(halo_strip, 0)) % 3
        order = [None] * 3
        for s in range(sensors):
            order[slot_of(k, s)] = s
        both = halo_ref[2]
        for h in range(2):
            lines = both if h == 0 else pltpu.roll(both, HALF, axis=1)
            plain = edge_ref[e, h, 0] + rotate(halo_ref[h], turn, cols)
            lines = edge_ref[e, h, 1] + rotate(lines, turn, cols)
            modes = modes + jnp.dot(
                slope_terms(plain, lines, em_ref[e, h]),
                stacked(modes_ref, [None if s is None else (s, k) for s in order], h, cols),
                preferred_element_type=jnp.float32,
            )
    live = (lax.broadcasted_iota(jnp.int32, (frames, LANES), 0) < live_ref[0]).astype(jnp.float32)
    info = gain_ref[...] * modes * jnp.concatenate([live] * (modes.shape[1] // LANES), axis=1)
    own = lane_iota(frames) == lax.broadcasted_iota(jnp.int32, (frames, LANES), 0)
    counts = jnp.sum(jnp.where(own, count_ref[...] * live, 0.0), axis=0, keepdims=True)
    share = modes.shape[1] // tiles
    pack = LANES // share
    rows = frames // pack
    pad = jnp.zeros((out_ref.shape[1] - rows - 1, LANES), jnp.float32)
    for t in range(tiles):
        piece = jnp.concatenate(
            [info[g * rows : (g + 1) * rows, t * share : (t + 1) * share] for g in range(pack)], axis=1
        )
        piece = jnp.concatenate([piece, counts, pad], axis=0)
        for b in range(blocks):
            out_ref[t * blocks + b] = piece


def shifted(x, by, fill, back):
    rows = x.shape[0]
    if by % 8 == 0:
        pad = jnp.full((by, x.shape[1]), fill, x.dtype)
        if back:
            return jnp.concatenate([x[by:], pad], axis=0)
        return jnp.concatenate([pad, x[: rows - by]], axis=0)
    row = lax.broadcasted_iota(jnp.int32, (rows, 1), 0)
    if back:
        return jnp.where(row < rows - by, pltpu.roll(x, rows - by, axis=0), fill)
    return jnp.where(row >= by, pltpu.roll(x, by, axis=0), fill)


def kernel_smooth(
    tiles, blocks, frames, total_subaps, in_ref, noise_ref, gain_ref, mean_ref, var_ref, mean_scr, var_scr
):
    share = mean_ref.shape[1]
    total = blocks * frames
    tile = lax.axis_index("tile")
    time = lax.axis_index("tm")
    pack = LANES // share
    rows = frames // pack

    def own_modes(v):
        out = v[:, 0:share]
        for t in range(1, tiles):
            out = jnp.where(tile == t, v[:, t * share : (t + 1) * share], out)
        return out

    q = own_modes(noise_ref[...])
    gain = own_modes(gain_ref[...])
    own = lane_iota(frames) == lax.broadcasted_iota(jnp.int32, (frames, LANES), 0)
    infos = []
    counts = []
    for b in range(blocks):
        v = in_ref[b]
        for t in range(1, tiles):
            v = v + in_ref[t * blocks + b]
        for g in range(pack):
            infos.append(v[0:rows, g * share : (g + 1) * share])
        counts.append(jnp.sum(jnp.where(own, v[rows : rows + 1], 0.0), axis=1, keepdims=True))
    info_mean = jnp.concatenate(infos, axis=0)
    prec = gain * jnp.concatenate(counts, axis=0) / total_subaps
    row = lax.broadcasted_iota(jnp.int32, (total, 1), 0)
    first = row == 0
    retain = 1.0 / (1.0 + q * prec)
    a = jnp.where(first, 0.0, retain)
    c = jnp.where(first, 1.0 / (1.0 + prec), q * retain)
    b = c * info_mean
    e = a * info_mean
    j = a * prec
    by = 1
    while by < total:
        a1 = shifted(a, by, 1.0, False)
        b1 = shifted(b, by, 0.0, False)
        c1 = shifted(c, by, 0.0, False)
        e1 = shifted(e, by, 0.0, False)
        j1 = shifted(j, by, 0.0, False)
        damp = 1.0 / (1.0 + c1 * j)
        left = a * damp
        right = a1 * damp
        b = left * (b1 + c1 * e) + b
        c = left * a * c1 + c
        e, j = right * (e - j * b1) + e1, right * a1 * j + j1
        a = left * a1
        by *= 2
    g = jnp.where(row == total - 1, 0.0, c / (c + q))
    m = (1.0 - g) * b
    v = c * (1.0 - g)
    by = 1
    while by < total:
        g1 = shifted(g, by, 1.0, True)
        m1 = shifted(m, by, 0.0, True)
        v1 = shifted(v, by, 0.0, True)
        m = g * m1 + m
        v = g * g * v1 + v
        g = g * g1
        by *= 2
    mean_scr[...] = m
    var_scr[...] = v
    start = pl.multiple_of(time * frames, 8)
    mean_ref[...] = mean_scr[pl.ds(start, frames), :]
    var_ref[...] = var_scr[pl.ds(start, frames), :]


def body(pixels, offsets, mask, frame_count, slope_to_modes, process_noise, mode_gain):
    sensors, frames, lines, width = pixels.shape
    sub_rows, sub_cols = mask.shape[2], mask.shape[3]
    modes = process_noise.shape[0]
    tiles = lax.axis_size("tile")
    blocks = lax.axis_size("tm")
    share = modes // tiles
    total_subaps = sensors * sub_rows * tiles * sub_cols
    f32 = jnp.float32
    bf16 = jnp.bfloat16
    x = jnp.transpose(pixels, (0, 2, 1, 3)).reshape(sensors, lines * frames, width)
    off = jnp.transpose(offsets, (0, 1, 3, 2))
    msk = jnp.transpose(mask, (0, 2, 1, 3))
    block = SIDE * frames
    x, off, msk, slope_to_modes = (
        pltpu.with_memory_space_constraint(v, pltpu.HBM) for v in (x, off, msk, slope_to_modes)
    )
    inner = sub_rows - 2
    depth = max(half_columns(h, sub_cols, width)[1] for h in range(2))
    params = pltpu.CompilerParams(vmem_limit_bytes=VMEM_LIMIT)

    def cost(chunks):
        return pl.CostEstimate(
            flops=2 * chunks * block * width * 256, bytes_accessed=chunks * block * width * 2, transcendentals=0
        )

    up, down, parts, geo, mask_v, modes_v, ahead, modes_first, count_first = pl.pallas_call(
        functools.partial(kernel_first, sub_rows, sub_cols, frames),
        out_shape=(
            jax.ShapeDtypeStruct((3, frames, LANES), f32),
            jax.ShapeDtypeStruct((3, frames, LANES), f32),
            pltpu.VMEM((sensors, sub_rows, 2, 2, frames, LANES), f32),
            pltpu.VMEM((sensors, sub_rows, 8, LANES), f32),
            pltpu.VMEM(msk.shape, msk.dtype),
            pltpu.VMEM(slope_to_modes.shape, bf16),
            pltpu.VMEM((inner, block, width), bf16),
            pltpu.VMEM((frames, modes), f32),
            pltpu.VMEM((frames, LANES), f32),
        ),
        in_specs=[HBM] * 4,
        out_specs=(VMEM,) * 9,
        scratch_shapes=[
            pltpu.VMEM((sensors - 1, sub_rows, block, width), bf16),
            pltpu.VMEM((2, block, width), bf16),
            pltpu.VMEM((sub_rows, 2, depth, LANES), bf16),
            pltpu.VMEM(off.shape, off.dtype),
            pltpu.SemaphoreType.DMA((sensors, sub_rows)),
            pltpu.SemaphoreType.DMA((3,)),
        ],
        compiler_params=params,
        cost_estimate=cost(sensors * sub_rows - inner),
        name="first_moments",
    )(x, off, msk, slope_to_modes)
    onward = [(i, i + 1) for i in range(tiles - 1)]
    backward = [(j, i) for i, j in onward]
    from_before = lax.ppermute(up, "tile", onward)
    from_after = lax.ppermute(down, "tile", backward)
    partial_modes, edge, edge_mask, count = pl.pallas_call(
        functools.partial(kernel_second, sub_rows, sub_cols, frames),
        out_shape=(
            pltpu.VMEM((frames, modes), f32),
            pltpu.VMEM((2, 2, 2, frames, LANES), f32),
            pltpu.VMEM((2, 2, frames, LANES), f32),
            pltpu.VMEM((frames, LANES), f32),
        ),
        in_specs=[VMEM] * 7,
        out_specs=(VMEM,) * 4,
        scratch_shapes=[
            pltpu.VMEM((inner, 2, depth, LANES), bf16),
            pltpu.VMEM((1, sub_rows, 2, 2, frames, LANES), f32),
        ],
        compiler_params=params,
        cost_estimate=cost(inner),
        name="second_moments",
    )(ahead, geo, parts, mask_v, modes_v, modes_first, count_first)
    gain = mode_gain.reshape(1, modes)
    packed = -(-(frames * share // LANES + 1) // 8) * 8
    payload = pl.pallas_call(
        functools.partial(kernel_join, sub_rows, sub_cols, frames, tiles, blocks),
        out_shape=jax.ShapeDtypeStruct((tiles * blocks, packed, LANES), f32),
        in_specs=[pl.BlockSpec(memory_space=pltpu.SMEM)] + [VMEM] * 8,
        out_specs=VMEM,
        compiler_params=params,
        name="join_halo",
    )(frame_count, from_before, from_after, partial_modes, edge, edge_mask, count, modes_v, gain)
    info = lax.all_to_all(payload, ("tile", "tm"), 0, 0)
    return pl.pallas_call(
        functools.partial(kernel_smooth, tiles, blocks, frames, float(total_subaps)),
        out_shape=(
            jax.ShapeDtypeStruct((frames, share), f32),
            jax.ShapeDtypeStruct((frames, share), f32),
        ),
        in_specs=[VMEM] * 3,
        out_specs=(VMEM, VMEM),
        scratch_shapes=[
            pltpu.VMEM((blocks * frames, share), f32),
            pltpu.VMEM((blocks * frames, share), f32),
        ],
        compiler_params=params,
        name="smooth",
    )(info, process_noise.reshape(1, modes), gain)


def solution(mesh):
    return jax.shard_map(
        body,
        mesh=mesh,
        in_specs=(
            P("grp", "tm", "tile", None),
            P("grp", None, None, None),
            P("grp", "tm", "tile", None),
            P(("grp", "tm")),
            P(None, None, "tile", None, None),
            P(),
            P(),
        ),
        out_specs=(P(("grp", "tm"), "tile"), P(("grp", "tm"), "tile")),
        check_vma=False,
    )
```

```python
import functools

import jax
import jax.numpy as jnp
from jax import lax
from jax.experimental import pallas as pl
from jax.experimental.pallas import tpu as pltpu
from jax.sharding import PartitionSpec as P

SIDE = 20
SHIFT = 6
CENTRE = (SIDE - 1) / 2.0
LANES = 128
HALF = LANES // 2
VMEM_LIMIT = 24 * 1024 * 1024
VMEM = pl.BlockSpec(memory_space=pltpu.VMEM)
HBM = pl.BlockSpec(memory_space=pl.ANY)


def slot_of(strip, sensor):
    return (strip + 1 + sensor) % 3


def half_columns(half, sub_cols, width):
    cols = sub_cols // 2
    first = max(0, half * cols * SIDE - SHIFT) // LANES * LANES
    end = min(width, -(-((half + 1) * cols * SIDE + SHIFT) // 16) * 16)
    return first, end - first


def lane_iota(rows=1):
    return lax.broadcasted_iota(jnp.int32, (rows, LANES), 1)


def half_lane(rows=1):
    lane = lane_iota(rows)
    return jnp.where(lane >= HALF, lane - HALF, lane)


def by_slot(values, cols):
    lane = half_lane()
    out = jnp.zeros_like(values[0])
    for q, v in enumerate(values):
        if v is not None:
            out = jnp.where((lane >= q * cols) & (lane < (q + 1) * cols), v, out)
    return out


def side_by_side(pieces):
    rows, cols = pieces[0].shape
    pad = jnp.zeros((rows, HALF - 3 * cols), pieces[0].dtype)
    return jnp.concatenate([*pieces, pad, *pieces, pad], axis=1)


def rotate(x, slots, cols):
    shift = slots * cols
    if shift == 0:
        return x
    near = pltpu.roll(x, shift, axis=1)
    far = pltpu.roll(x, LANES - 3 * cols + shift, axis=1)
    return jnp.where(half_lane() >= shift, near, far)


def geometry(geo_ref, off_ref, sensors, sub_rows, sub_cols, width):
    cols = sub_cols // 2
    lane = half_lane()
    index = lane - cols * (lane >= cols).astype(jnp.int32)
    index = index - cols * (lane >= 2 * cols).astype(jnp.int32)
    used = lane < 3 * cols
    tile = lax.axis_index("tile")
    total_rows = off_ref.shape[1]
    for s in range(sensors):
        spread_rows = []
        for k in range(-1, sub_rows + 1):
            row = jnp.clip(tile * sub_rows + k, 0, total_rows - 1)
            v = off_ref[s, row].astype(jnp.float32)
            spread_rows.append([side_by_side([v[:, h * cols : (h + 1) * cols]] * 3) for h in range(2)])
        for i in range(sub_rows):
            for h in range(2):
                first, _ = half_columns(h, sub_cols, width)
                col_base = (SIDE * (index + h * cols) - first).astype(jnp.float32) + CENTRE
                cs = [None] * 3
                rs = [None] * 3
                for k in (i - 1, i, i + 1):
                    q = slot_of(k, s)
                    v = spread_rows[k + 1][h]
                    cs[q] = v[1:2] + col_base
                    rs[q] = v[0:1] + (SIDE * (k - i) + CENTRE)
                geo_ref[s, i, 2 * h : 2 * h + 1, :] = jnp.where(used, by_slot(cs, cols), -1000.0)
                geo_ref[s, i, 2 * h + 1 : 2 * h + 2, :] = jnp.where(used, by_slot(rs, cols), -1000.0)


def build_weights(col_pos, w_ref):
    base = lax.broadcasted_iota(jnp.int32, (16, LANES), 0).astype(jnp.float32) - col_pos
    left = lane_iota(16) < HALF
    for t in range(w_ref.shape[0] // 16):
        d = base + float(16 * t)
        value = jnp.where(left, 1.0, d)
        w_ref[16 * t : 16 * t + 16, :] = jnp.where(jnp.abs(d) < 10.0, value, 0.0).astype(jnp.bfloat16)


def row_sums(row_pos, r, frames, first_row=0):
    plain = jnp.zeros((frames, LANES), jnp.float32)
    lines = jnp.zeros((frames, LANES), jnp.float32)
    for y in range(r.shape[0] // frames):
        d = float(y + first_row) - row_pos
        inside = jnp.abs(d) < 10.0
        one = jnp.where(inside, 1.0, 0.0)
        centred = jnp.where(inside, d, 0.0)
        piece = r[y * frames : (y + 1) * frames, :]
        plain = plain + one * piece
        lines = lines + centred * piece
    return plain, lines


def block_weights(geo_ref, w_ref):
    for h in range(2):
        build_weights(geo_ref[2 * h : 2 * h + 1, :], w_ref.at[h])


def block_moments(pixels, geo_ref, w_ref, sub_cols, frames, first_row=0):
    out = []
    for h in range(2):
        first, size = half_columns(h, sub_cols, pixels.shape[1])
        r = jnp.dot(
            pixels[:, first : first + size], w_ref[h, 0:size, :], preferred_element_type=jnp.float32
        )
        out.append(row_sums(geo_ref[2 * h + 1 : 2 * h + 2, :], r, frames, first_row))
    return out


def kernel_halo(
    sub_rows, sub_cols, frames, x_hbm, off_hbm, up_ref, down_ref, geo_ref,
    buf, w_ref, p_ref, off_ref, sem, off_sem,
):
    sensors, lines, width = x_hbm.shape
    reach = SHIFT * frames
    last = sub_rows - 1
    cols = sub_cols // 2

    def copy(s, e):
        return pltpu.make_async_copy(
            x_hbm.at[s, pl.ds(e * (lines - reach), reach)], buf.at[s, e], sem.at[s, e]
        )

    off_copy = pltpu.make_async_copy(off_hbm, off_ref, off_sem)
    off_copy.start()
    for s in range(sensors):
        for e in range(2):
            copy(s, e).start()
    off_copy.wait()
    geometry(geo_ref, off_ref, sensors, sub_rows, sub_cols, width)
    for s in range(sensors):
        for e in range(2):
            block_weights(geo_ref.at[s, e * last], w_ref.at[s, e])
    for s in range(sensors):
        for e in range(2):
            copy(s, e).wait()
    for s in range(sensors):
        for e in range(2):
            first_row = e * (SIDE - SHIFT)
            out = block_moments(
                buf.at[s, e], geo_ref.at[s, e * last], w_ref.at[s, e], sub_cols, frames, first_row
            )
            for h in range(2):
                for a in range(2):
                    p_ref[s, e, h, a] = out[h][a]
    left = lane_iota() < HALF
    for ref, e, strip in ((down_ref, 0, -1), (up_ref, 1, sub_rows)):
        pair = []
        for h in range(2):
            both = []
            for a in range(2):
                order = [None] * 3
                for s in range(sensors):
                    order[slot_of(strip, s)] = p_ref[s, e, h, a]
                both.append(by_slot(order, cols))
            ref[h] = both[0]
            pair.append(both[1])
        ref[2] = jnp.where(left, pair[0], pltpu.roll(pair[1], HALF, axis=1))


def slope_terms(plain, lines, mask):
    left = lane_iota() < HALF
    live = mask > 0.0
    flux = jnp.where(left, plain, pltpu.roll(plain, HALF, axis=1))
    moment = jnp.where(left, lines, plain)
    return jnp.where(live, moment / jnp.where(live, flux, 1.0) * mask, 0.0).astype(jnp.bfloat16)


def stacked(modes_ref, picks, half, cols):
    parts = []
    for x in (1, 0):
        used = 0
        for pick in picks:
            if pick is None:
                parts.append(jnp.zeros((cols, modes_ref.shape[-1]), jnp.float32))
            else:
                s, k = pick
                rows = modes_ref[x, s, k].astype(jnp.float32)
                parts.append(rows[half * cols : (half + 1) * cols])
            used += cols
        parts.append(jnp.zeros((HALF - used, modes_ref.shape[-1]), jnp.float32))
    return jnp.concatenate(parts, axis=0).astype(jnp.bfloat16)


def kernel_moments(
    sub_rows, sub_cols, frames, x_ref, geo_ref, mask_ref, modes_ref,
    pm_ref, edge_ref, em_ref, count_ref, w_ref, p_ref,
):
    sensors = x_ref.shape[0]
    block = SIDE * frames
    last = sub_rows - 1
    cols = sub_cols // 2

    def step(s, carry):
        for i in range(sub_rows):
            block_weights(geo_ref.at[s, i], w_ref.at[i])
        for i in range(sub_rows):
            out = block_moments(
                x_ref.at[s, i * block : (i + 1) * block], geo_ref.at[s, i], w_ref.at[i], sub_cols, frames
            )
            for h in range(2):
                for a in range(2):
                    p_ref[s, i, h, a] = out[h][a]
        return carry

    lax.fori_loop(0, sensors, step, 0)

    def strip_total(s, k, h, a):
        total = None
        for i in (k - 1, k, k + 1):
            if 0 <= i <= last:
                v = p_ref[s, i, h, a]
                total = v if total is None else total + v
        return total

    def mask_of(s, k, h):
        return mask_ref[s, k].astype(jnp.float32)[:, h * cols : (h + 1) * cols]

    count = jnp.zeros((frames, LANES), jnp.float32)
    for e, k in enumerate((0, last)):
        order = [None] * 3
        for s in range(sensors):
            order[slot_of(k, s)] = s
        for h in range(2):
            m = side_by_side([mask_of(s, k, h) for s in order])
            em_ref[e, h] = m
            count = count + m
            for a in range(2):
                edge_ref[e, h, a] = by_slot([strip_total(s, k, h, a) for s in order], cols)
    modes = jnp.zeros((frames, modes_ref.shape[-1]), jnp.float32)
    for s in range(sensors):
        for g in range(1, last, 3):
            order = [None] * 3
            for k in range(g, min(g + 3, last)):
                order[slot_of(k, s)] = k
            for h in range(2):
                none = jnp.zeros((frames, cols), jnp.float32)
                mask = side_by_side([none if k is None else mask_of(s, k, h) for k in order])
                count = count + mask
                plain, lines = (
                    by_slot([None if k is None else strip_total(s, k, h, a) for k in order], cols)
                    for a in range(2)
                )
                modes = modes + jnp.dot(
                    slope_terms(plain, lines, mask),
                    stacked(modes_ref, [None if k is None else (s, k) for k in order], h, cols),
                    preferred_element_type=jnp.float32,
                )
    pm_ref[...] = modes
    count_ref[...] = jnp.broadcast_to(0.5 * jnp.sum(count, axis=1, keepdims=True), count_ref.shape)


def kernel_join(
    sub_rows, sub_cols, frames, tiles, blocks,
    live_ref, before_ref, after_ref, pm_ref, edge_ref, em_ref, count_ref, modes_ref, gain_ref, out_ref,
):
    sensors = modes_ref.shape[1]
    last = sub_rows - 1
    cols = sub_cols // 2
    modes = pm_ref[...]
    for e, k in enumerate((0, last)):
        halo_ref = (before_ref, after_ref)[e]
        halo_strip = (sub_rows, -1)[e]
        turn = (slot_of(k, 0) - slot_of(halo_strip, 0)) % 3
        order = [None] * 3
        for s in range(sensors):
            order[slot_of(k, s)] = s
        both = halo_ref[2]
        for h in range(2):
            lines = both if h == 0 else pltpu.roll(both, HALF, axis=1)
            plain = edge_ref[e, h, 0] + rotate(halo_ref[h], turn, cols)
            lines = edge_ref[e, h, 1] + rotate(lines, turn, cols)
            modes = modes + jnp.dot(
                slope_terms(plain, lines, em_ref[e, h]),
                stacked(modes_ref, [None if s is None else (s, k) for s in order], h, cols),
                preferred_element_type=jnp.float32,
            )
    frame = lax.broadcasted_iota(jnp.int32, (frames, 1), 0)
    live = (frame < live_ref[0]).astype(jnp.float32)
    info = gain_ref[...] * modes * live
    own = lane_iota(frames) == lax.broadcasted_iota(jnp.int32, (frames, LANES), 0)
    counts = jnp.sum(jnp.where(own, count_ref[...] * live, 0.0), axis=0, keepdims=True)
    share = modes.shape[1] // tiles
    pack = LANES // share
    rows = frames // pack
    pad = jnp.zeros((out_ref.shape[1] - rows - 1, LANES), jnp.float32)
    for t in range(tiles):
        piece = jnp.concatenate(
            [info[g * rows : (g + 1) * rows, t * share : (t + 1) * share] for g in range(pack)], axis=1
        )
        piece = jnp.concatenate([piece, counts, pad], axis=0)
        for b in range(blocks):
            out_ref[t * blocks + b] = piece


def shifted(x, by, fill, back):
    rows = x.shape[0]
    if by % 8 == 0:
        pad = jnp.full((by, x.shape[1]), fill, x.dtype)
        if back:
            return jnp.concatenate([x[by:], pad], axis=0)
        return jnp.concatenate([pad, x[: rows - by]], axis=0)
    row = lax.broadcasted_iota(jnp.int32, (rows, 1), 0)
    if back:
        return jnp.where(row < rows - by, pltpu.roll(x, rows - by, axis=0), fill)
    return jnp.where(row >= by, pltpu.roll(x, by, axis=0), fill)


def kernel_smooth(
    tiles, blocks, frames, total_subaps, in_ref, noise_ref, gain_ref, mean_ref, var_ref, mean_scr, var_scr
):
    share = mean_ref.shape[1]
    total = blocks * frames
    tile = lax.axis_index("tile")
    time = lax.axis_index("tm")
    pack = LANES // share
    rows = frames // pack

    def own_modes(v):
        out = v[:, 0:share]
        for t in range(1, tiles):
            out = jnp.where(tile == t, v[:, t * share : (t + 1) * share], out)
        return out

    q = own_modes(noise_ref[...])
    gain = own_modes(gain_ref[...])
    own = lane_iota(frames) == lax.broadcasted_iota(jnp.int32, (frames, LANES), 0)
    infos = []
    counts = []
    for b in range(blocks):
        v = in_ref[b]
        for t in range(1, tiles):
            v = v + in_ref[t * blocks + b]
        for g in range(pack):
            infos.append(v[0:rows, g * share : (g + 1) * share])
        counts.append(jnp.sum(jnp.where(own, v[rows : rows + 1], 0.0), axis=1, keepdims=True))
    info_mean = jnp.concatenate(infos, axis=0)
    prec = gain * jnp.concatenate(counts, axis=0) / total_subaps
    row = lax.broadcasted_iota(jnp.int32, (total, 1), 0)
    first = row == 0
    retain = 1.0 / (1.0 + q * prec)
    a = jnp.where(first, 0.0, retain)
    c = jnp.where(first, 1.0 / (1.0 + prec), q * retain)
    b = c * info_mean
    e = a * info_mean
    j = a * prec
    by = 1
    while by < total:
        a1 = shifted(a, by, 1.0, False)
        b1 = shifted(b, by, 0.0, False)
        c1 = shifted(c, by, 0.0, False)
        e1 = shifted(e, by, 0.0, False)
        j1 = shifted(j, by, 0.0, False)
        damp = 1.0 / (1.0 + c1 * j)
        left = a * damp
        right = a1 * damp
        b = left * (b1 + c1 * e) + b
        c = left * a * c1 + c
        e, j = right * (e - j * b1) + e1, right * a1 * j + j1
        a = left * a1
        by *= 2
    g = jnp.where(row == total - 1, 0.0, c / (c + q))
    m = (1.0 - g) * b
    v = c * (1.0 - g)
    by = 1
    while by < total:
        g1 = shifted(g, by, 1.0, True)
        m1 = shifted(m, by, 0.0, True)
        v1 = shifted(v, by, 0.0, True)
        m = g * m1 + m
        v = g * g * v1 + v
        g = g * g1
        by *= 2
    mean_scr[...] = m
    var_scr[...] = v
    start = pl.multiple_of(time * frames, 8)
    mean_ref[...] = mean_scr[pl.ds(start, frames), :]
    var_ref[...] = var_scr[pl.ds(start, frames), :]


def body(pixels, offsets, mask, frame_count, slope_to_modes, process_noise, mode_gain):
    sensors, frames, lines, width = pixels.shape
    sub_rows, sub_cols = mask.shape[2], mask.shape[3]
    modes = process_noise.shape[0]
    tiles = lax.axis_size("tile")
    blocks = lax.axis_size("tm")
    share = modes // tiles
    total_subaps = sensors * sub_rows * tiles * sub_cols
    f32 = jnp.float32
    bf16 = jnp.bfloat16
    x = jnp.transpose(pixels, (0, 2, 1, 3)).reshape(sensors, lines * frames, width)
    off = jnp.transpose(offsets, (0, 1, 3, 2))
    msk = jnp.transpose(mask, (0, 2, 1, 3))
    pixels_v, mask_v, modes_v = (
        pltpu.with_memory_space_constraint(v, pltpu.VMEM) for v in (x, msk, slope_to_modes)
    )
    x, off = (pltpu.with_memory_space_constraint(v, pltpu.HBM) for v in (x, off))
    block = SIDE * frames
    depth = max(half_columns(h, sub_cols, width)[1] for h in range(2))
    params = pltpu.CompilerParams(vmem_limit_bytes=VMEM_LIMIT)

    def cost(chunks):
        return pl.CostEstimate(
            flops=2 * chunks * block * width * 256, bytes_accessed=chunks * block * width * 2, transcendentals=0
        )

    up, down, geo = pl.pallas_call(
        functools.partial(kernel_halo, sub_rows, sub_cols, frames),
        out_shape=(
            jax.ShapeDtypeStruct((3, frames, LANES), f32),
            jax.ShapeDtypeStruct((3, frames, LANES), f32),
            pltpu.VMEM((sensors, sub_rows, 8, LANES), f32),
        ),
        in_specs=[HBM] * 2,
        out_specs=(VMEM,) * 3,
        scratch_shapes=[
            pltpu.VMEM((sensors, 2, SHIFT * frames, width), bf16),
            pltpu.VMEM((sensors, 2, 2, depth, LANES), bf16),
            pltpu.VMEM((sensors, 2, 2, 2, frames, LANES), f32),
            pltpu.VMEM(off.shape, off.dtype),
            pltpu.SemaphoreType.DMA((sensors, 2)),
            pltpu.SemaphoreType.DMA,
        ],
        compiler_params=params,
        cost_estimate=cost(2),
        name="halo_moments",
    )(x, off)
    onward = [(i, i + 1) for i in range(tiles - 1)]
    backward = [(j, i) for i, j in onward]
    from_before = lax.ppermute(up, "tile", onward)
    from_after = lax.ppermute(down, "tile", backward)
    partial_modes, edge, edge_mask, count = pl.pallas_call(
        functools.partial(kernel_moments, sub_rows, sub_cols, frames),
        out_shape=(
            pltpu.VMEM((frames, modes), f32),
            pltpu.VMEM((2, 2, 2, frames, LANES), f32),
            pltpu.VMEM((2, 2, frames, LANES), f32),
            pltpu.VMEM((frames, LANES), f32),
        ),
        in_specs=[VMEM] * 4,
        out_specs=(VMEM,) * 4,
        scratch_shapes=[
            pltpu.VMEM((sub_rows, 2, depth, LANES), bf16),
            pltpu.VMEM((sensors, sub_rows, 2, 2, frames, LANES), f32),
        ],
        compiler_params=params,
        cost_estimate=cost(sensors * sub_rows),
        name="moments",
    )(pixels_v, geo, mask_v, modes_v)
    gain = mode_gain.reshape(1, modes)
    packed = -(-(frames * share // LANES + 1) // 8) * 8
    payload = pl.pallas_call(
        functools.partial(kernel_join, sub_rows, sub_cols, frames, tiles, blocks),
        out_shape=jax.ShapeDtypeStruct((tiles * blocks, packed, LANES), f32),
        in_specs=[pl.BlockSpec(memory_space=pltpu.SMEM)] + [VMEM] * 8,
        out_specs=VMEM,
        compiler_params=params,
        name="join_halo",
    )(frame_count, from_before, from_after, partial_modes, edge, edge_mask, count, modes_v, gain)
    info = lax.all_to_all(payload, ("tile", "tm"), 0, 0)
    return pl.pallas_call(
        functools.partial(kernel_smooth, tiles, blocks, frames, float(total_subaps)),
        out_shape=(
            jax.ShapeDtypeStruct((frames, share), f32),
            jax.ShapeDtypeStruct((frames, share), f32),
        ),
        in_specs=[VMEM] * 3,
        out_specs=(VMEM, VMEM),
        scratch_shapes=[
            pltpu.VMEM((blocks * frames, share), f32),
            pltpu.VMEM((blocks * frames, share), f32),
        ],
        compiler_params=params,
        name="smooth",
    )(info, process_noise.reshape(1, modes), gain)


def solution(mesh):
    return jax.shard_map(
        body,
        mesh=mesh,
        in_specs=(
            P("grp", "tm", "tile", None),
            P("grp", None, None, None),
            P("grp", "tm", "tile", None),
            P(("grp", "tm")),
            P(None, None, "tile", None, None),
            P(),
            P(),
        ),
        out_specs=(P(("grp", "tm"), "tile"), P(("grp", "tm"), "tile")),
        check_vma=False,
    )
```

```python
import functools

import jax
import jax.numpy as jnp
from jax import lax
from jax.experimental import pallas as pl
from jax.experimental.pallas import tpu as pltpu
from jax.sharding import PartitionSpec as P

SIDE = 20
SHIFT = 6
CENTRE = (SIDE - 1) / 2.0
LANES = 128
HALF = LANES // 2
VMEM_LIMIT = 24 * 1024 * 1024
VMEM = pl.BlockSpec(memory_space=pltpu.VMEM)
HBM = pl.BlockSpec(memory_space=pl.ANY)


def slot_of(strip, sensor):
    return (strip + 1 + sensor) % 3


def half_columns(half, sub_cols, width):
    cols = sub_cols // 2
    first = max(0, half * cols * SIDE - SHIFT) // LANES * LANES
    end = min(width, -(-((half + 1) * cols * SIDE + SHIFT) // 16) * 16)
    return first, end - first


def lane_iota(rows=1):
    return lax.broadcasted_iota(jnp.int32, (rows, LANES), 1)


def half_lane(rows=1):
    lane = lane_iota(rows)
    return jnp.where(lane >= HALF, lane - HALF, lane)


def by_slot(values, cols):
    lane = half_lane()
    out = jnp.zeros_like(values[0])
    for q, v in enumerate(values):
        if v is not None:
            out = jnp.where((lane >= q * cols) & (lane < (q + 1) * cols), v, out)
    return out


def side_by_side(pieces):
    rows, cols = pieces[0].shape
    pad = jnp.zeros((rows, HALF - 3 * cols), pieces[0].dtype)
    return jnp.concatenate([*pieces, pad, *pieces, pad], axis=1)


def rotate(x, slots, cols):
    shift = slots * cols
    if shift == 0:
        return x
    near = pltpu.roll(x, shift, axis=1)
    far = pltpu.roll(x, LANES - 3 * cols + shift, axis=1)
    return jnp.where(half_lane() >= shift, near, far)


def geometry(geo_ref, off_ref, sensors, sub_rows, sub_cols, width):
    cols = sub_cols // 2
    lane = half_lane()
    index = lane - cols * (lane >= cols).astype(jnp.int32)
    index = index - cols * (lane >= 2 * cols).astype(jnp.int32)
    used = lane < 3 * cols
    tile = lax.axis_index("tile")
    total_rows = off_ref.shape[1]
    for s in range(sensors):
        spread_rows = []
        for k in range(-1, sub_rows + 1):
            row = jnp.clip(tile * sub_rows + k, 0, total_rows - 1)
            v = off_ref[s, row].astype(jnp.float32)
            spread_rows.append([side_by_side([v[:, h * cols : (h + 1) * cols]] * 3) for h in range(2)])
        for i in range(sub_rows):
            for h in range(2):
                first, _ = half_columns(h, sub_cols, width)
                col_base = (SIDE * (index + h * cols) - first).astype(jnp.float32) + CENTRE
                cs = [None] * 3
                rs = [None] * 3
                for k in (i - 1, i, i + 1):
                    q = slot_of(k, s)
                    v = spread_rows[k + 1][h]
                    cs[q] = v[1:2] + col_base
                    rs[q] = v[0:1] + (SIDE * (k - i) + CENTRE)
                geo_ref[s, i, 2 * h : 2 * h + 1, :] = jnp.where(used, by_slot(cs, cols), -1000.0)
                geo_ref[s, i, 2 * h + 1 : 2 * h + 2, :] = jnp.where(used, by_slot(rs, cols), -1000.0)


def build_weights(col_pos, w_ref):
    base = lax.broadcasted_iota(jnp.int32, (16, LANES), 0).astype(jnp.float32) - col_pos
    left = lane_iota(16) < HALF
    for t in range(w_ref.shape[0] // 16):
        d = base + float(16 * t)
        value = jnp.where(left, 1.0, d)
        w_ref[16 * t : 16 * t + 16, :] = jnp.where(jnp.abs(d) < 10.0, value, 0.0).astype(jnp.bfloat16)


def row_sums(row_pos, r, frames, first_row=0):
    plain = jnp.zeros((frames, LANES), jnp.float32)
    lines = jnp.zeros((frames, LANES), jnp.float32)
    for y in range(r.shape[0] // frames):
        d = float(y + first_row) - row_pos
        inside = jnp.abs(d) < 10.0
        one = jnp.where(inside, 1.0, 0.0)
        centred = jnp.where(inside, d, 0.0)
        piece = r[y * frames : (y + 1) * frames, :]
        plain = plain + one * piece
        lines = lines + centred * piece
    return plain, lines


def block_weights(geo_ref, w_ref):
    for h in range(2):
        build_weights(geo_ref[2 * h : 2 * h + 1, :], w_ref.at[h])


def block_moments(pixels, geo_ref, w_ref, sub_cols, frames, first_row=0):
    out = []
    for h in range(2):
        first, size = half_columns(h, sub_cols, pixels.shape[1])
        r = jnp.dot(
            pixels[:, first : first + size], w_ref[h, 0:size, :], preferred_element_type=jnp.float32
        )
        out.append(row_sums(geo_ref[2 * h + 1 : 2 * h + 2, :], r, frames, first_row))
    return out


def kernel_halo(
    sub_rows, sub_cols, frames, x_hbm, off_hbm, mask_hbm, modes_hbm,
    up_ref, down_ref, geo_ref, w_ref, mask_ref, modes_ref,
    buf, p_ref, off_ref, sem, side_sem,
):
    sensors, lines, width = x_hbm.shape
    reach = SHIFT * frames
    last = sub_rows - 1
    cols = sub_cols // 2

    def copy(s, e):
        return pltpu.make_async_copy(
            x_hbm.at[s, pl.ds(e * (lines - reach), reach)], buf.at[s, e], sem.at[s, e]
        )

    off_copy = pltpu.make_async_copy(off_hbm, off_ref, side_sem.at[0])
    mask_copy = pltpu.make_async_copy(mask_hbm, mask_ref, side_sem.at[1])
    modes_copy = pltpu.make_async_copy(modes_hbm, modes_ref, side_sem.at[2])
    off_copy.start()
    for s in range(sensors):
        for e in range(2):
            copy(s, e).start()
    mask_copy.start()
    modes_copy.start()
    off_copy.wait()
    geometry(geo_ref, off_ref, sensors, sub_rows, sub_cols, width)
    for s in range(sensors):
        for e in range(2):
            block_weights(geo_ref.at[s, e * last], w_ref.at[s, e])
    for s in range(sensors):
        for e in range(2):
            copy(s, e).wait()
    for s in range(sensors):
        for e in range(2):
            first_row = e * (SIDE - SHIFT)
            out = block_moments(
                buf.at[s, e], geo_ref.at[s, e * last], w_ref.at[s, e], sub_cols, frames, first_row
            )
            for h in range(2):
                for a in range(2):
                    p_ref[s, e, h, a] = out[h][a]
    left = lane_iota() < HALF
    for ref, e, strip in ((down_ref, 0, -1), (up_ref, 1, sub_rows)):
        pair = []
        for h in range(2):
            both = []
            for a in range(2):
                order = [None] * 3
                for s in range(sensors):
                    order[slot_of(strip, s)] = p_ref[s, e, h, a]
                both.append(by_slot(order, cols))
            ref[h] = both[0]
            pair.append(both[1])
        ref[2] = jnp.where(left, pair[0], pltpu.roll(pair[1], HALF, axis=1))
    mask_copy.wait()
    modes_copy.wait()


def slope_terms(plain, lines, mask):
    left = lane_iota() < HALF
    live = mask > 0.0
    flux = jnp.where(left, plain, pltpu.roll(plain, HALF, axis=1))
    moment = jnp.where(left, lines, plain)
    return jnp.where(live, moment / jnp.where(live, flux, 1.0) * mask, 0.0).astype(jnp.bfloat16)


def stacked(modes_ref, picks, half, cols):
    parts = []
    for x in (1, 0):
        used = 0
        for pick in picks:
            if pick is None:
                parts.append(jnp.zeros((cols, modes_ref.shape[-1]), jnp.float32))
            else:
                s, k = pick
                rows = modes_ref[x, s, k].astype(jnp.float32)
                parts.append(rows[half * cols : (half + 1) * cols])
            used += cols
        parts.append(jnp.zeros((HALF - used, modes_ref.shape[-1]), jnp.float32))
    return jnp.concatenate(parts, axis=0).astype(jnp.bfloat16)


def kernel_moments(
    sub_rows, sub_cols, frames, x_ref, geo_ref, edge_w_ref, mask_ref, modes_ref,
    pm_ref, edge_ref, em_ref, count_ref, w_ref, p_ref,
):
    sensors = x_ref.shape[0]
    block = SIDE * frames
    last = sub_rows - 1
    cols = sub_cols // 2

    def step(s, carry):
        for i in range(1, last):
            block_weights(geo_ref.at[s, i], w_ref.at[i - 1])
        for i in range(sub_rows):
            weights = edge_w_ref.at[s, i // last] if i in (0, last) else w_ref.at[i - 1]
            out = block_moments(
                x_ref.at[s, i * block : (i + 1) * block], geo_ref.at[s, i], weights, sub_cols, frames
            )
            for h in range(2):
                for a in range(2):
                    p_ref[s, i, h, a] = out[h][a]
        return carry

    lax.fori_loop(0, sensors, step, 0)

    def strip_total(s, k, h, a):
        total = None
        for i in (k - 1, k, k + 1):
            if 0 <= i <= last:
                v = p_ref[s, i, h, a]
                total = v if total is None else total + v
        return total

    def mask_of(s, k, h):
        return mask_ref[s, k].astype(jnp.float32)[:, h * cols : (h + 1) * cols]

    count = jnp.zeros((frames, LANES), jnp.float32)
    for e, k in enumerate((0, last)):
        order = [None] * 3
        for s in range(sensors):
            order[slot_of(k, s)] = s
        for h in range(2):
            m = side_by_side([mask_of(s, k, h) for s in order])
            em_ref[e, h] = m
            count = count + m
            for a in range(2):
                edge_ref[e, h, a] = by_slot([strip_total(s, k, h, a) for s in order], cols)
    modes = jnp.zeros((frames, modes_ref.shape[-1]), jnp.float32)
    for s in range(sensors):
        for g in range(1, last, 3):
            order = [None] * 3
            for k in range(g, min(g + 3, last)):
                order[slot_of(k, s)] = k
            for h in range(2):
                none = jnp.zeros((frames, cols), jnp.float32)
                mask = side_by_side([none if k is None else mask_of(s, k, h) for k in order])
                count = count + mask
                plain, lines = (
                    by_slot([None if k is None else strip_total(s, k, h, a) for k in order], cols)
                    for a in range(2)
                )
                modes = modes + jnp.dot(
                    slope_terms(plain, lines, mask),
                    stacked(modes_ref, [None if k is None else (s, k) for k in order], h, cols),
                    preferred_element_type=jnp.float32,
                )
    pm_ref[...] = modes
    count_ref[...] = jnp.broadcast_to(0.5 * jnp.sum(count, axis=1, keepdims=True), count_ref.shape)


def kernel_join(
    sub_rows, sub_cols, frames, tiles, blocks,
    live_ref, before_ref, after_ref, pm_ref, edge_ref, em_ref, count_ref, modes_ref, gain_ref, out_ref,
):
    sensors = modes_ref.shape[1]
    last = sub_rows - 1
    cols = sub_cols // 2
    modes = pm_ref[...]
    for e, k in enumerate((0, last)):
        halo_ref = (before_ref, after_ref)[e]
        halo_strip = (sub_rows, -1)[e]
        turn = (slot_of(k, 0) - slot_of(halo_strip, 0)) % 3
        order = [None] * 3
        for s in range(sensors):
            order[slot_of(k, s)] = s
        both = halo_ref[2]
        for h in range(2):
            lines = both if h == 0 else pltpu.roll(both, HALF, axis=1)
            plain = edge_ref[e, h, 0] + rotate(halo_ref[h], turn, cols)
            lines = edge_ref[e, h, 1] + rotate(lines, turn, cols)
            modes = modes + jnp.dot(
                slope_terms(plain, lines, em_ref[e, h]),
                stacked(modes_ref, [None if s is None else (s, k) for s in order], h, cols),
                preferred_element_type=jnp.float32,
            )
    frame = lax.broadcasted_iota(jnp.int32, (frames, 1), 0)
    live = (frame < live_ref[0]).astype(jnp.float32)
    info = gain_ref[...] * modes * live
    own = lane_iota(frames) == lax.broadcasted_iota(jnp.int32, (frames, LANES), 0)
    counts = jnp.sum(jnp.where(own, count_ref[...] * live, 0.0), axis=0, keepdims=True)
    share = modes.shape[1] // tiles
    pack = LANES // share
    rows = frames // pack
    pad = jnp.zeros((out_ref.shape[1] - rows - 1, LANES), jnp.float32)
    for t in range(tiles):
        piece = jnp.concatenate(
            [info[g * rows : (g + 1) * rows, t * share : (t + 1) * share] for g in range(pack)], axis=1
        )
        piece = jnp.concatenate([piece, counts, pad], axis=0)
        for b in range(blocks):
            out_ref[t * blocks + b] = piece


def shifted(x, by, fill, back):
    rows = x.shape[0]
    if by % 8 == 0:
        pad = jnp.full((by, x.shape[1]), fill, x.dtype)
        if back:
            return jnp.concatenate([x[by:], pad], axis=0)
        return jnp.concatenate([pad, x[: rows - by]], axis=0)
    row = lax.broadcasted_iota(jnp.int32, (rows, 1), 0)
    if back:
        return jnp.where(row < rows - by, pltpu.roll(x, rows - by, axis=0), fill)
    return jnp.where(row >= by, pltpu.roll(x, by, axis=0), fill)


def kernel_smooth(
    tiles, blocks, frames, total_subaps, in_ref, noise_ref, gain_ref, mean_ref, var_ref, mean_scr, var_scr
):
    share = mean_ref.shape[1]
    total = blocks * frames
    tile = lax.axis_index("tile")
    time = lax.axis_index("tm")
    pack = LANES // share
    rows = frames // pack

    def own_modes(v):
        out = v[:, 0:share]
        for t in range(1, tiles):
            out = jnp.where(tile == t, v[:, t * share : (t + 1) * share], out)
        return out

    q = own_modes(noise_ref[...])
    gain = own_modes(gain_ref[...])
    own = lane_iota(frames) == lax.broadcasted_iota(jnp.int32, (frames, LANES), 0)
    infos = []
    counts = []
    for b in range(blocks):
        v = in_ref[b]
        for t in range(1, tiles):
            v = v + in_ref[t * blocks + b]
        for g in range(pack):
            infos.append(v[0:rows, g * share : (g + 1) * share])
        counts.append(jnp.sum(jnp.where(own, v[rows : rows + 1], 0.0), axis=1, keepdims=True))
    info_mean = jnp.concatenate(infos, axis=0)
    prec = gain * jnp.concatenate(counts, axis=0) / total_subaps
    row = lax.broadcasted_iota(jnp.int32, (total, 1), 0)
    first = row == 0
    retain = 1.0 / (1.0 + q * prec)
    a = jnp.where(first, 0.0, retain)
    c = jnp.where(first, 1.0 / (1.0 + prec), q * retain)
    b = c * info_mean
    e = a * info_mean
    j = a * prec
    by = 1
    while by < total:
        a1 = shifted(a, by, 1.0, False)
        b1 = shifted(b, by, 0.0, False)
        c1 = shifted(c, by, 0.0, False)
        e1 = shifted(e, by, 0.0, False)
        j1 = shifted(j, by, 0.0, False)
        damp = 1.0 / (1.0 + c1 * j)
        left = a * damp
        right = a1 * damp
        b = left * (b1 + c1 * e) + b
        c = left * a * c1 + c
        e, j = right * (e - j * b1) + e1, right * a1 * j + j1
        a = left * a1
        by *= 2
    g = jnp.where(row == total - 1, 0.0, c / (c + q))
    m = (1.0 - g) * b
    v = c * (1.0 - g)
    by = 1
    while by < total:
        g1 = shifted(g, by, 1.0, True)
        m1 = shifted(m, by, 0.0, True)
        v1 = shifted(v, by, 0.0, True)
        m = g * m1 + m
        v = g * g * v1 + v
        g = g * g1
        by *= 2
    mean_scr[...] = m
    var_scr[...] = v
    start = pl.multiple_of(time * frames, 8)
    mean_ref[...] = mean_scr[pl.ds(start, frames), :]
    var_ref[...] = var_scr[pl.ds(start, frames), :]


def body(pixels, offsets, mask, frame_count, slope_to_modes, process_noise, mode_gain):
    sensors, frames, lines, width = pixels.shape
    sub_rows, sub_cols = mask.shape[2], mask.shape[3]
    modes = process_noise.shape[0]
    tiles = lax.axis_size("tile")
    blocks = lax.axis_size("tm")
    share = modes // tiles
    total_subaps = sensors * sub_rows * tiles * sub_cols
    f32 = jnp.float32
    bf16 = jnp.bfloat16
    x = jnp.transpose(pixels, (0, 2, 1, 3)).reshape(sensors, lines * frames, width)
    off = jnp.transpose(offsets, (0, 1, 3, 2))
    msk = jnp.transpose(mask, (0, 2, 1, 3))
    pixels_v = pltpu.with_memory_space_constraint(x, pltpu.VMEM)
    x, off, msk, slope_to_modes = (
        pltpu.with_memory_space_constraint(v, pltpu.HBM) for v in (x, off, msk, slope_to_modes)
    )
    block = SIDE * frames
    depth = max(half_columns(h, sub_cols, width)[1] for h in range(2))
    params = pltpu.CompilerParams(vmem_limit_bytes=VMEM_LIMIT)

    def cost(chunks):
        return pl.CostEstimate(
            flops=2 * chunks * block * width * 256, bytes_accessed=chunks * block * width * 2, transcendentals=0
        )

    up, down, geo, edge_weights, mask_v, modes_v = pl.pallas_call(
        functools.partial(kernel_halo, sub_rows, sub_cols, frames),
        out_shape=(
            jax.ShapeDtypeStruct((3, frames, LANES), f32),
            jax.ShapeDtypeStruct((3, frames, LANES), f32),
            pltpu.VMEM((sensors, sub_rows, 8, LANES), f32),
            pltpu.VMEM((sensors, 2, 2, depth, LANES), bf16),
            pltpu.VMEM(msk.shape, msk.dtype),
            pltpu.VMEM(slope_to_modes.shape, bf16),
        ),
        in_specs=[HBM] * 4,
        out_specs=(VMEM,) * 6,
        scratch_shapes=[
            pltpu.VMEM((sensors, 2, SHIFT * frames, width), bf16),
            pltpu.VMEM((sensors, 2, 2, 2, frames, LANES), f32),
            pltpu.VMEM(off.shape, off.dtype),
            pltpu.SemaphoreType.DMA((sensors, 2)),
            pltpu.SemaphoreType.DMA((3,)),
        ],
        compiler_params=params,
        cost_estimate=cost(2),
        name="halo_moments",
    )(x, off, msk, slope_to_modes)
    onward = [(i, i + 1) for i in range(tiles - 1)]
    backward = [(j, i) for i, j in onward]
    from_before = lax.ppermute(up, "tile", onward)
    from_after = lax.ppermute(down, "tile", backward)
    partial_modes, edge, edge_mask, count = pl.pallas_call(
        functools.partial(kernel_moments, sub_rows, sub_cols, frames),
        out_shape=(
            pltpu.VMEM((frames, modes), f32),
            pltpu.VMEM((2, 2, 2, frames, LANES), f32),
            pltpu.VMEM((2, 2, frames, LANES), f32),
            pltpu.VMEM((frames, LANES), f32),
        ),
        in_specs=[VMEM] * 5,
        out_specs=(VMEM,) * 4,
        scratch_shapes=[
            pltpu.VMEM((sub_rows - 2, 2, depth, LANES), bf16),
            pltpu.VMEM((sensors, sub_rows, 2, 2, frames, LANES), f32),
        ],
        compiler_params=params,
        cost_estimate=cost(sensors * sub_rows),
        name="moments",
    )(pixels_v, geo, edge_weights, mask_v, modes_v)
    gain = mode_gain.reshape(1, modes)
    packed = -(-(frames * share // LANES + 1) // 8) * 8
    payload = pl.pallas_call(
        functools.partial(kernel_join, sub_rows, sub_cols, frames, tiles, blocks),
        out_shape=jax.ShapeDtypeStruct((tiles * blocks, packed, LANES), f32),
        in_specs=[pl.BlockSpec(memory_space=pltpu.SMEM)] + [VMEM] * 8,
        out_specs=VMEM,
        compiler_params=params,
        name="join_halo",
    )(frame_count, from_before, from_after, partial_modes, edge, edge_mask, count, modes_v, gain)
    info = lax.all_to_all(payload, ("tile", "tm"), 0, 0)
    return pl.pallas_call(
        functools.partial(kernel_smooth, tiles, blocks, frames, float(total_subaps)),
        out_shape=(
            jax.ShapeDtypeStruct((frames, share), f32),
            jax.ShapeDtypeStruct((frames, share), f32),
        ),
        in_specs=[VMEM] * 3,
        out_specs=(VMEM, VMEM),
        scratch_shapes=[
            pltpu.VMEM((blocks * frames, share), f32),
            pltpu.VMEM((blocks * frames, share), f32),
        ],
        compiler_params=params,
        name="smooth",
    )(info, process_noise.reshape(1, modes), gain)


def solution(mesh):
    return jax.shard_map(
        body,
        mesh=mesh,
        in_specs=(
            P("grp", "tm", "tile", None),
            P("grp", None, None, None),
            P("grp", "tm", "tile", None),
            P(("grp", "tm")),
            P(None, None, "tile", None, None),
            P(),
            P(),
        ),
        out_specs=(P(("grp", "tm"), "tile"), P(("grp", "tm"), "tile")),
        check_vma=False,
    )
```

```python
import functools

import jax
import jax.numpy as jnp
from jax import lax
from jax.experimental import pallas as pl
from jax.experimental.pallas import tpu as pltpu
from jax.sharding import PartitionSpec as P

SIDE = 20
SHIFT = 6
CENTRE = (SIDE - 1) / 2.0
LANES = 128
HALF = LANES // 2
TILE = 2 * LANES
VMEM_LIMIT = 24 * 1024 * 1024
VMEM = pl.BlockSpec(memory_space=pltpu.VMEM)
HBM = pl.BlockSpec(memory_space=pl.ANY)


def slot_of(strip, sensor):
    return (strip + 1 + sensor) % 3


def half_columns(half, sub_cols, width):
    cols = sub_cols // 2
    first = max(0, half * cols * SIDE - SHIFT) // LANES * LANES
    end = min(width, -(-((half + 1) * cols * SIDE + SHIFT) // 16) * 16)
    return first, end - first


def lane_iota(rows=1):
    return lax.broadcasted_iota(jnp.int32, (rows, LANES), 1)


def half_lane(rows=1):
    lane = lane_iota(rows)
    return jnp.where(lane >= HALF, lane - HALF, lane)


def by_slot(values, cols):
    lane = half_lane()
    out = jnp.zeros_like(values[0])
    for q, v in enumerate(values):
        if v is not None:
            out = jnp.where((lane >= q * cols) & (lane < (q + 1) * cols), v, out)
    return out


def side_by_side(pieces):
    rows, cols = pieces[0].shape
    group = jnp.concatenate([*pieces, jnp.zeros((rows, HALF - 3 * cols), pieces[0].dtype)], axis=1)
    return jnp.concatenate([group, group], axis=1)


def rotate(x, slots, cols):
    shift = slots * cols
    if shift == 0:
        return x
    near = pltpu.roll(x, shift, axis=1)
    far = pltpu.roll(x, LANES - 3 * cols + shift, axis=1)
    return jnp.where(half_lane() >= shift, near, far)


def geometry(geo_ref, off_ref, table_ref, spread_ref, sensors, sub_rows, sub_cols, width):
    cols = sub_cols // 2
    lane = half_lane()
    index = lane - cols * (lane >= cols).astype(jnp.int32)
    index = index - cols * (lane >= 2 * cols).astype(jnp.int32)
    used = lane < 3 * cols
    tile = lax.axis_index("tile")
    total_rows = off_ref.shape[1]
    for s in range(sensors):
        for k in range(-1, sub_rows + 1):
            row = jnp.clip(tile * sub_rows + k, 0, total_rows - 1)
            n = 2 * (s * (sub_rows + 2) + k + 1)
            table_ref[n : n + 2, :] = off_ref[s, row].astype(jnp.float32)
    table = table_ref[...]
    for h in range(2):
        spread_ref[h] = side_by_side([table[:, h * cols : (h + 1) * cols]] * 3)
    for s in range(sensors):
        for i in range(sub_rows):
            for h in range(2):
                first, _ = half_columns(h, sub_cols, width)
                col_base = (SIDE * (index + h * cols) - first).astype(jnp.float32) + CENTRE
                cs = [None] * 3
                rs = [None] * 3
                for k in (i - 1, i, i + 1):
                    q = slot_of(k, s)
                    n = 2 * (s * (sub_rows + 2) + k + 1)
                    cs[q] = spread_ref[h, n + 1 : n + 2, :]
                    rs[q] = spread_ref[h, n : n + 1, :] + (SIDE * (k - i) + CENTRE)
                geo_ref[s, i, 2 * h : 2 * h + 1, :] = jnp.where(used, by_slot(cs, cols) + col_base, -1000.0)
                geo_ref[s, i, 2 * h + 1 : 2 * h + 2, :] = jnp.where(used, by_slot(rs, cols), -1000.0)


def window_weights(col_pos, first, count):
    base = lax.broadcasted_iota(jnp.int32, (16, LANES), 0).astype(jnp.float32) - col_pos
    left = lane_iota(16) < HALF
    for t in range(count // 16):
        d = base + float(16 * t)
        value = jnp.where(left, 1.0, d)
        yield first + 16 * t, jnp.where(jnp.abs(d) < 10.0, value, 0.0).astype(jnp.bfloat16)


def clear_weights(wide_ref, rest):
    zero = jnp.zeros((16, LANES), jnp.bfloat16)
    for n in range(wide_ref.shape[0]):
        for t in range(0, TILE, 16):
            wide_ref[n, t : t + 16, 0:LANES] = zero
            wide_ref[n, t : t + 16, LANES:] = zero
        for t in range(0, rest, 16):
            wide_ref[n, TILE + t : TILE + t + 16, LANES:] = zero
            wide_ref[n, TILE + rest + t : TILE + rest + t + 16, 0:LANES] = zero


def block_weights(geo_ref, narrow_ref, wide_ref, sub_cols, width):
    rest = width - 3 * TILE
    for h in range(2):
        first, count = half_columns(h, sub_cols, width)
        lanes = slice(h * LANES, (h + 1) * LANES)
        for c, piece in window_weights(geo_ref[2 * h : 2 * h + 1, :], first, count):
            if c < TILE:
                narrow_ref[0, c : c + 16, :] = piece
            elif c < 2 * TILE:
                wide_ref[c - TILE : c - TILE + 16, lanes] = piece
            elif c < 3 * TILE:
                narrow_ref[1, c - 2 * TILE : c - 2 * TILE + 16, :] = piece
            else:
                at = c - 2 * TILE
                wide_ref[at : at + 16, 0:LANES] = piece
                wide_ref[at + rest : at + rest + 16, LANES:] = piece


def block_moments(pixels, geo_ref, narrow_ref, wide_ref, frames, first_row=0):
    f32 = jnp.float32
    rows, width = pixels.shape
    rest = width - 3 * TILE
    a = jnp.dot(pixels[:, 0:TILE], narrow_ref[0], preferred_element_type=f32)
    m = jnp.dot(pixels[:, TILE : 2 * TILE], wide_ref[0:TILE, :], preferred_element_type=f32)
    b = jnp.dot(pixels[:, 2 * TILE : 3 * TILE], narrow_ref[1], preferred_element_type=f32)
    split = rows // 2 if (rows // 2) % 16 == 0 else rows
    tail = pixels[0:split, 3 * TILE :]
    if split < rows:
        tail = jnp.concatenate([tail, pixels[split:, 3 * TILE :]], axis=1)
        r = jnp.dot(tail, wide_ref[TILE:, :], preferred_element_type=f32)
    else:
        r = jnp.dot(tail, wide_ref[TILE : TILE + rest, 0:LANES], preferred_element_type=f32)
    out = [[jnp.zeros((frames, LANES), f32) for _ in range(2)] for _ in range(2)]
    for y in range(rows // frames):
        at = slice(y * frames, (y + 1) * frames)
        if y * frames < split:
            extra = r[at, 0:LANES]
        else:
            extra = r[y * frames - split : (y + 1) * frames - split, LANES:]
        pieces = (a[at] + m[at, 0:LANES], m[at, LANES:] + b[at] + extra)
        for h in range(2):
            d = float(y + first_row) - geo_ref[2 * h + 1 : 2 * h + 2, :]
            inside = jnp.abs(d) < 10.0
            out[h][0] = out[h][0] + jnp.where(inside, 1.0, 0.0) * pieces[h]
            out[h][1] = out[h][1] + jnp.where(inside, d, 0.0) * pieces[h]
    return out


def kernel_halo(
    sub_rows, sub_cols, frames, x_hbm, off_hbm, mask_hbm, modes_hbm,
    up_ref, down_ref, geo_ref, narrow_ref, wide_ref, mask_ref, modes_ref,
    buf, p_ref, off_ref, table_ref, spread_ref, sem, side_sem,
):
    sensors, lines, width = x_hbm.shape
    reach = SHIFT * frames
    last = sub_rows - 1
    cols = sub_cols // 2

    def copy(s, e):
        return pltpu.make_async_copy(
            x_hbm.at[s, pl.ds(e * (lines - reach), reach)], buf.at[s, e], sem.at[s, e]
        )

    off_copy = pltpu.make_async_copy(off_hbm, off_ref, side_sem.at[0])
    mask_copy = pltpu.make_async_copy(mask_hbm, mask_ref, side_sem.at[1])
    modes_copy = pltpu.make_async_copy(modes_hbm, modes_ref, side_sem.at[2])
    off_copy.start()
    for s in range(sensors):
        for e in range(2):
            copy(s, e).start()
    mask_copy.start()
    modes_copy.start()
    for s in range(sensors):
        clear_weights(wide_ref.at[s], width - 3 * TILE)
    off_copy.wait()
    geometry(geo_ref, off_ref, table_ref, spread_ref, sensors, sub_rows, sub_cols, width)
    for s in range(sensors):
        for e in range(2):
            block_weights(geo_ref.at[s, e * last], narrow_ref.at[s, e], wide_ref.at[s, e], sub_cols, width)
    for s in range(sensors):
        for e in range(2):
            copy(s, e).wait()
    for s in range(sensors):
        for e in range(2):
            first_row = e * (SIDE - SHIFT)
            out = block_moments(
                buf.at[s, e], geo_ref.at[s, e * last], narrow_ref.at[s, e], wide_ref.at[s, e], frames, first_row
            )
            for h in range(2):
                for a in range(2):
                    p_ref[s, e, h, a] = out[h][a]
    left = lane_iota() < HALF
    for ref, e, strip in ((down_ref, 0, -1), (up_ref, 1, sub_rows)):
        pair = []
        for h in range(2):
            both = []
            for a in range(2):
                order = [None] * 3
                for s in range(sensors):
                    order[slot_of(strip, s)] = p_ref[s, e, h, a]
                both.append(by_slot(order, cols))
            ref[h] = both[0]
            pair.append(both[1])
        ref[2] = jnp.where(left, pair[0], pltpu.roll(pair[1], HALF, axis=1))
    mask_copy.wait()
    modes_copy.wait()


def slope_terms(plain, lines, mask):
    left = lane_iota() < HALF
    live = mask > 0.0
    flux = jnp.where(left, plain, pltpu.roll(plain, HALF, axis=1))
    moment = jnp.where(left, lines, plain)
    return jnp.where(live, moment / jnp.where(live, flux, 1.0) * mask, 0.0).astype(jnp.bfloat16)


def stacked(modes_ref, picks, half, cols):
    parts = []
    for x in (1, 0):
        used = 0
        for pick in picks:
            if pick is None:
                parts.append(jnp.zeros((cols, modes_ref.shape[-1]), jnp.float32))
            else:
                s, k = pick
                rows = modes_ref[x, s, k].astype(jnp.float32)
                parts.append(rows[half * cols : (half + 1) * cols])
            used += cols
        parts.append(jnp.zeros((HALF - used, modes_ref.shape[-1]), jnp.float32))
    return jnp.concatenate(parts, axis=0).astype(jnp.bfloat16)


def kernel_moments(
    sub_rows, sub_cols, frames, x_ref, geo_ref, edge_narrow_ref, edge_wide_ref, mask_ref, modes_ref,
    pm_ref, edge_ref, em_ref, count_ref, narrow_ref, wide_ref, p_ref,
):
    sensors = x_ref.shape[0]
    block = SIDE * frames
    last = sub_rows - 1
    cols = sub_cols // 2

    width = x_ref.shape[2]
    clear_weights(wide_ref, width - 3 * TILE)

    def step(s, carry):
        for i in range(1, last):
            block_weights(geo_ref.at[s, i], narrow_ref.at[i - 1], wide_ref.at[i - 1], sub_cols, width)
        for i in range(sub_rows):
            if i in (0, last):
                weights = (edge_narrow_ref.at[s, i // last], edge_wide_ref.at[s, i // last])
            else:
                weights = (narrow_ref.at[i - 1], wide_ref.at[i - 1])
            out = block_moments(
                x_ref.at[s, i * block : (i + 1) * block], geo_ref.at[s, i], *weights, frames
            )
            for h in range(2):
                for a in range(2):
                    p_ref[s, i, h, a] = out[h][a]
        return carry

    lax.fori_loop(0, sensors, step, 0)

    def strip_total(s, k, h, a):
        total = None
        for i in (k - 1, k, k + 1):
            if 0 <= i <= last:
                v = p_ref[s, i, h, a]
                total = v if total is None else total + v
        return total

    def mask_of(s, k, h):
        return mask_ref[s, k].astype(jnp.float32)[:, h * cols : (h + 1) * cols]

    count = jnp.zeros((frames, LANES), jnp.float32)
    for e, k in enumerate((0, last)):
        order = [None] * 3
        for s in range(sensors):
            order[slot_of(k, s)] = s
        for h in range(2):
            m = side_by_side([mask_of(s, k, h) for s in order])
            em_ref[e, h] = m
            count = count + m
            for a in range(2):
                edge_ref[e, h, a] = by_slot([strip_total(s, k, h, a) for s in order], cols)
    modes = jnp.zeros((frames, modes_ref.shape[-1]), jnp.float32)
    for s in range(sensors):
        for g in range(1, last, 3):
            order = [None] * 3
            for k in range(g, min(g + 3, last)):
                order[slot_of(k, s)] = k
            for h in range(2):
                none = jnp.zeros((frames, cols), jnp.float32)
                mask = side_by_side([none if k is None else mask_of(s, k, h) for k in order])
                count = count + mask
                plain, lines = (
                    by_slot([None if k is None else strip_total(s, k, h, a) for k in order], cols)
                    for a in range(2)
                )
                modes = modes + jnp.dot(
                    slope_terms(plain, lines, mask),
                    stacked(modes_ref, [None if k is None else (s, k) for k in order], h, cols),
                    preferred_element_type=jnp.float32,
                )
    pm_ref[...] = modes
    count_ref[...] = jnp.broadcast_to(0.5 * jnp.sum(count, axis=1, keepdims=True), count_ref.shape)


def kernel_join(
    sub_rows, sub_cols, frames, tiles, blocks,
    live_ref, before_ref, after_ref, pm_ref, edge_ref, em_ref, count_ref, modes_ref, gain_ref, out_ref,
):
    sensors = modes_ref.shape[1]
    last = sub_rows - 1
    cols = sub_cols // 2
    modes = pm_ref[...]
    for e, k in enumerate((0, last)):
        halo_ref = (before_ref, after_ref)[e]
        halo_strip = (sub_rows, -1)[e]
        turn = (slot_of(k, 0) - slot_of(halo_strip, 0)) % 3
        order = [None] * 3
        for s in range(sensors):
            order[slot_of(k, s)] = s
        both = halo_ref[2]
        for h in range(2):
            lines = both if h == 0 else pltpu.roll(both, HALF, axis=1)
            plain = edge_ref[e, h, 0] + rotate(halo_ref[h], turn, cols)
            lines = edge_ref[e, h, 1] + rotate(lines, turn, cols)
            modes = modes + jnp.dot(
                slope_terms(plain, lines, em_ref[e, h]),
                stacked(modes_ref, [None if s is None else (s, k) for s in order], h, cols),
                preferred_element_type=jnp.float32,
            )
    frame = lax.broadcasted_iota(jnp.int32, (frames, 1), 0)
    live = (frame < live_ref[0]).astype(jnp.float32)
    info = gain_ref[...] * modes * live
    own = lane_iota(frames) == lax.broadcasted_iota(jnp.int32, (frames, LANES), 0)
    counts = jnp.sum(jnp.where(own, count_ref[...] * live, 0.0), axis=0, keepdims=True)
    share = modes.shape[1] // tiles
    pack = LANES // share
    rows = frames // pack
    pad = jnp.zeros((out_ref.shape[1] - rows - 1, LANES), jnp.float32)
    for t in range(tiles):
        piece = jnp.concatenate(
            [info[g * rows : (g + 1) * rows, t * share : (t + 1) * share] for g in range(pack)], axis=1
        )
        piece = jnp.concatenate([piece, counts, pad], axis=0)
        for b in range(blocks):
            out_ref[t * blocks + b] = piece


def shifted(x, by, fill, back):
    rows = x.shape[0]
    if by % 8 == 0:
        pad = jnp.full((by, x.shape[1]), fill, x.dtype)
        if back:
            return jnp.concatenate([x[by:], pad], axis=0)
        return jnp.concatenate([pad, x[: rows - by]], axis=0)
    row = lax.broadcasted_iota(jnp.int32, (rows, 1), 0)
    if back:
        return jnp.where(row < rows - by, pltpu.roll(x, rows - by, axis=0), fill)
    return jnp.where(row >= by, pltpu.roll(x, by, axis=0), fill)


def filter_join(early, late):
    a1, b1, c1, e1, j1 = early
    a, b, c, e, j = late
    damp = 1.0 / (1.0 + c1 * j)
    left = a * damp
    right = a1 * damp
    return (
        left * a1,
        left * (b1 + c1 * e) + b,
        left * a * c1 + c,
        right * (e - j * b1) + e1,
        right * a1 * j + j1,
    )


def smoother_join(late, early):
    g1, m1, v1 = late
    g, m, v = early
    return g * g1, g * m1 + m, g * g * v1 + v


def scan_lanes(values, ident, join, back, share):
    rows = values[0].shape[0]
    by = 1
    while by < rows:
        values = join(tuple(shifted(x, by, i, back) for x, i in zip(values, ident)), values)
        by *= 2
    edge = slice(0, 1) if back else slice(rows - 1, rows)
    ends = tuple(x[edge] for x in values)
    lane = lane_iota()

    def over(x, groups, i):
        step = groups * share
        if back:
            return jnp.where(lane < LANES - step, pltpu.roll(x, LANES - step, axis=1), i)
        return jnp.where(lane >= step, pltpu.roll(x, step, axis=1), i)

    groups = 1
    while groups * share < LANES - share:
        ends = join(tuple(over(x, groups, i) for x, i in zip(ends, ident)), ends)
        groups *= 2
    return join(tuple(over(x, 1, i) for x, i in zip(ends, ident)), values)


def kernel_smooth(
    tiles, blocks, frames, total_subaps, in_ref, noise_ref, gain_ref, mean_ref, var_ref, mean_scr, var_scr
):
    share = mean_ref.shape[1]
    tile = lax.axis_index("tile")
    time = lax.axis_index("tm")
    pack = LANES // share
    rows = frames // pack
    per_group = blocks // pack
    lane = lane_iota()

    def own_modes(v):
        out = v[:, 0:share]
        for t in range(1, tiles):
            out = jnp.where(tile == t, v[:, t * share : (t + 1) * share], out)
        return jnp.concatenate([out] * pack, axis=1)

    q = own_modes(noise_ref[...])
    gain = own_modes(gain_ref[...])
    own = lane_iota(frames) == lax.broadcasted_iota(jnp.int32, (frames, LANES), 0)
    infos = [None] * per_group
    counts = [None] * per_group
    for b in range(blocks):
        v = in_ref[b]
        for t in range(1, tiles):
            v = v + in_ref[t * blocks + b]
        group, place = divmod(b, per_group)
        parts = []
        for g in range(pack):
            turn = (group - g) % pack * share
            parts.append(pltpu.roll(v, turn, axis=1)[0:rows] if turn else v[0:rows])
        info = jnp.concatenate(parts, axis=0)
        count = jnp.sum(jnp.where(own, v[rows : rows + 1], 0.0), axis=1, keepdims=True)
        if group == 0:
            infos[place] = info
            counts[place] = jnp.broadcast_to(count, (frames, LANES))
        else:
            infos[place] = jnp.where(lane >= group * share, info, infos[place])
            counts[place] = jnp.where(lane >= group * share, count, counts[place])
    info_mean = jnp.concatenate(infos, axis=0)
    prec = gain * jnp.concatenate(counts, axis=0) / total_subaps
    length = per_group * frames
    row = lax.broadcasted_iota(jnp.int32, (length, LANES), 0)
    wide_lane = lane_iota(length)
    first = (row == 0) & (wide_lane < share)
    last = (row == length - 1) & (wide_lane >= LANES - share)
    retain = 1.0 / (1.0 + q * prec)
    a = jnp.where(first, 0.0, retain)
    c = jnp.where(first, 1.0 / (1.0 + prec), q * retain)
    _, b, c, _, _ = scan_lanes(
        (a, c * info_mean, c, a * info_mean, a * prec), (1.0, 0.0, 0.0, 0.0, 0.0), filter_join, False, share
    )
    g = jnp.where(last, 0.0, c / (c + q))
    _, m, v = scan_lanes((g, (1.0 - g) * b, c * (1.0 - g)), (1.0, 0.0, 0.0), smoother_join, True, share)
    mean_scr[...] = m
    var_scr[...] = v
    start = pl.multiple_of(time % per_group * frames, 8)
    for scr, out_ref in ((mean_scr, mean_ref), (var_scr, var_ref)):
        piece = scr[pl.ds(start, frames), :]
        out = piece[:, 0:share]
        for g in range(1, pack):
            out = jnp.where(time // per_group == g, piece[:, g * share : (g + 1) * share], out)
        out_ref[...] = out


def body(pixels, offsets, mask, frame_count, slope_to_modes, process_noise, mode_gain):
    sensors, frames, lines, width = pixels.shape
    sub_rows, sub_cols = mask.shape[2], mask.shape[3]
    modes = process_noise.shape[0]
    tiles = lax.axis_size("tile")
    blocks = lax.axis_size("tm")
    share = modes // tiles
    total_subaps = sensors * sub_rows * tiles * sub_cols
    f32 = jnp.float32
    bf16 = jnp.bfloat16
    x = jnp.transpose(pixels, (0, 2, 1, 3)).reshape(sensors, lines * frames, width)
    off = jnp.transpose(offsets, (0, 1, 3, 2))
    msk = jnp.transpose(mask, (0, 2, 1, 3))
    pixels_v = pltpu.with_memory_space_constraint(x, pltpu.VMEM)
    x, off, msk, slope_to_modes = (
        pltpu.with_memory_space_constraint(v, pltpu.HBM) for v in (x, off, msk, slope_to_modes)
    )
    block = SIDE * frames
    narrow = (2, TILE, LANES)
    wide = (TILE + 2 * (width - 3 * TILE), 2 * LANES)
    table_rows = -(-2 * sensors * (sub_rows + 2) // 8) * 8
    params = pltpu.CompilerParams(vmem_limit_bytes=VMEM_LIMIT)

    def cost(chunks):
        return pl.CostEstimate(
            flops=2 * chunks * block * width * 256, bytes_accessed=chunks * block * width * 2, transcendentals=0
        )

    up, down, geo, edge_narrow, edge_wide, mask_v, modes_v = pl.pallas_call(
        functools.partial(kernel_halo, sub_rows, sub_cols, frames),
        out_shape=(
            jax.ShapeDtypeStruct((3, frames, LANES), f32),
            jax.ShapeDtypeStruct((3, frames, LANES), f32),
            pltpu.VMEM((sensors, sub_rows, 8, LANES), f32),
            pltpu.VMEM((sensors, 2, *narrow), bf16),
            pltpu.VMEM((sensors, 2, *wide), bf16),
            pltpu.VMEM(msk.shape, msk.dtype),
            pltpu.VMEM(slope_to_modes.shape, bf16),
        ),
        in_specs=[HBM] * 4,
        out_specs=(VMEM,) * 7,
        scratch_shapes=[
            pltpu.VMEM((sensors, 2, SHIFT * frames, width), bf16),
            pltpu.VMEM((sensors, 2, 2, 2, frames, LANES), f32),
            pltpu.VMEM(off.shape, off.dtype),
            pltpu.VMEM((table_rows, sub_cols), f32),
            pltpu.VMEM((2, table_rows, LANES), f32),
            pltpu.SemaphoreType.DMA((sensors, 2)),
            pltpu.SemaphoreType.DMA((3,)),
        ],
        compiler_params=params,
        cost_estimate=cost(2),
        name="halo_moments",
    )(x, off, msk, slope_to_modes)
    onward = [(i, i + 1) for i in range(tiles - 1)]
    backward = [(j, i) for i, j in onward]
    from_before = lax.ppermute(up, "tile", onward)
    from_after = lax.ppermute(down, "tile", backward)
    partial_modes, edge, edge_mask, count = pl.pallas_call(
        functools.partial(kernel_moments, sub_rows, sub_cols, frames),
        out_shape=(
            pltpu.VMEM((frames, modes), f32),
            pltpu.VMEM((2, 2, 2, frames, LANES), f32),
            pltpu.VMEM((2, 2, frames, LANES), f32),
            pltpu.VMEM((frames, LANES), f32),
        ),
        in_specs=[VMEM] * 6,
        out_specs=(VMEM,) * 4,
        scratch_shapes=[
            pltpu.VMEM((sub_rows - 2, *narrow), bf16),
            pltpu.VMEM((sub_rows - 2, *wide), bf16),
            pltpu.VMEM((sensors, sub_rows, 2, 2, frames, LANES), f32),
        ],
        compiler_params=params,
        cost_estimate=cost(sensors * sub_rows),
        name="moments",
    )(pixels_v, geo, edge_narrow, edge_wide, mask_v, modes_v)
    gain = mode_gain.reshape(1, modes)
    packed = -(-(frames * share // LANES + 1) // 8) * 8
    payload = pl.pallas_call(
        functools.partial(kernel_join, sub_rows, sub_cols, frames, tiles, blocks),
        out_shape=jax.ShapeDtypeStruct((tiles * blocks, packed, LANES), f32),
        in_specs=[pl.BlockSpec(memory_space=pltpu.SMEM)] + [VMEM] * 8,
        out_specs=VMEM,
        compiler_params=params,
        name="join_halo",
    )(frame_count, from_before, from_after, partial_modes, edge, edge_mask, count, modes_v, gain)
    info = lax.all_to_all(payload, ("tile", "tm"), 0, 0)
    return pl.pallas_call(
        functools.partial(kernel_smooth, tiles, blocks, frames, float(total_subaps)),
        out_shape=(
            jax.ShapeDtypeStruct((frames, share), f32),
            jax.ShapeDtypeStruct((frames, share), f32),
        ),
        in_specs=[VMEM] * 3,
        out_specs=(VMEM, VMEM),
        scratch_shapes=[
            pltpu.VMEM((blocks * frames * share // LANES, LANES), f32),
            pltpu.VMEM((blocks * frames * share // LANES, LANES), f32),
        ],
        compiler_params=params,
        name="smooth",
    )(info, process_noise.reshape(1, modes), gain)


def solution(mesh):
    return jax.shard_map(
        body,
        mesh=mesh,
        in_specs=(
            P("grp", "tm", "tile", None),
            P("grp", None, None, None),
            P("grp", "tm", "tile", None),
            P(("grp", "tm")),
            P(None, None, "tile", None, None),
            P(),
            P(),
        ),
        out_specs=(P(("grp", "tm"), "tile"), P(("grp", "tm"), "tile")),
        check_vma=False,
    )
```

```python
import functools

import jax
import jax.numpy as jnp
from jax import lax
from jax.experimental import pallas as pl
from jax.experimental.pallas import tpu as pltpu
from jax.sharding import PartitionSpec as P

SIDE = 20
SHIFT = 6
CENTRE = (SIDE - 1) / 2.0
LANES = 128
HALF = LANES // 2
TILE = 2 * LANES
VMEM_LIMIT = 24 * 1024 * 1024
VMEM = pl.BlockSpec(memory_space=pltpu.VMEM)
HBM = pl.BlockSpec(memory_space=pl.ANY)


def slot_of(strip, sensor):
    return (strip + 1 + sensor) % 3


def half_columns(half, sub_cols, width):
    cols = sub_cols // 2
    first = max(0, half * cols * SIDE - SHIFT) // LANES * LANES
    end = min(width, -(-((half + 1) * cols * SIDE + SHIFT) // 16) * 16)
    return first, end - first


def lane_iota(rows=1):
    return lax.broadcasted_iota(jnp.int32, (rows, LANES), 1)


def half_lane(rows=1):
    lane = lane_iota(rows)
    return jnp.where(lane >= HALF, lane - HALF, lane)


def by_slot(values, cols):
    lane = half_lane()
    out = jnp.zeros_like(values[0])
    for q, v in enumerate(values):
        if v is not None:
            out = jnp.where((lane >= q * cols) & (lane < (q + 1) * cols), v, out)
    return out


def side_by_side(pieces):
    rows, cols = pieces[0].shape
    group = jnp.concatenate([*pieces, jnp.zeros((rows, HALF - 3 * cols), pieces[0].dtype)], axis=1)
    return jnp.concatenate([group, group], axis=1)


def rotate(x, slots, cols):
    shift = slots * cols
    if shift == 0:
        return x
    near = pltpu.roll(x, shift, axis=1)
    far = pltpu.roll(x, LANES - 3 * cols + shift, axis=1)
    return jnp.where(half_lane() >= shift, near, far)


def geometry(geo_ref, off_ref, table_ref, spread_ref, sensors, sub_rows, sub_cols, width):
    cols = sub_cols // 2
    lane = half_lane()
    index = lane - cols * (lane >= cols).astype(jnp.int32)
    index = index - cols * (lane >= 2 * cols).astype(jnp.int32)
    used = lane < 3 * cols
    tile = lax.axis_index("tile")
    total_rows = off_ref.shape[1]
    for s in range(sensors):
        for k in range(-1, sub_rows + 1):
            row = jnp.clip(tile * sub_rows + k, 0, total_rows - 1)
            n = 2 * (s * (sub_rows + 2) + k + 1)
            table_ref[n : n + 2, :] = off_ref[s, row].astype(jnp.float32)
    table = table_ref[...]
    for h in range(2):
        spread_ref[h] = side_by_side([table[:, h * cols : (h + 1) * cols]] * 3)
    for s in range(sensors):
        for i in range(sub_rows):
            for h in range(2):
                first, _ = half_columns(h, sub_cols, width)
                col_base = (SIDE * (index + h * cols) - first).astype(jnp.float32) + CENTRE
                cs = [None] * 3
                rs = [None] * 3
                for k in (i - 1, i, i + 1):
                    q = slot_of(k, s)
                    n = 2 * (s * (sub_rows + 2) + k + 1)
                    cs[q] = spread_ref[h, n + 1 : n + 2, :]
                    rs[q] = spread_ref[h, n : n + 1, :] + (SIDE * (k - i) + CENTRE)
                geo_ref[s, i, 2 * h : 2 * h + 1, :] = jnp.where(used, by_slot(cs, cols) + col_base, -1000.0)
                geo_ref[s, i, 2 * h + 1 : 2 * h + 2, :] = jnp.where(used, by_slot(rs, cols), -1000.0)


def window_weights(col_pos, first, count):
    base = lax.broadcasted_iota(jnp.int32, (16, LANES), 0).astype(jnp.float32) - col_pos
    left = lane_iota(16) < HALF
    for t in range(count // 16):
        d = base + float(16 * t)
        value = jnp.where(left, 1.0, d)
        yield first + 16 * t, jnp.where(jnp.abs(d) < 10.0, value, 0.0).astype(jnp.bfloat16)


def clear_weights(wide_ref, rest):
    zero = jnp.zeros((16, LANES), jnp.bfloat16)
    for n in range(wide_ref.shape[0]):
        for t in range(0, TILE, 16):
            wide_ref[n, t : t + 16, 0:LANES] = zero
            wide_ref[n, t : t + 16, LANES:] = zero
        for t in range(0, rest, 16):
            wide_ref[n, TILE + t : TILE + t + 16, LANES:] = zero
            wide_ref[n, TILE + rest + t : TILE + rest + t + 16, 0:LANES] = zero


def block_weights(geo_ref, narrow_ref, wide_ref, sub_cols, width):
    rest = width - 3 * TILE
    for h in range(2):
        first, count = half_columns(h, sub_cols, width)
        lanes = slice(h * LANES, (h + 1) * LANES)
        for c, piece in window_weights(geo_ref[2 * h : 2 * h + 1, :], first, count):
            if c < TILE:
                narrow_ref[0, c : c + 16, :] = piece
            elif c < 2 * TILE:
                wide_ref[c - TILE : c - TILE + 16, lanes] = piece
            elif c < 3 * TILE:
                narrow_ref[1, c - 2 * TILE : c - 2 * TILE + 16, :] = piece
            else:
                at = c - 2 * TILE
                wide_ref[at : at + 16, 0:LANES] = piece
                wide_ref[at + rest : at + rest + 16, LANES:] = piece


def block_moments(pixels, geo_ref, narrow_ref, wide_ref, frames, first_row=0):
    f32 = jnp.float32
    rows, width = pixels.shape
    rest = width - 3 * TILE
    a = jnp.dot(pixels[:, 0:TILE], narrow_ref[0], preferred_element_type=f32)
    m = jnp.dot(pixels[:, TILE : 2 * TILE], wide_ref[0:TILE, :], preferred_element_type=f32)
    b = jnp.dot(pixels[:, 2 * TILE : 3 * TILE], narrow_ref[1], preferred_element_type=f32)
    split = rows // 2 if (rows // 2) % 16 == 0 else rows
    tail = pixels[0:split, 3 * TILE :]
    if split < rows:
        tail = jnp.concatenate([tail, pixels[split:, 3 * TILE :]], axis=1)
        r = jnp.dot(tail, wide_ref[TILE:, :], preferred_element_type=f32)
    else:
        r = jnp.dot(tail, wide_ref[TILE : TILE + rest, 0:LANES], preferred_element_type=f32)
    out = [[jnp.zeros((frames, LANES), f32) for _ in range(2)] for _ in range(2)]
    for y in range(rows // frames):
        at = slice(y * frames, (y + 1) * frames)
        if y * frames < split:
            extra = r[at, 0:LANES]
        else:
            extra = r[y * frames - split : (y + 1) * frames - split, LANES:]
        pieces = (a[at] + m[at, 0:LANES], m[at, LANES:] + b[at] + extra)
        for h in range(2):
            d = float(y + first_row) - geo_ref[2 * h + 1 : 2 * h + 2, :]
            inside = jnp.abs(d) < 10.0
            out[h][0] = out[h][0] + jnp.where(inside, 1.0, 0.0) * pieces[h]
            out[h][1] = out[h][1] + jnp.where(inside, d, 0.0) * pieces[h]
    return out


def kernel_halo(
    sub_rows, sub_cols, frames, x_hbm, off_hbm, mask_hbm, modes_hbm,
    up_ref, down_ref, geo_ref, narrow_ref, wide_ref, mask_ref, modes_ref,
    buf, p_ref, off_ref, table_ref, spread_ref, sem, side_sem,
):
    sensors, lines, width = x_hbm.shape
    reach = SHIFT * frames
    last = sub_rows - 1
    cols = sub_cols // 2

    def copy(s, e):
        return pltpu.make_async_copy(
            x_hbm.at[s, pl.ds(e * (lines - reach), reach)], buf.at[s, e], sem.at[s, e]
        )

    off_copy = pltpu.make_async_copy(off_hbm, off_ref, side_sem.at[0])
    mask_copy = pltpu.make_async_copy(mask_hbm, mask_ref, side_sem.at[1])
    modes_copy = pltpu.make_async_copy(modes_hbm, modes_ref, side_sem.at[2])
    off_copy.start()
    for s in range(sensors):
        for e in range(2):
            copy(s, e).start()
    mask_copy.start()
    modes_copy.start()
    for s in range(sensors):
        clear_weights(wide_ref.at[s], width - 3 * TILE)
    off_copy.wait()
    geometry(geo_ref, off_ref, table_ref, spread_ref, sensors, sub_rows, sub_cols, width)
    for s in range(sensors):
        for e in range(2):
            block_weights(geo_ref.at[s, e * last], narrow_ref.at[s, e], wide_ref.at[s, e], sub_cols, width)
    for s in range(sensors):
        for e in range(2):
            copy(s, e).wait()
            first_row = e * (SIDE - SHIFT)
            out = block_moments(
                buf.at[s, e], geo_ref.at[s, e * last], narrow_ref.at[s, e], wide_ref.at[s, e], frames, first_row
            )
            for h in range(2):
                for a in range(2):
                    p_ref[s, e, h, a] = out[h][a]
    left = lane_iota() < HALF
    for ref, e, strip in ((down_ref, 0, -1), (up_ref, 1, sub_rows)):
        pair = []
        for h in range(2):
            both = []
            for a in range(2):
                order = [None] * 3
                for s in range(sensors):
                    order[slot_of(strip, s)] = p_ref[s, e, h, a]
                both.append(by_slot(order, cols))
            ref[h] = both[0]
            pair.append(both[1])
        ref[2] = jnp.where(left, pair[0], pltpu.roll(pair[1], HALF, axis=1))
    mask_copy.wait()
    modes_copy.wait()


def slope_terms(plain, lines, mask):
    left = lane_iota() < HALF
    live = mask > 0.0
    flux = jnp.where(left, plain, pltpu.roll(plain, HALF, axis=1))
    moment = jnp.where(left, lines, plain)
    return jnp.where(live, moment / jnp.where(live, flux, 1.0) * mask, 0.0).astype(jnp.bfloat16)


def stacked(modes_ref, picks, half, cols):
    parts = []
    for x in (1, 0):
        used = 0
        for pick in picks:
            if pick is None:
                parts.append(jnp.zeros((cols, modes_ref.shape[-1]), jnp.float32))
            else:
                s, k = pick
                rows = modes_ref[x, s, k].astype(jnp.float32)
                parts.append(rows[half * cols : (half + 1) * cols])
            used += cols
        parts.append(jnp.zeros((HALF - used, modes_ref.shape[-1]), jnp.float32))
    return jnp.concatenate(parts, axis=0).astype(jnp.bfloat16)


def kernel_moments(
    sub_rows, sub_cols, frames, x_ref, geo_ref, edge_narrow_ref, edge_wide_ref, mask_ref, modes_ref,
    pm_ref, edge_ref, em_ref, count_ref, narrow_ref, wide_ref, p_ref,
):
    sensors = x_ref.shape[0]
    block = SIDE * frames
    last = sub_rows - 1
    cols = sub_cols // 2

    width = x_ref.shape[2]
    clear_weights(wide_ref, width - 3 * TILE)

    def step(s, carry):
        for i in range(1, last):
            block_weights(geo_ref.at[s, i], narrow_ref.at[i - 1], wide_ref.at[i - 1], sub_cols, width)
        for i in range(sub_rows):
            if i in (0, last):
                weights = (edge_narrow_ref.at[s, i // last], edge_wide_ref.at[s, i // last])
            else:
                weights = (narrow_ref.at[i - 1], wide_ref.at[i - 1])
            out = block_moments(
                x_ref.at[s, i * block : (i + 1) * block], geo_ref.at[s, i], *weights, frames
            )
            for h in range(2):
                for a in range(2):
                    p_ref[s, i, h, a] = out[h][a]
        return carry

    lax.fori_loop(0, sensors, step, 0)

    def strip_total(s, k, h, a):
        total = None
        for i in (k - 1, k, k + 1):
            if 0 <= i <= last:
                v = p_ref[s, i, h, a]
                total = v if total is None else total + v
        return total

    def mask_of(s, k, h):
        return mask_ref[s, k].astype(jnp.float32)[:, h * cols : (h + 1) * cols]

    count = jnp.zeros((frames, LANES), jnp.float32)
    for e, k in enumerate((0, last)):
        order = [None] * 3
        for s in range(sensors):
            order[slot_of(k, s)] = s
        for h in range(2):
            m = side_by_side([mask_of(s, k, h) for s in order])
            em_ref[e, h] = m
            count = count + m
            for a in range(2):
                edge_ref[e, h, a] = by_slot([strip_total(s, k, h, a) for s in order], cols)
    modes = jnp.zeros((frames, modes_ref.shape[-1]), jnp.float32)
    for s in range(sensors):
        for g in range(1, last, 3):
            order = [None] * 3
            for k in range(g, min(g + 3, last)):
                order[slot_of(k, s)] = k
            for h in range(2):
                none = jnp.zeros((frames, cols), jnp.float32)
                mask = side_by_side([none if k is None else mask_of(s, k, h) for k in order])
                count = count + mask
                plain, lines = (
                    by_slot([None if k is None else strip_total(s, k, h, a) for k in order], cols)
                    for a in range(2)
                )
                modes = modes + jnp.dot(
                    slope_terms(plain, lines, mask),
                    stacked(modes_ref, [None if k is None else (s, k) for k in order], h, cols),
                    preferred_element_type=jnp.float32,
                )
    pm_ref[...] = modes
    count_ref[...] = jnp.broadcast_to(0.5 * jnp.sum(count, axis=1, keepdims=True), count_ref.shape)


def kernel_join(
    sub_rows, sub_cols, frames, tiles, blocks,
    live_ref, before_ref, after_ref, pm_ref, edge_ref, em_ref, count_ref, modes_ref, gain_ref, out_ref,
):
    sensors = modes_ref.shape[1]
    last = sub_rows - 1
    cols = sub_cols // 2
    modes = pm_ref[...]
    for e, k in enumerate((0, last)):
        halo_ref = (before_ref, after_ref)[e]
        halo_strip = (sub_rows, -1)[e]
        turn = (slot_of(k, 0) - slot_of(halo_strip, 0)) % 3
        order = [None] * 3
        for s in range(sensors):
            order[slot_of(k, s)] = s
        both = halo_ref[2]
        for h in range(2):
            lines = both if h == 0 else pltpu.roll(both, HALF, axis=1)
            plain = edge_ref[e, h, 0] + rotate(halo_ref[h], turn, cols)
            lines = edge_ref[e, h, 1] + rotate(lines, turn, cols)
            modes = modes + jnp.dot(
                slope_terms(plain, lines, em_ref[e, h]),
                stacked(modes_ref, [None if s is None else (s, k) for s in order], h, cols),
                preferred_element_type=jnp.float32,
            )
    frame = lax.broadcasted_iota(jnp.int32, (frames, 1), 0)
    live = (frame < live_ref[0:1, 0:1]).astype(jnp.float32)
    info = gain_ref[...] * modes * live
    own = lane_iota(frames) == lax.broadcasted_iota(jnp.int32, (frames, LANES), 0)
    counts = jnp.sum(jnp.where(own, count_ref[...] * live, 0.0), axis=0, keepdims=True)
    share = modes.shape[1] // tiles
    pack = LANES // share
    rows = frames // pack
    pad = jnp.zeros((out_ref.shape[1] - rows - 1, LANES), jnp.float32)
    for t in range(tiles):
        piece = jnp.concatenate(
            [info[g * rows : (g + 1) * rows, t * share : (t + 1) * share] for g in range(pack)], axis=1
        )
        piece = jnp.concatenate([piece, counts, pad], axis=0)
        for b in range(blocks):
            out_ref[t * blocks + b] = piece


def shifted(x, by, fill, back):
    rows = x.shape[0]
    if by % 8 == 0:
        pad = jnp.full((by, x.shape[1]), fill, x.dtype)
        if back:
            return jnp.concatenate([x[by:], pad], axis=0)
        return jnp.concatenate([pad, x[: rows - by]], axis=0)
    row = lax.broadcasted_iota(jnp.int32, (rows, 1), 0)
    if back:
        return jnp.where(row < rows - by, pltpu.roll(x, rows - by, axis=0), fill)
    return jnp.where(row >= by, pltpu.roll(x, by, axis=0), fill)


def kernel_smooth(
    tiles, blocks, frames, total_subaps, in_ref, noise_ref, gain_ref, mean_ref, var_ref, mean_scr, var_scr
):
    share = mean_ref.shape[1]
    total = blocks * frames
    tile = lax.axis_index("tile")
    time = lax.axis_index("tm")
    pack = LANES // share
    rows = frames // pack

    def own_modes(v):
        out = v[:, 0:share]
        for t in range(1, tiles):
            out = jnp.where(tile == t, v[:, t * share : (t + 1) * share], out)
        return out

    q = own_modes(noise_ref[...])
    gain = own_modes(gain_ref[...])
    own = lane_iota(frames) == lax.broadcasted_iota(jnp.int32, (frames, LANES), 0)
    infos = []
    counts = []
    for b in range(blocks):
        v = in_ref[b]
        for t in range(1, tiles):
            v = v + in_ref[t * blocks + b]
        for g in range(pack):
            infos.append(v[0:rows, g * share : (g + 1) * share])
        counts.append(jnp.sum(jnp.where(own, v[rows : rows + 1], 0.0), axis=1, keepdims=True))
    info_mean = jnp.concatenate(infos, axis=0)
    prec = gain * jnp.concatenate(counts, axis=0) / total_subaps
    row = lax.broadcasted_iota(jnp.int32, (total, 1), 0)
    first = row == 0
    retain = 1.0 / (1.0 + q * prec)
    a = jnp.where(first, 0.0, retain)
    c = jnp.where(first, 1.0 / (1.0 + prec), q * retain)
    b = c * info_mean
    e = a * info_mean
    j = a * prec
    by = 1
    while by < total:
        a1 = shifted(a, by, 1.0, False)
        b1 = shifted(b, by, 0.0, False)
        c1 = shifted(c, by, 0.0, False)
        e1 = shifted(e, by, 0.0, False)
        j1 = shifted(j, by, 0.0, False)
        damp = 1.0 / (1.0 + c1 * j)
        left = a * damp
        right = a1 * damp
        b = left * (b1 + c1 * e) + b
        c = left * a * c1 + c
        e, j = right * (e - j * b1) + e1, right * a1 * j + j1
        a = left * a1
        by *= 2
    g = jnp.where(row == total - 1, 0.0, c / (c + q))
    m = (1.0 - g) * b
    v = c * (1.0 - g)
    by = 1
    while by < total:
        g1 = shifted(g, by, 1.0, True)
        m1 = shifted(m, by, 0.0, True)
        v1 = shifted(v, by, 0.0, True)
        m = g * m1 + m
        v = g * g * v1 + v
        g = g * g1
        by *= 2
    mean_scr[...] = m
    var_scr[...] = v
    start = pl.multiple_of(time * frames, 8)
    mean_ref[...] = mean_scr[pl.ds(start, frames), :]
    var_ref[...] = var_scr[pl.ds(start, frames), :]


def body(pixels, offsets, mask, frame_count, slope_to_modes, process_noise, mode_gain):
    sensors, frames, lines, width = pixels.shape
    sub_rows, sub_cols = mask.shape[2], mask.shape[3]
    modes = process_noise.shape[0]
    tiles = lax.axis_size("tile")
    blocks = lax.axis_size("tm")
    share = modes // tiles
    total_subaps = sensors * sub_rows * tiles * sub_cols
    f32 = jnp.float32
    bf16 = jnp.bfloat16
    x = jnp.transpose(pixels, (0, 2, 1, 3)).reshape(sensors, lines * frames, width)
    off = jnp.transpose(offsets, (0, 1, 3, 2))
    msk = jnp.transpose(mask, (0, 2, 1, 3))
    pixels_v = pltpu.with_memory_space_constraint(x, pltpu.VMEM)
    x, off, msk, slope_to_modes = (
        pltpu.with_memory_space_constraint(v, pltpu.HBM) for v in (x, off, msk, slope_to_modes)
    )
    block = SIDE * frames
    narrow = (2, TILE, LANES)
    wide = (TILE + 2 * (width - 3 * TILE), 2 * LANES)
    table_rows = -(-2 * sensors * (sub_rows + 2) // 8) * 8
    params = pltpu.CompilerParams(vmem_limit_bytes=VMEM_LIMIT)

    def cost(chunks):
        return pl.CostEstimate(
            flops=2 * chunks * block * width * 256, bytes_accessed=chunks * block * width * 2, transcendentals=0
        )

    up, down, geo, edge_narrow, edge_wide, mask_v, modes_v = pl.pallas_call(
        functools.partial(kernel_halo, sub_rows, sub_cols, frames),
        out_shape=(
            jax.ShapeDtypeStruct((3, frames, LANES), f32),
            jax.ShapeDtypeStruct((3, frames, LANES), f32),
            pltpu.VMEM((sensors, sub_rows, 8, LANES), f32),
            pltpu.VMEM((sensors, 2, *narrow), bf16),
            pltpu.VMEM((sensors, 2, *wide), bf16),
            pltpu.VMEM(msk.shape, msk.dtype),
            pltpu.VMEM(slope_to_modes.shape, bf16),
        ),
        in_specs=[HBM] * 4,
        out_specs=(VMEM,) * 7,
        scratch_shapes=[
            pltpu.VMEM((sensors, 2, SHIFT * frames, width), bf16),
            pltpu.VMEM((sensors, 2, 2, 2, frames, LANES), f32),
            pltpu.VMEM(off.shape, off.dtype),
            pltpu.VMEM((table_rows, sub_cols), f32),
            pltpu.VMEM((2, table_rows, LANES), f32),
            pltpu.SemaphoreType.DMA((sensors, 2)),
            pltpu.SemaphoreType.DMA((3,)),
        ],
        compiler_params=params,
        cost_estimate=cost(2),
        name="halo_moments",
    )(x, off, msk, slope_to_modes)
    onward = [(i, i + 1) for i in range(tiles - 1)]
    backward = [(j, i) for i, j in onward]
    from_before = lax.ppermute(up, "tile", onward)
    from_after = lax.ppermute(down, "tile", backward)
    partial_modes, edge, edge_mask, count = pl.pallas_call(
        functools.partial(kernel_moments, sub_rows, sub_cols, frames),
        out_shape=(
            pltpu.VMEM((frames, modes), f32),
            pltpu.VMEM((2, 2, 2, frames, LANES), f32),
            pltpu.VMEM((2, 2, frames, LANES), f32),
            pltpu.VMEM((frames, LANES), f32),
        ),
        in_specs=[VMEM] * 6,
        out_specs=(VMEM,) * 4,
        scratch_shapes=[
            pltpu.VMEM((sub_rows - 2, *narrow), bf16),
            pltpu.VMEM((sub_rows - 2, *wide), bf16),
            pltpu.VMEM((sensors, sub_rows, 2, 2, frames, LANES), f32),
        ],
        compiler_params=params,
        cost_estimate=cost(sensors * sub_rows),
        name="moments",
    )(pixels_v, geo, edge_narrow, edge_wide, mask_v, modes_v)
    gain = mode_gain.reshape(1, modes)
    packed = -(-(frames * share // LANES + 1) // 8) * 8
    payload = pl.pallas_call(
        functools.partial(kernel_join, sub_rows, sub_cols, frames, tiles, blocks),
        out_shape=jax.ShapeDtypeStruct((tiles * blocks, packed, LANES), f32),
        in_specs=[VMEM] * 9,
        out_specs=VMEM,
        compiler_params=pltpu.CompilerParams(
            vmem_limit_bytes=VMEM_LIMIT, allow_input_fusion=[True] + [False] * 8
        ),
        name="join_halo",
    )(jnp.broadcast_to(frame_count[:, None], (8, LANES)), from_before, from_after, partial_modes, edge, edge_mask, count, modes_v, gain)
    info = lax.all_to_all(payload, ("tile", "tm"), 0, 0)
    return pl.pallas_call(
        functools.partial(kernel_smooth, tiles, blocks, frames, float(total_subaps)),
        out_shape=(
            jax.ShapeDtypeStruct((frames, share), f32),
            jax.ShapeDtypeStruct((frames, share), f32),
        ),
        in_specs=[VMEM] * 3,
        out_specs=(VMEM, VMEM),
        scratch_shapes=[
            pltpu.VMEM((blocks * frames, share), f32),
            pltpu.VMEM((blocks * frames, share), f32),
        ],
        compiler_params=params,
        name="smooth",
    )(info, process_noise.reshape(1, modes), gain)


def solution(mesh):
    return jax.shard_map(
        body,
        mesh=mesh,
        in_specs=(
            P("grp", "tm", "tile", None),
            P("grp", None, None, None),
            P("grp", "tm", "tile", None),
            P(("grp", "tm")),
            P(None, None, "tile", None, None),
            P(),
            P(),
        ),
        out_specs=(P(("grp", "tm"), "tile"), P(("grp", "tm"), "tile")),
        check_vma=False,
    )
```

```python
import functools

import jax
import jax.numpy as jnp
from jax import lax
from jax.experimental import pallas as pl
from jax.experimental.pallas import tpu as pltpu
from jax.sharding import PartitionSpec as P

SIDE = 20
SHIFT = 6
CENTRE = (SIDE - 1) / 2.0
LANES = 128
HALF = LANES // 2
TILE = 2 * LANES
VMEM_LIMIT = 24 * 1024 * 1024
VMEM = pl.BlockSpec(memory_space=pltpu.VMEM)
HBM = pl.BlockSpec(memory_space=pl.ANY)


def slot_of(strip, sensor):
    return (strip + 1 + sensor) % 3


def half_columns(half, sub_cols, width):
    cols = sub_cols // 2
    first = max(0, half * cols * SIDE - SHIFT) // LANES * LANES
    end = min(width, -(-((half + 1) * cols * SIDE + SHIFT) // 16) * 16)
    return first, end - first


def lane_iota(rows=1):
    return lax.broadcasted_iota(jnp.int32, (rows, LANES), 1)


def half_lane(rows=1):
    lane = lane_iota(rows)
    return jnp.where(lane >= HALF, lane - HALF, lane)


def by_slot(values, cols):
    lane = half_lane()
    out = jnp.zeros_like(values[0])
    for q, v in enumerate(values):
        if v is not None:
            out = jnp.where((lane >= q * cols) & (lane < (q + 1) * cols), v, out)
    return out


def side_by_side(pieces):
    rows, cols = pieces[0].shape
    group = jnp.concatenate([*pieces, jnp.zeros((rows, HALF - 3 * cols), pieces[0].dtype)], axis=1)
    return jnp.concatenate([group, group], axis=1)


def rotate(x, slots, cols):
    shift = slots * cols
    if shift == 0:
        return x
    near = pltpu.roll(x, shift, axis=1)
    far = pltpu.roll(x, LANES - 3 * cols + shift, axis=1)
    return jnp.where(half_lane() >= shift, near, far)


def geometry(geo_ref, off_ref, table_ref, spread_ref, sensors, sub_rows, sub_cols, width):
    cols = sub_cols // 2
    lane = half_lane()
    index = lane - cols * (lane >= cols).astype(jnp.int32)
    index = index - cols * (lane >= 2 * cols).astype(jnp.int32)
    used = lane < 3 * cols
    tile = lax.axis_index("tile")
    total_rows = off_ref.shape[1]
    for s in range(sensors):
        for k in range(-1, sub_rows + 1):
            row = jnp.clip(tile * sub_rows + k, 0, total_rows - 1)
            n = 2 * (s * (sub_rows + 2) + k + 1)
            table_ref[n : n + 2, :] = off_ref[s, row].astype(jnp.float32)
    table = table_ref[...]
    for h in range(2):
        spread_ref[h] = side_by_side([table[:, h * cols : (h + 1) * cols]] * 3)
    for s in range(sensors):
        for i in range(sub_rows):
            for h in range(2):
                first, _ = half_columns(h, sub_cols, width)
                col_base = (SIDE * (index + h * cols) - first).astype(jnp.float32) + CENTRE
                cs = [None] * 3
                rs = [None] * 3
                for k in (i - 1, i, i + 1):
                    q = slot_of(k, s)
                    n = 2 * (s * (sub_rows + 2) + k + 1)
                    cs[q] = spread_ref[h, n + 1 : n + 2, :]
                    rs[q] = spread_ref[h, n : n + 1, :] + (SIDE * (k - i) + CENTRE)
                geo_ref[s, i, 2 * h : 2 * h + 1, :] = jnp.where(used, by_slot(cs, cols) + col_base, -1000.0)
                geo_ref[s, i, 2 * h + 1 : 2 * h + 2, :] = jnp.where(used, by_slot(rs, cols), -1000.0)


def window_weights(col_pos, first, count):
    base = lax.broadcasted_iota(jnp.int32, (16, LANES), 0).astype(jnp.float32) - col_pos
    left = lane_iota(16) < HALF
    for t in range(count // 16):
        d = base + float(16 * t)
        value = jnp.where(left, 1.0, d)
        yield first + 16 * t, jnp.where(jnp.abs(d) < 10.0, value, 0.0).astype(jnp.bfloat16)


def clear_weights(wide_ref, sub_cols, width):
    zero = jnp.zeros((16, LANES), jnp.bfloat16)
    rest = width - 3 * TILE
    end = sum(half_columns(0, sub_cols, width)) - TILE
    begin = half_columns(1, sub_cols, width)[0] - TILE
    for n in range(wide_ref.shape[0]):
        for t in range(end, TILE, 16):
            wide_ref[n, t : t + 16, 0:LANES] = zero
        for t in range(0, begin, 16):
            wide_ref[n, t : t + 16, LANES:] = zero
        for t in range(0, rest, 16):
            wide_ref[n, TILE + t : TILE + t + 16, LANES:] = zero
            wide_ref[n, TILE + rest + t : TILE + rest + t + 16, 0:LANES] = zero


def block_weights(geo_ref, narrow_ref, wide_ref, sub_cols, width):
    rest = width - 3 * TILE
    for h in range(2):
        first, count = half_columns(h, sub_cols, width)
        lanes = slice(h * LANES, (h + 1) * LANES)
        for c, piece in window_weights(geo_ref[2 * h : 2 * h + 1, :], first, count):
            if c < TILE:
                narrow_ref[0, c : c + 16, :] = piece
            elif c < 2 * TILE:
                wide_ref[c - TILE : c - TILE + 16, lanes] = piece
            elif c < 3 * TILE:
                narrow_ref[1, c - 2 * TILE : c - 2 * TILE + 16, :] = piece
            else:
                at = c - 2 * TILE
                wide_ref[at : at + 16, 0:LANES] = piece
                wide_ref[at + rest : at + rest + 16, LANES:] = piece


def block_moments(pixels, geo_ref, narrow_ref, wide_ref, frames, first_row=0):
    f32 = jnp.float32
    rows, width = pixels.shape
    rest = width - 3 * TILE
    a = jnp.dot(pixels[:, 0:TILE], narrow_ref[0], preferred_element_type=f32)
    m = jnp.dot(pixels[:, TILE : 2 * TILE], wide_ref[0:TILE, :], preferred_element_type=f32)
    b = jnp.dot(pixels[:, 2 * TILE : 3 * TILE], narrow_ref[1], preferred_element_type=f32)
    split = rows // 2 if (rows // 2) % 16 == 0 else rows
    tail = pixels[0:split, 3 * TILE :]
    if split < rows:
        tail = jnp.concatenate([tail, pixels[split:, 3 * TILE :]], axis=1)
        r = jnp.dot(tail, wide_ref[TILE:, :], preferred_element_type=f32)
    else:
        r = jnp.dot(tail, wide_ref[TILE : TILE + rest, 0:LANES], preferred_element_type=f32)
    out = [[jnp.zeros((frames, LANES), f32) for _ in range(2)] for _ in range(2)]
    for y in range(rows // frames):
        at = slice(y * frames, (y + 1) * frames)
        if y * frames < split:
            extra = r[at, 0:LANES]
        else:
            extra = r[y * frames - split : (y + 1) * frames - split, LANES:]
        pieces = (a[at] + m[at, 0:LANES], m[at, LANES:] + b[at] + extra)
        for h in range(2):
            d = float(y + first_row) - geo_ref[2 * h + 1 : 2 * h + 2, :]
            inside = jnp.abs(d) < 10.0
            out[h][0] = out[h][0] + jnp.where(inside, 1.0, 0.0) * pieces[h]
            out[h][1] = out[h][1] + jnp.where(inside, d, 0.0) * pieces[h]
    return out


def kernel_halo(
    sub_rows, sub_cols, frames, x_hbm, off_hbm, mask_hbm, modes_hbm,
    up_ref, down_ref, geo_ref, narrow_ref, wide_ref, mask_ref, modes_ref,
    buf, p_ref, off_ref, table_ref, spread_ref, sem, side_sem,
):
    sensors, lines, width = x_hbm.shape
    reach = SHIFT * frames
    last = sub_rows - 1
    cols = sub_cols // 2

    def copy(s, e):
        return pltpu.make_async_copy(
            x_hbm.at[s, pl.ds(e * (lines - reach), reach)], buf.at[s, e], sem.at[s, e]
        )

    off_copy = pltpu.make_async_copy(off_hbm, off_ref, side_sem.at[0])
    mask_copy = pltpu.make_async_copy(mask_hbm, mask_ref, side_sem.at[1])
    modes_copy = pltpu.make_async_copy(modes_hbm, modes_ref, side_sem.at[2])
    off_copy.start()
    for s in range(sensors):
        for e in range(2):
            copy(s, e).start()
    mask_copy.start()
    modes_copy.start()
    for s in range(sensors):
        clear_weights(wide_ref.at[s], sub_cols, width)
    off_copy.wait()
    geometry(geo_ref, off_ref, table_ref, spread_ref, sensors, sub_rows, sub_cols, width)
    for s in range(sensors):
        for e in range(2):
            block_weights(geo_ref.at[s, e * last], narrow_ref.at[s, e], wide_ref.at[s, e], sub_cols, width)
    for s in range(sensors):
        for e in range(2):
            copy(s, e).wait()
    for s in range(sensors):
        for e in range(2):
            first_row = e * (SIDE - SHIFT)
            out = block_moments(
                buf.at[s, e], geo_ref.at[s, e * last], narrow_ref.at[s, e], wide_ref.at[s, e], frames, first_row
            )
            for h in range(2):
                for a in range(2):
                    p_ref[s, e, h, a] = out[h][a]
    left = lane_iota() < HALF
    for ref, e, strip in ((down_ref, 0, -1), (up_ref, 1, sub_rows)):
        pair = []
        for h in range(2):
            both = []
            for a in range(2):
                order = [None] * 3
                for s in range(sensors):
                    order[slot_of(strip, s)] = p_ref[s, e, h, a]
                both.append(by_slot(order, cols))
            ref[h] = both[0]
            pair.append(both[1])
        ref[2] = jnp.where(left, pair[0], pltpu.roll(pair[1], HALF, axis=1))
    mask_copy.wait()
    modes_copy.wait()


def slope_terms(plain, lines, mask):
    left = lane_iota() < HALF
    live = mask > 0.0
    flux = jnp.where(left, plain, pltpu.roll(plain, HALF, axis=1))
    moment = jnp.where(left, lines, plain)
    return jnp.where(live, moment / jnp.where(live, flux, 1.0) * mask, 0.0).astype(jnp.bfloat16)


def stacked(modes_ref, picks, half, cols):
    parts = []
    for x in (1, 0):
        used = 0
        for pick in picks:
            if pick is None:
                parts.append(jnp.zeros((cols, modes_ref.shape[-1]), jnp.float32))
            else:
                s, k = pick
                rows = modes_ref[x, s, k].astype(jnp.float32)
                parts.append(rows[half * cols : (half + 1) * cols])
            used += cols
        parts.append(jnp.zeros((HALF - used, modes_ref.shape[-1]), jnp.float32))
    return jnp.concatenate(parts, axis=0).astype(jnp.bfloat16)


def kernel_moments(
    sub_rows, sub_cols, frames, x_ref, geo_ref, edge_narrow_ref, edge_wide_ref, mask_ref, modes_ref,
    pm_ref, edge_ref, em_ref, count_ref, narrow_ref, wide_ref, p_ref,
):
    sensors = x_ref.shape[0]
    block = SIDE * frames
    last = sub_rows - 1
    cols = sub_cols // 2

    width = x_ref.shape[2]
    for s in range(sensors):
        clear_weights(wide_ref.at[s], sub_cols, width)
        for i in range(1, last):
            block_weights(geo_ref.at[s, i], narrow_ref.at[s, i - 1], wide_ref.at[s, i - 1], sub_cols, width)
    for s in range(sensors):
        for i in range(sub_rows):
            if i in (0, last):
                weights = (edge_narrow_ref.at[s, i // last], edge_wide_ref.at[s, i // last])
            else:
                weights = (narrow_ref.at[s, i - 1], wide_ref.at[s, i - 1])
            out = block_moments(
                x_ref.at[s, i * block : (i + 1) * block], geo_ref.at[s, i], *weights, frames
            )
            for h in range(2):
                for a in range(2):
                    p_ref[s, i, h, a] = out[h][a]

    def strip_total(s, k, h, a):
        total = None
        for i in (k - 1, k, k + 1):
            if 0 <= i <= last:
                v = p_ref[s, i, h, a]
                total = v if total is None else total + v
        return total

    def mask_of(s, k, h):
        return mask_ref[s, k].astype(jnp.float32)[:, h * cols : (h + 1) * cols]

    count = jnp.zeros((frames, LANES), jnp.float32)
    for e, k in enumerate((0, last)):
        order = [None] * 3
        for s in range(sensors):
            order[slot_of(k, s)] = s
        for h in range(2):
            m = side_by_side([mask_of(s, k, h) for s in order])
            em_ref[e, h] = m
            count = count + m
            for a in range(2):
                edge_ref[e, h, a] = by_slot([strip_total(s, k, h, a) for s in order], cols)
    modes = jnp.zeros((frames, modes_ref.shape[-1]), jnp.float32)
    for s in range(sensors):
        for g in range(1, last, 3):
            order = [None] * 3
            for k in range(g, min(g + 3, last)):
                order[slot_of(k, s)] = k
            for h in range(2):
                none = jnp.zeros((frames, cols), jnp.float32)
                mask = side_by_side([none if k is None else mask_of(s, k, h) for k in order])
                count = count + mask
                plain, lines = (
                    by_slot([None if k is None else strip_total(s, k, h, a) for k in order], cols)
                    for a in range(2)
                )
                modes = modes + jnp.dot(
                    slope_terms(plain, lines, mask),
                    stacked(modes_ref, [None if k is None else (s, k) for k in order], h, cols),
                    preferred_element_type=jnp.float32,
                )
    pm_ref[...] = modes
    count_ref[...] = jnp.broadcast_to(0.5 * jnp.sum(count, axis=1, keepdims=True), count_ref.shape)


def kernel_join(
    sub_rows, sub_cols, frames, tiles, blocks,
    live_ref, before_ref, after_ref, pm_ref, edge_ref, em_ref, count_ref, modes_ref, gain_ref, out_ref,
):
    sensors = modes_ref.shape[1]
    last = sub_rows - 1
    cols = sub_cols // 2
    modes = pm_ref[...]
    for e, k in enumerate((0, last)):
        halo_ref = (before_ref, after_ref)[e]
        halo_strip = (sub_rows, -1)[e]
        turn = (slot_of(k, 0) - slot_of(halo_strip, 0)) % 3
        order = [None] * 3
        for s in range(sensors):
            order[slot_of(k, s)] = s
        both = halo_ref[2]
        for h in range(2):
            lines = both if h == 0 else pltpu.roll(both, HALF, axis=1)
            plain = edge_ref[e, h, 0] + rotate(halo_ref[h], turn, cols)
            lines = edge_ref[e, h, 1] + rotate(lines, turn, cols)
            modes = modes + jnp.dot(
                slope_terms(plain, lines, em_ref[e, h]),
                stacked(modes_ref, [None if s is None else (s, k) for s in order], h, cols),
                preferred_element_type=jnp.float32,
            )
    frame = lax.broadcasted_iota(jnp.int32, (frames, 1), 0)
    live = (frame < live_ref[0]).astype(jnp.float32)
    info = gain_ref[...] * modes * live
    own = lane_iota(frames) == lax.broadcasted_iota(jnp.int32, (frames, LANES), 0)
    counts = jnp.sum(jnp.where(own, count_ref[...] * live, 0.0), axis=0, keepdims=True)
    share = modes.shape[1] // tiles
    pack = LANES // share
    rows = frames // pack
    pad = jnp.zeros((out_ref.shape[1] - rows - 1, LANES), jnp.float32)
    for t in range(tiles):
        piece = jnp.concatenate(
            [info[g * rows : (g + 1) * rows, t * share : (t + 1) * share] for g in range(pack)], axis=1
        )
        piece = jnp.concatenate([piece, counts, pad], axis=0)
        for b in range(blocks):
            out_ref[t * blocks + b] = piece


def shifted(x, by, fill, back):
    rows = x.shape[0]
    if by % 8 == 0:
        pad = jnp.full((by, x.shape[1]), fill, x.dtype)
        if back:
            return jnp.concatenate([x[by:], pad], axis=0)
        return jnp.concatenate([pad, x[: rows - by]], axis=0)
    row = lax.broadcasted_iota(jnp.int32, (rows, 1), 0)
    if back:
        return jnp.where(row < rows - by, pltpu.roll(x, rows - by, axis=0), fill)
    return jnp.where(row >= by, pltpu.roll(x, by, axis=0), fill)


def kernel_smooth(
    tiles, blocks, frames, total_subaps, in_ref, noise_ref, gain_ref, mean_ref, var_ref, mean_scr, var_scr
):
    share = mean_ref.shape[1]
    total = blocks * frames
    tile = lax.axis_index("tile")
    time = lax.axis_index("tm")
    pack = LANES // share
    rows = frames // pack

    def own_modes(v):
        out = v[:, 0:share]
        for t in range(1, tiles):
            out = jnp.where(tile == t, v[:, t * share : (t + 1) * share], out)
        return out

    q = own_modes(noise_ref[...])
    gain = own_modes(gain_ref[...])
    own = lane_iota(frames) == lax.broadcasted_iota(jnp.int32, (frames, LANES), 0)
    infos = []
    counts = []
    for b in range(blocks):
        v = in_ref[b]
        for t in range(1, tiles):
            v = v + in_ref[t * blocks + b]
        for g in range(pack):
            infos.append(v[0:rows, g * share : (g + 1) * share])
        counts.append(jnp.sum(jnp.where(own, v[rows : rows + 1], 0.0), axis=1, keepdims=True))
    info_mean = jnp.concatenate(infos, axis=0)
    prec = gain * jnp.concatenate(counts, axis=0) / total_subaps
    row = lax.broadcasted_iota(jnp.int32, (total, 1), 0)
    first = row == 0
    retain = 1.0 / (1.0 + q * prec)
    a = jnp.where(first, 0.0, retain)
    c = jnp.where(first, 1.0 / (1.0 + prec), q * retain)
    b = c * info_mean
    e = a * info_mean
    j = a * prec
    by = 1
    while by < total:
        a1 = shifted(a, by, 1.0, False)
        b1 = shifted(b, by, 0.0, False)
        c1 = shifted(c, by, 0.0, False)
        e1 = shifted(e, by, 0.0, False)
        j1 = shifted(j, by, 0.0, False)
        damp = 1.0 / (1.0 + c1 * j)
        left = a * damp
        right = a1 * damp
        b = left * (b1 + c1 * e) + b
        c = left * a * c1 + c
        e, j = right * (e - j * b1) + e1, right * a1 * j + j1
        a = left * a1
        by *= 2
    g = jnp.where(row == total - 1, 0.0, c / (c + q))
    m = (1.0 - g) * b
    v = c * (1.0 - g)
    by = 1
    while by < total:
        g1 = shifted(g, by, 1.0, True)
        m1 = shifted(m, by, 0.0, True)
        v1 = shifted(v, by, 0.0, True)
        m = g * m1 + m
        v = g * g * v1 + v
        g = g * g1
        by *= 2
    mean_scr[...] = m
    var_scr[...] = v
    start = pl.multiple_of(time * frames, 8)
    mean_ref[...] = mean_scr[pl.ds(start, frames), :]
    var_ref[...] = var_scr[pl.ds(start, frames), :]


def body(pixels, offsets, mask, frame_count, slope_to_modes, process_noise, mode_gain):
    sensors, frames, lines, width = pixels.shape
    sub_rows, sub_cols = mask.shape[2], mask.shape[3]
    modes = process_noise.shape[0]
    tiles = lax.axis_size("tile")
    blocks = lax.axis_size("tm")
    share = modes // tiles
    total_subaps = sensors * sub_rows * tiles * sub_cols
    f32 = jnp.float32
    bf16 = jnp.bfloat16
    x = jnp.transpose(pixels, (0, 2, 1, 3)).reshape(sensors, lines * frames, width)
    off = jnp.transpose(offsets, (0, 1, 3, 2))
    msk = jnp.transpose(mask, (0, 2, 1, 3))
    pixels_v = pltpu.with_memory_space_constraint(x, pltpu.VMEM)
    x, off, msk, slope_to_modes = (
        pltpu.with_memory_space_constraint(v, pltpu.HBM) for v in (x, off, msk, slope_to_modes)
    )
    block = SIDE * frames
    narrow = (2, TILE, LANES)
    wide = (TILE + 2 * (width - 3 * TILE), 2 * LANES)
    table_rows = -(-2 * sensors * (sub_rows + 2) // 8) * 8
    params = pltpu.CompilerParams(vmem_limit_bytes=VMEM_LIMIT)

    def cost(chunks):
        return pl.CostEstimate(
            flops=2 * chunks * block * width * 256, bytes_accessed=chunks * block * width * 2, transcendentals=0
        )

    up, down, geo, edge_narrow, edge_wide, mask_v, modes_v = pl.pallas_call(
        functools.partial(kernel_halo, sub_rows, sub_cols, frames),
        out_shape=(
            jax.ShapeDtypeStruct((3, frames, LANES), f32),
            jax.ShapeDtypeStruct((3, frames, LANES), f32),
            pltpu.VMEM((sensors, sub_rows, 8, LANES), f32),
            pltpu.VMEM((sensors, 2, *narrow), bf16),
            pltpu.VMEM((sensors, 2, *wide), bf16),
            pltpu.VMEM(msk.shape, msk.dtype),
            pltpu.VMEM(slope_to_modes.shape, bf16),
        ),
        in_specs=[HBM] * 4,
        out_specs=(VMEM,) * 7,
        scratch_shapes=[
            pltpu.VMEM((sensors, 2, SHIFT * frames, width), bf16),
            pltpu.VMEM((sensors, 2, 2, 2, frames, LANES), f32),
            pltpu.VMEM(off.shape, off.dtype),
            pltpu.VMEM((table_rows, sub_cols), f32),
            pltpu.VMEM((2, table_rows, LANES), f32),
            pltpu.SemaphoreType.DMA((sensors, 2)),
            pltpu.SemaphoreType.DMA((3,)),
        ],
        compiler_params=params,
        cost_estimate=cost(2),
        name="halo_moments",
    )(x, off, msk, slope_to_modes)
    onward = [(i, i + 1) for i in range(tiles - 1)]
    backward = [(j, i) for i, j in onward]
    from_before = lax.ppermute(up, "tile", onward)
    from_after = lax.ppermute(down, "tile", backward)
    partial_modes, edge, edge_mask, count = pl.pallas_call(
        functools.partial(kernel_moments, sub_rows, sub_cols, frames),
        out_shape=(
            pltpu.VMEM((frames, modes), f32),
            pltpu.VMEM((2, 2, 2, frames, LANES), f32),
            pltpu.VMEM((2, 2, frames, LANES), f32),
            pltpu.VMEM((frames, LANES), f32),
        ),
        in_specs=[VMEM] * 6,
        out_specs=(VMEM,) * 4,
        scratch_shapes=[
            pltpu.VMEM((sensors, sub_rows - 2, *narrow), bf16),
            pltpu.VMEM((sensors, sub_rows - 2, *wide), bf16),
            pltpu.VMEM((sensors, sub_rows, 2, 2, frames, LANES), f32),
        ],
        compiler_params=params,
        cost_estimate=cost(sensors * sub_rows),
        name="moments",
    )(pixels_v, geo, edge_narrow, edge_wide, mask_v, modes_v)
    gain = mode_gain.reshape(1, modes)
    packed = -(-(frames * share // LANES + 1) // 8) * 8
    payload = pl.pallas_call(
        functools.partial(kernel_join, sub_rows, sub_cols, frames, tiles, blocks),
        out_shape=jax.ShapeDtypeStruct((tiles * blocks, packed, LANES), f32),
        in_specs=[pl.BlockSpec(memory_space=pltpu.SMEM)] + [VMEM] * 8,
        out_specs=VMEM,
        compiler_params=params,
        name="join_halo",
    )(frame_count, from_before, from_after, partial_modes, edge, edge_mask, count, modes_v, gain)
    info = lax.all_to_all(payload, ("tile", "tm"), 0, 0)
    return pl.pallas_call(
        functools.partial(kernel_smooth, tiles, blocks, frames, float(total_subaps)),
        out_shape=(
            jax.ShapeDtypeStruct((frames, share), f32),
            jax.ShapeDtypeStruct((frames, share), f32),
        ),
        in_specs=[VMEM] * 3,
        out_specs=(VMEM, VMEM),
        scratch_shapes=[
            pltpu.VMEM((blocks * frames, share), f32),
            pltpu.VMEM((blocks * frames, share), f32),
        ],
        compiler_params=params,
        name="smooth",
    )(info, process_noise.reshape(1, modes), gain)


def solution(mesh):
    return jax.shard_map(
        body,
        mesh=mesh,
        in_specs=(
            P("grp", "tm", "tile", None),
            P("grp", None, None, None),
            P("grp", "tm", "tile", None),
            P(("grp", "tm")),
            P(None, None, "tile", None, None),
            P(),
            P(),
        ),
        out_specs=(P(("grp", "tm"), "tile"), P(("grp", "tm"), "tile")),
        check_vma=False,
    )
```

```python
import functools

import jax
import jax.numpy as jnp
from jax import lax
from jax.experimental import pallas as pl
from jax.experimental.pallas import tpu as pltpu
from jax.sharding import PartitionSpec as P

SIDE = 20
SHIFT = 6
CENTRE = (SIDE - 1) / 2.0
LANES = 128
HALF = LANES // 2
TILE = 2 * LANES
VMEM_LIMIT = 24 * 1024 * 1024
VMEM = pl.BlockSpec(memory_space=pltpu.VMEM)
HBM = pl.BlockSpec(memory_space=pl.ANY)


def slot_of(strip, sensor):
    return (strip + 1 + sensor) % 3


def half_columns(half, sub_cols, width):
    cols = sub_cols // 2
    first = max(0, half * cols * SIDE - SHIFT) // LANES * LANES
    end = min(width, -(-((half + 1) * cols * SIDE + SHIFT) // 16) * 16)
    return first, end - first


def lane_iota(rows=1):
    return lax.broadcasted_iota(jnp.int32, (rows, LANES), 1)


def half_lane(rows=1):
    lane = lane_iota(rows)
    return jnp.where(lane >= HALF, lane - HALF, lane)


def by_slot(values, cols):
    lane = half_lane()
    out = jnp.zeros_like(values[0])
    for q, v in enumerate(values):
        if v is not None:
            out = jnp.where((lane >= q * cols) & (lane < (q + 1) * cols), v, out)
    return out


def side_by_side(pieces):
    rows, cols = pieces[0].shape
    group = jnp.concatenate([*pieces, jnp.zeros((rows, HALF - 3 * cols), pieces[0].dtype)], axis=1)
    return jnp.concatenate([group, group], axis=1)


def rotate(x, slots, cols):
    shift = slots * cols
    if shift == 0:
        return x
    near = pltpu.roll(x, shift, axis=1)
    far = pltpu.roll(x, LANES - 3 * cols + shift, axis=1)
    return jnp.where(half_lane() >= shift, near, far)


def geometry(geo_ref, off_ref, table_ref, spread_ref, sensors, sub_rows, sub_cols, width):
    cols = sub_cols // 2
    lane = half_lane()
    index = lane - cols * (lane >= cols).astype(jnp.int32)
    index = index - cols * (lane >= 2 * cols).astype(jnp.int32)
    used = lane < 3 * cols
    tile = lax.axis_index("tile")
    total_rows = off_ref.shape[1]
    for s in range(sensors):
        for k in range(-1, sub_rows + 1):
            row = jnp.clip(tile * sub_rows + k, 0, total_rows - 1)
            n = 2 * (s * (sub_rows + 2) + k + 1)
            table_ref[n : n + 2, :] = off_ref[s, row].astype(jnp.float32)
    table = table_ref[...]
    for h in range(2):
        spread_ref[h] = side_by_side([table[:, h * cols : (h + 1) * cols]] * 3)
    for s in range(sensors):
        for i in range(sub_rows):
            for h in range(2):
                first, _ = half_columns(h, sub_cols, width)
                col_base = (SIDE * (index + h * cols) - first).astype(jnp.float32) + CENTRE
                cs = [None] * 3
                rs = [None] * 3
                for k in (i - 1, i, i + 1):
                    q = slot_of(k, s)
                    n = 2 * (s * (sub_rows + 2) + k + 1)
                    cs[q] = spread_ref[h, n + 1 : n + 2, :]
                    rs[q] = spread_ref[h, n : n + 1, :] + (SIDE * (k - i) + CENTRE)
                geo_ref[s, i, 2 * h : 2 * h + 1, :] = jnp.where(used, by_slot(cs, cols) + col_base, -1000.0)
                geo_ref[s, i, 2 * h + 1 : 2 * h + 2, :] = jnp.where(used, by_slot(rs, cols), -1000.0)


def window_weights(col_pos, first, count):
    base = lax.broadcasted_iota(jnp.int32, (16, LANES), 0).astype(jnp.float32) - col_pos
    left = lane_iota(16) < HALF
    for t in range(count // 16):
        d = base + float(16 * t)
        value = jnp.where(left, 1.0, d)
        yield first + 16 * t, jnp.where(jnp.abs(d) < 10.0, value, 0.0).astype(jnp.bfloat16)


def clear_weights(wide_ref, sub_cols, width):
    zero = jnp.zeros((16, LANES), jnp.bfloat16)
    rest = width - 3 * TILE
    end = sum(half_columns(0, sub_cols, width)) - TILE
    begin = half_columns(1, sub_cols, width)[0] - TILE
    for n in range(wide_ref.shape[0]):
        for t in range(end, TILE, 16):
            wide_ref[n, t : t + 16, 0:LANES] = zero
        for t in range(0, begin, 16):
            wide_ref[n, t : t + 16, LANES:] = zero
        for t in range(0, rest, 16):
            wide_ref[n, TILE + t : TILE + t + 16, LANES:] = zero
            wide_ref[n, TILE + rest + t : TILE + rest + t + 16, 0:LANES] = zero


def block_weights(geo_ref, narrow_ref, wide_ref, sub_cols, width):
    rest = width - 3 * TILE
    for h in range(2):
        first, count = half_columns(h, sub_cols, width)
        lanes = slice(h * LANES, (h + 1) * LANES)
        for c, piece in window_weights(geo_ref[2 * h : 2 * h + 1, :], first, count):
            if c < TILE:
                narrow_ref[0, c : c + 16, :] = piece
            elif c < 2 * TILE:
                wide_ref[c - TILE : c - TILE + 16, lanes] = piece
            elif c < 3 * TILE:
                narrow_ref[1, c - 2 * TILE : c - 2 * TILE + 16, :] = piece
            else:
                at = c - 2 * TILE
                wide_ref[at : at + 16, 0:LANES] = piece
                wide_ref[at + rest : at + rest + 16, LANES:] = piece


def row_weights(geo_ref, line_ref):
    count = line_ref.shape[2]
    row = lax.broadcasted_iota(jnp.int32, (count, LANES), 0).astype(jnp.float32)
    for h in range(2):
        d = row - geo_ref[2 * h + 1 : 2 * h + 2, :]
        inside = jnp.abs(d) < 10.0
        line_ref[h, 0] = jnp.where(inside, 1.0, 0.0)
        line_ref[h, 1] = jnp.where(inside, d, 0.0)


def block_moments(pixels, line_ref, narrow_ref, wide_ref, frames, first_row=0):
    f32 = jnp.float32
    rows, width = pixels.shape
    rest = width - 3 * TILE
    a = jnp.dot(pixels[:, 0:TILE], narrow_ref[0], preferred_element_type=f32)
    m = jnp.dot(pixels[:, TILE : 2 * TILE], wide_ref[0:TILE, :], preferred_element_type=f32)
    b = jnp.dot(pixels[:, 2 * TILE : 3 * TILE], narrow_ref[1], preferred_element_type=f32)
    split = rows // 2 if (rows // 2) % 16 == 0 else rows
    tail = pixels[0:split, 3 * TILE :]
    if split < rows:
        tail = jnp.concatenate([tail, pixels[split:, 3 * TILE :]], axis=1)
        r = jnp.dot(tail, wide_ref[TILE:, :], preferred_element_type=f32)
    else:
        r = jnp.dot(tail, wide_ref[TILE : TILE + rest, 0:LANES], preferred_element_type=f32)
    out = [[jnp.zeros((frames, LANES), f32) for _ in range(2)] for _ in range(2)]
    for y in range(rows // frames):
        at = slice(y * frames, (y + 1) * frames)
        if y * frames < split:
            extra = r[at, 0:LANES]
        else:
            extra = r[y * frames - split : (y + 1) * frames - split, LANES:]
        pieces = (a[at] + m[at, 0:LANES], m[at, LANES:] + b[at] + extra)
        for h in range(2):
            at_row = slice(first_row + y, first_row + y + 1)
            out[h][0] = out[h][0] + line_ref[h, 0, at_row, :] * pieces[h]
            out[h][1] = out[h][1] + line_ref[h, 1, at_row, :] * pieces[h]
    return out


def kernel_halo(
    sub_rows, sub_cols, frames, x_hbm, off_hbm, mask_hbm, modes_hbm,
    up_ref, down_ref, geo_ref, narrow_ref, wide_ref, mask_ref, modes_ref,
    buf, p_ref, line_ref, off_ref, table_ref, spread_ref, sem, side_sem,
):
    sensors, lines, width = x_hbm.shape
    reach = SHIFT * frames
    last = sub_rows - 1
    cols = sub_cols // 2

    def copy(s, e):
        return pltpu.make_async_copy(
            x_hbm.at[s, pl.ds(e * (lines - reach), reach)], buf.at[s, e], sem.at[s, e]
        )

    off_copy = pltpu.make_async_copy(off_hbm, off_ref, side_sem.at[0])
    mask_copy = pltpu.make_async_copy(mask_hbm, mask_ref, side_sem.at[1])
    modes_copy = pltpu.make_async_copy(modes_hbm, modes_ref, side_sem.at[2])
    off_copy.start()
    for s in range(sensors):
        for e in range(2):
            copy(s, e).start()
    mask_copy.start()
    modes_copy.start()
    for s in range(sensors):
        clear_weights(wide_ref.at[s], sub_cols, width)
    off_copy.wait()
    geometry(geo_ref, off_ref, table_ref, spread_ref, sensors, sub_rows, sub_cols, width)
    for s in range(sensors):
        for e in range(2):
            block_weights(geo_ref.at[s, e * last], narrow_ref.at[s, e], wide_ref.at[s, e], sub_cols, width)
            row_weights(geo_ref.at[s, e * last], line_ref.at[s, e])
    for s in range(sensors):
        for e in range(2):
            copy(s, e).wait()
    for s in range(sensors):
        for e in range(2):
            first_row = e * (SIDE - SHIFT)
            out = block_moments(
                buf.at[s, e], line_ref.at[s, e], narrow_ref.at[s, e], wide_ref.at[s, e], frames, first_row
            )
            for h in range(2):
                for a in range(2):
                    p_ref[s, e, h, a] = out[h][a]
    left = lane_iota() < HALF
    for ref, e, strip in ((down_ref, 0, -1), (up_ref, 1, sub_rows)):
        pair = []
        for h in range(2):
            both = []
            for a in range(2):
                order = [None] * 3
                for s in range(sensors):
                    order[slot_of(strip, s)] = p_ref[s, e, h, a]
                both.append(by_slot(order, cols))
            ref[h] = both[0]
            pair.append(both[1])
        ref[2] = jnp.where(left, pair[0], pltpu.roll(pair[1], HALF, axis=1))
    mask_copy.wait()
    modes_copy.wait()


def slope_terms(plain, lines, mask):
    left = lane_iota() < HALF
    live = mask > 0.0
    flux = jnp.where(left, plain, pltpu.roll(plain, HALF, axis=1))
    moment = jnp.where(left, lines, plain)
    return jnp.where(live, moment / jnp.where(live, flux, 1.0) * mask, 0.0).astype(jnp.bfloat16)


def stacked(modes_ref, picks, half, cols):
    parts = []
    for x in (1, 0):
        used = 0
        for pick in picks:
            if pick is None:
                parts.append(jnp.zeros((cols, modes_ref.shape[-1]), jnp.float32))
            else:
                s, k = pick
                rows = modes_ref[x, s, k].astype(jnp.float32)
                parts.append(rows[half * cols : (half + 1) * cols])
            used += cols
        parts.append(jnp.zeros((HALF - used, modes_ref.shape[-1]), jnp.float32))
    return jnp.concatenate(parts, axis=0).astype(jnp.bfloat16)


def kernel_moments(
    sub_rows, sub_cols, frames, x_ref, geo_ref, edge_narrow_ref, edge_wide_ref, mask_ref, modes_ref,
    pm_ref, edge_ref, em_ref, count_ref, narrow_ref, wide_ref, p_ref, line_ref,
):
    sensors = x_ref.shape[0]
    block = SIDE * frames
    last = sub_rows - 1
    cols = sub_cols // 2

    width = x_ref.shape[2]
    for s in range(sensors):
        clear_weights(wide_ref.at[s], sub_cols, width)
        for i in range(sub_rows):
            row_weights(geo_ref.at[s, i], line_ref.at[s, i])
        for i in range(1, last):
            block_weights(geo_ref.at[s, i], narrow_ref.at[s, i - 1], wide_ref.at[s, i - 1], sub_cols, width)
    for s in range(sensors):
        for i in range(sub_rows):
            if i in (0, last):
                weights = (edge_narrow_ref.at[s, i // last], edge_wide_ref.at[s, i // last])
            else:
                weights = (narrow_ref.at[s, i - 1], wide_ref.at[s, i - 1])
            out = block_moments(
                x_ref.at[s, i * block : (i + 1) * block], line_ref.at[s, i], *weights, frames
            )
            for h in range(2):
                for a in range(2):
                    p_ref[s, i, h, a] = out[h][a]

    def strip_total(s, k, h, a):
        total = None
        for i in (k - 1, k, k + 1):
            if 0 <= i <= last:
                v = p_ref[s, i, h, a]
                total = v if total is None else total + v
        return total

    def mask_of(s, k, h):
        return mask_ref[s, k].astype(jnp.float32)[:, h * cols : (h + 1) * cols]

    count = jnp.zeros((frames, LANES), jnp.float32)
    for e, k in enumerate((0, last)):
        order = [None] * 3
        for s in range(sensors):
            order[slot_of(k, s)] = s
        for h in range(2):
            m = side_by_side([mask_of(s, k, h) for s in order])
            em_ref[e, h] = m
            count = count + m
            for a in range(2):
                edge_ref[e, h, a] = by_slot([strip_total(s, k, h, a) for s in order], cols)
    modes = jnp.zeros((frames, modes_ref.shape[-1]), jnp.float32)
    for s in range(sensors):
        for g in range(1, last, 3):
            order = [None] * 3
            for k in range(g, min(g + 3, last)):
                order[slot_of(k, s)] = k
            for h in range(2):
                none = jnp.zeros((frames, cols), jnp.float32)
                mask = side_by_side([none if k is None else mask_of(s, k, h) for k in order])
                count = count + mask
                plain, lines = (
                    by_slot([None if k is None else strip_total(s, k, h, a) for k in order], cols)
                    for a in range(2)
                )
                modes = modes + jnp.dot(
                    slope_terms(plain, lines, mask),
                    stacked(modes_ref, [None if k is None else (s, k) for k in order], h, cols),
                    preferred_element_type=jnp.float32,
                )
    pm_ref[...] = modes
    count_ref[...] = jnp.broadcast_to(0.5 * jnp.sum(count, axis=1, keepdims=True), count_ref.shape)


def kernel_join(
    sub_rows, sub_cols, frames, tiles, blocks,
    live_ref, before_ref, after_ref, pm_ref, edge_ref, em_ref, count_ref, modes_ref, gain_ref, out_ref,
):
    sensors = modes_ref.shape[1]
    last = sub_rows - 1
    cols = sub_cols // 2
    modes = pm_ref[...]
    for e, k in enumerate((0, last)):
        halo_ref = (before_ref, after_ref)[e]
        halo_strip = (sub_rows, -1)[e]
        turn = (slot_of(k, 0) - slot_of(halo_strip, 0)) % 3
        order = [None] * 3
        for s in range(sensors):
            order[slot_of(k, s)] = s
        both = halo_ref[2]
        for h in range(2):
            lines = both if h == 0 else pltpu.roll(both, HALF, axis=1)
            plain = edge_ref[e, h, 0] + rotate(halo_ref[h], turn, cols)
            lines = edge_ref[e, h, 1] + rotate(lines, turn, cols)
            modes = modes + jnp.dot(
                slope_terms(plain, lines, em_ref[e, h]),
                stacked(modes_ref, [None if s is None else (s, k) for s in order], h, cols),
                preferred_element_type=jnp.float32,
            )
    frame = lax.broadcasted_iota(jnp.int32, (frames, 1), 0)
    live = (frame < live_ref[0]).astype(jnp.float32)
    info = gain_ref[...] * modes * live
    own = lane_iota(frames) == lax.broadcasted_iota(jnp.int32, (frames, LANES), 0)
    counts = jnp.sum(jnp.where(own, count_ref[...] * live, 0.0), axis=0, keepdims=True)
    share = modes.shape[1] // tiles
    pack = LANES // share
    rows = frames // pack
    for t in range(tiles):
        piece = jnp.concatenate(
            [info[g * rows : (g + 1) * rows, t * share : (t + 1) * share] for g in range(pack)], axis=1
        )
        piece = jnp.concatenate([piece, counts], axis=0).reshape(rows + 1, 1, LANES)
        for b in range(blocks):
            out_ref[t * blocks + b] = piece


def shifted(x, by, fill, back):
    rows = x.shape[0]
    if by % 8 == 0:
        pad = jnp.full((by, x.shape[1]), fill, x.dtype)
        if back:
            return jnp.concatenate([x[by:], pad], axis=0)
        return jnp.concatenate([pad, x[: rows - by]], axis=0)
    row = lax.broadcasted_iota(jnp.int32, (rows, 1), 0)
    if back:
        return jnp.where(row < rows - by, pltpu.roll(x, rows - by, axis=0), fill)
    return jnp.where(row >= by, pltpu.roll(x, by, axis=0), fill)


def kernel_smooth(
    tiles, blocks, frames, total_subaps, in_ref, noise_ref, gain_ref, mean_ref, var_ref, mean_scr, var_scr
):
    share = mean_ref.shape[1]
    total = blocks * frames
    tile = lax.axis_index("tile")
    time = lax.axis_index("tm")
    pack = LANES // share
    rows = frames // pack

    def own_modes(v):
        out = v[:, 0:share]
        for t in range(1, tiles):
            out = jnp.where(tile == t, v[:, t * share : (t + 1) * share], out)
        return out

    q = own_modes(noise_ref[...])
    gain = own_modes(gain_ref[...])
    own = lane_iota(frames) == lax.broadcasted_iota(jnp.int32, (frames, LANES), 0)
    infos = []
    counts = []
    for b in range(blocks):
        v = in_ref[b]
        for t in range(1, tiles):
            v = v + in_ref[t * blocks + b]
        v = v.reshape(rows + 1, LANES)
        for g in range(pack):
            infos.append(v[0:rows, g * share : (g + 1) * share])
        counts.append(jnp.sum(jnp.where(own, v[rows : rows + 1], 0.0), axis=1, keepdims=True))
    info_mean = jnp.concatenate(infos, axis=0)
    prec = gain * jnp.concatenate(counts, axis=0) / total_subaps
    row = lax.broadcasted_iota(jnp.int32, (total, 1), 0)
    first = row == 0
    retain = 1.0 / (1.0 + q * prec)
    a = jnp.where(first, 0.0, retain)
    c = jnp.where(first, 1.0 / (1.0 + prec), q * retain)
    b = c * info_mean
    e = a * info_mean
    j = a * prec
    by = 1
    while by < total:
        a1 = shifted(a, by, 1.0, False)
        b1 = shifted(b, by, 0.0, False)
        c1 = shifted(c, by, 0.0, False)
        e1 = shifted(e, by, 0.0, False)
        j1 = shifted(j, by, 0.0, False)
        damp = 1.0 / (1.0 + c1 * j)
        left = a * damp
        right = a1 * damp
        b = left * (b1 + c1 * e) + b
        c = left * a * c1 + c
        e, j = right * (e - j * b1) + e1, right * a1 * j + j1
        a = left * a1
        by *= 2
    g = jnp.where(row == total - 1, 0.0, c / (c + q))
    m = (1.0 - g) * b
    v = c * (1.0 - g)
    by = 1
    while by < total:
        g1 = shifted(g, by, 1.0, True)
        m1 = shifted(m, by, 0.0, True)
        v1 = shifted(v, by, 0.0, True)
        m = g * m1 + m
        v = g * g * v1 + v
        g = g * g1
        by *= 2
    mean_scr[...] = m
    var_scr[...] = v
    start = pl.multiple_of(time * frames, 8)
    mean_ref[...] = mean_scr[pl.ds(start, frames), :]
    var_ref[...] = var_scr[pl.ds(start, frames), :]


def body(pixels, offsets, mask, frame_count, slope_to_modes, process_noise, mode_gain):
    sensors, frames, lines, width = pixels.shape
    sub_rows, sub_cols = mask.shape[2], mask.shape[3]
    modes = process_noise.shape[0]
    tiles = lax.axis_size("tile")
    blocks = lax.axis_size("tm")
    share = modes // tiles
    total_subaps = sensors * sub_rows * tiles * sub_cols
    f32 = jnp.float32
    bf16 = jnp.bfloat16
    x = jnp.transpose(pixels, (0, 2, 1, 3)).reshape(sensors, lines * frames, width)
    off = jnp.transpose(offsets, (0, 1, 3, 2))
    msk = jnp.transpose(mask, (0, 2, 1, 3))
    pixels_v = pltpu.with_memory_space_constraint(x, pltpu.VMEM)
    x, off, msk, slope_to_modes = (
        pltpu.with_memory_space_constraint(v, pltpu.HBM) for v in (x, off, msk, slope_to_modes)
    )
    block = SIDE * frames
    narrow = (2, TILE, LANES)
    line_rows = -(-SIDE // 8) * 8
    wide = (TILE + 2 * (width - 3 * TILE), 2 * LANES)
    table_rows = -(-2 * sensors * (sub_rows + 2) // 8) * 8
    params = pltpu.CompilerParams(vmem_limit_bytes=VMEM_LIMIT)

    def cost(chunks):
        return pl.CostEstimate(
            flops=2 * chunks * block * width * 256, bytes_accessed=chunks * block * width * 2, transcendentals=0
        )

    up, down, geo, edge_narrow, edge_wide, mask_v, modes_v = pl.pallas_call(
        functools.partial(kernel_halo, sub_rows, sub_cols, frames),
        out_shape=(
            jax.ShapeDtypeStruct((3, frames, LANES), f32),
            jax.ShapeDtypeStruct((3, frames, LANES), f32),
            pltpu.VMEM((sensors, sub_rows, 8, LANES), f32),
            pltpu.VMEM((sensors, 2, *narrow), bf16),
            pltpu.VMEM((sensors, 2, *wide), bf16),
            pltpu.VMEM(msk.shape, msk.dtype),
            pltpu.VMEM(slope_to_modes.shape, bf16),
        ),
        in_specs=[HBM] * 4,
        out_specs=(VMEM,) * 7,
        scratch_shapes=[
            pltpu.VMEM((sensors, 2, SHIFT * frames, width), bf16),
            pltpu.VMEM((sensors, 2, 2, 2, frames, LANES), f32),
            pltpu.VMEM((sensors, 2, 2, 2, line_rows, LANES), f32),
            pltpu.VMEM(off.shape, off.dtype),
            pltpu.VMEM((table_rows, sub_cols), f32),
            pltpu.VMEM((2, table_rows, LANES), f32),
            pltpu.SemaphoreType.DMA((sensors, 2)),
            pltpu.SemaphoreType.DMA((3,)),
        ],
        compiler_params=params,
        cost_estimate=cost(2),
        name="halo_moments",
    )(x, off, msk, slope_to_modes)
    onward = [(i, i + 1) for i in range(tiles - 1)]
    backward = [(j, i) for i, j in onward]
    from_before = lax.ppermute(up, "tile", onward)
    from_after = lax.ppermute(down, "tile", backward)
    partial_modes, edge, edge_mask, count = pl.pallas_call(
        functools.partial(kernel_moments, sub_rows, sub_cols, frames),
        out_shape=(
            pltpu.VMEM((frames, modes), f32),
            pltpu.VMEM((2, 2, 2, frames, LANES), f32),
            pltpu.VMEM((2, 2, frames, LANES), f32),
            pltpu.VMEM((frames, LANES), f32),
        ),
        in_specs=[VMEM] * 6,
        out_specs=(VMEM,) * 4,
        scratch_shapes=[
            pltpu.VMEM((sensors, sub_rows - 2, *narrow), bf16),
            pltpu.VMEM((sensors, sub_rows - 2, *wide), bf16),
            pltpu.VMEM((sensors, sub_rows, 2, 2, frames, LANES), f32),
            pltpu.VMEM((sensors, sub_rows, 2, 2, line_rows, LANES), f32),
        ],
        compiler_params=params,
        cost_estimate=cost(sensors * sub_rows),
        name="moments",
    )(pixels_v, geo, edge_narrow, edge_wide, mask_v, modes_v)
    gain = mode_gain.reshape(1, modes)
    packed = frames * share // LANES + 1
    payload = pl.pallas_call(
        functools.partial(kernel_join, sub_rows, sub_cols, frames, tiles, blocks),
        out_shape=jax.ShapeDtypeStruct((tiles * blocks, packed, 1, LANES), f32),
        in_specs=[pl.BlockSpec(memory_space=pltpu.SMEM)] + [VMEM] * 8,
        out_specs=VMEM,
        compiler_params=params,
        name="join_halo",
    )(frame_count, from_before, from_after, partial_modes, edge, edge_mask, count, modes_v, gain)
    info = lax.all_to_all(payload, ("tile", "tm"), 0, 0)
    return pl.pallas_call(
        functools.partial(kernel_smooth, tiles, blocks, frames, float(total_subaps)),
        out_shape=(
            jax.ShapeDtypeStruct((frames, share), f32),
            jax.ShapeDtypeStruct((frames, share), f32),
        ),
        in_specs=[VMEM] * 3,
        out_specs=(VMEM, VMEM),
        scratch_shapes=[
            pltpu.VMEM((blocks * frames, share), f32),
            pltpu.VMEM((blocks * frames, share), f32),
        ],
        compiler_params=params,
        name="smooth",
    )(info, process_noise.reshape(1, modes), gain)


def solution(mesh):
    return jax.shard_map(
        body,
        mesh=mesh,
        in_specs=(
            P("grp", "tm", "tile", None),
            P("grp", None, None, None),
            P("grp", "tm", "tile", None),
            P(("grp", "tm")),
            P(None, None, "tile", None, None),
            P(),
            P(),
        ),
        out_specs=(P(("grp", "tm"), "tile"), P(("grp", "tm"), "tile")),
        check_vma=False,
    )
```

```python
import functools

import jax
import jax.numpy as jnp
from jax import lax
from jax.experimental import pallas as pl
from jax.experimental.pallas import tpu as pltpu
from jax.sharding import PartitionSpec as P

SIDE = 20
SHIFT = 6
CENTRE = (SIDE - 1) / 2.0
LANES = 128
HALF = LANES // 2
TILE = 2 * LANES
VMEM_LIMIT = 24 * 1024 * 1024
VMEM = pl.BlockSpec(memory_space=pltpu.VMEM)
HBM = pl.BlockSpec(memory_space=pl.ANY)


def slot_of(strip, sensor):
    return (strip + 1 + sensor) % 3


def half_columns(half, sub_cols, width):
    cols = sub_cols // 2
    first = max(0, half * cols * SIDE - SHIFT) // LANES * LANES
    end = min(width, -(-((half + 1) * cols * SIDE + SHIFT) // 16) * 16)
    return first, end - first


def lane_iota(rows=1):
    return lax.broadcasted_iota(jnp.int32, (rows, LANES), 1)


def half_lane(rows=1):
    lane = lane_iota(rows)
    return jnp.where(lane >= HALF, lane - HALF, lane)


def by_slot(values, cols):
    lane = half_lane()
    out = jnp.zeros_like(values[0])
    for q, v in enumerate(values):
        if v is not None:
            out = jnp.where((lane >= q * cols) & (lane < (q + 1) * cols), v, out)
    return out


def side_by_side(pieces):
    rows, cols = pieces[0].shape
    group = jnp.concatenate([*pieces, jnp.zeros((rows, HALF - 3 * cols), pieces[0].dtype)], axis=1)
    return jnp.concatenate([group, group], axis=1)


def rotate(x, slots, cols):
    shift = slots * cols
    if shift == 0:
        return x
    near = pltpu.roll(x, shift, axis=1)
    far = pltpu.roll(x, LANES - 3 * cols + shift, axis=1)
    return jnp.where(half_lane() >= shift, near, far)


def geometry(geo_ref, off_ref, table_ref, spread_ref, sensors, sub_rows, sub_cols, width):
    cols = sub_cols // 2
    lane = half_lane()
    index = lane - cols * (lane >= cols).astype(jnp.int32)
    index = index - cols * (lane >= 2 * cols).astype(jnp.int32)
    used = lane < 3 * cols
    tile = lax.axis_index("tile")
    total_rows = off_ref.shape[1]
    for s in range(sensors):
        for k in range(-1, sub_rows + 1):
            row = jnp.clip(tile * sub_rows + k, 0, total_rows - 1)
            n = 2 * (s * (sub_rows + 2) + k + 1)
            table_ref[n : n + 2, :] = off_ref[s, row].astype(jnp.float32)
    table = table_ref[...]
    for h in range(2):
        spread_ref[h] = side_by_side([table[:, h * cols : (h + 1) * cols]] * 3)
    for s in range(sensors):
        for i in range(sub_rows):
            for h in range(2):
                first, _ = half_columns(h, sub_cols, width)
                col_base = (SIDE * (index + h * cols) - first).astype(jnp.float32) + CENTRE
                cs = [None] * 3
                rs = [None] * 3
                for k in (i - 1, i, i + 1):
                    q = slot_of(k, s)
                    n = 2 * (s * (sub_rows + 2) + k + 1)
                    cs[q] = spread_ref[h, n + 1 : n + 2, :]
                    rs[q] = spread_ref[h, n : n + 1, :] + (SIDE * (k - i) + CENTRE)
                geo_ref[s, i, 2 * h : 2 * h + 1, :] = jnp.where(used, by_slot(cs, cols) + col_base, -1000.0)
                geo_ref[s, i, 2 * h + 1 : 2 * h + 2, :] = jnp.where(used, by_slot(rs, cols), -1000.0)


def window_weights(col_pos, first, count):
    base = lax.broadcasted_iota(jnp.int32, (16, LANES), 0).astype(jnp.float32) - col_pos
    bf16 = jnp.bfloat16
    left = lane_iota(16) < HALF
    plain = jnp.where(left, 1.0, 0.0).astype(bf16)
    plain_lane = plain > jnp.bfloat16(0.5)
    for t in range(count // 16):
        d = (base + float(16 * t)).astype(bf16)
        value = jnp.where(plain_lane, jnp.bfloat16(1.0), d)
        yield first + 16 * t, jnp.where(jnp.abs(d) < jnp.bfloat16(10.0), value, jnp.bfloat16(0.0))


def clear_weights(wide_ref, sub_cols, width):
    zero = jnp.zeros((16, LANES), jnp.bfloat16)
    rest = width - 3 * TILE
    end = sum(half_columns(0, sub_cols, width)) - TILE
    begin = half_columns(1, sub_cols, width)[0] - TILE
    for n in range(wide_ref.shape[0]):
        for t in range(end, TILE, 16):
            wide_ref[n, t : t + 16, 0:LANES] = zero
        for t in range(0, begin, 16):
            wide_ref[n, t : t + 16, LANES:] = zero
        for t in range(0, rest, 16):
            wide_ref[n, TILE + t : TILE + t + 16, LANES:] = zero
            wide_ref[n, TILE + rest + t : TILE + rest + t + 16, 0:LANES] = zero


def block_weights(geo_ref, narrow_ref, wide_ref, sub_cols, width):
    rest = width - 3 * TILE
    for h in range(2):
        first, count = half_columns(h, sub_cols, width)
        lanes = slice(h * LANES, (h + 1) * LANES)
        for c, piece in window_weights(geo_ref[2 * h : 2 * h + 1, :], first, count):
            if c < TILE:
                narrow_ref[0, c : c + 16, :] = piece
            elif c < 2 * TILE:
                wide_ref[c - TILE : c - TILE + 16, lanes] = piece
            elif c < 3 * TILE:
                narrow_ref[1, c - 2 * TILE : c - 2 * TILE + 16, :] = piece
            else:
                at = c - 2 * TILE
                wide_ref[at : at + 16, 0:LANES] = piece
                wide_ref[at + rest : at + rest + 16, LANES:] = piece


def row_weights(geo_ref, line_ref):
    count = line_ref.shape[2]
    row = lax.broadcasted_iota(jnp.int32, (count, LANES), 0).astype(jnp.float32)
    for h in range(2):
        d = row - geo_ref[2 * h + 1 : 2 * h + 2, :]
        inside = jnp.abs(d) < 10.0
        line_ref[h, 0] = jnp.where(inside, 1.0, 0.0)
        line_ref[h, 1] = jnp.where(inside, d, 0.0)


def block_moments(pixels, line_ref, narrow_ref, wide_ref, frames, first_row=0):
    f32 = jnp.float32
    rows, width = pixels.shape
    rest = width - 3 * TILE
    a = jnp.dot(pixels[:, 0:TILE], narrow_ref[0], preferred_element_type=f32)
    m = jnp.dot(pixels[:, TILE : 2 * TILE], wide_ref[0:TILE, :], preferred_element_type=f32)
    b = jnp.dot(pixels[:, 2 * TILE : 3 * TILE], narrow_ref[1], preferred_element_type=f32)
    split = rows // 2 if (rows // 2) % 16 == 0 else rows
    tail = pixels[0:split, 3 * TILE :]
    if split < rows:
        tail = jnp.concatenate([tail, pixels[split:, 3 * TILE :]], axis=1)
        r = jnp.dot(tail, wide_ref[TILE:, :], preferred_element_type=f32)
    else:
        r = jnp.dot(tail, wide_ref[TILE : TILE + rest, 0:LANES], preferred_element_type=f32)
    out = [[jnp.zeros((frames, LANES), f32) for _ in range(2)] for _ in range(2)]
    for y in range(rows // frames):
        at = slice(y * frames, (y + 1) * frames)
        if y * frames < split:
            extra = r[at, 0:LANES]
        else:
            extra = r[y * frames - split : (y + 1) * frames - split, LANES:]
        pieces = (a[at] + m[at, 0:LANES], m[at, LANES:] + b[at] + extra)
        for h in range(2):
            at_row = slice(first_row + y, first_row + y + 1)
            out[h][0] = out[h][0] + line_ref[h, 0, at_row, :] * pieces[h]
            out[h][1] = out[h][1] + line_ref[h, 1, at_row, :] * pieces[h]
    return out


def kernel_halo(
    sub_rows, sub_cols, frames, x_hbm, off_hbm, mask_hbm, modes_hbm,
    up_ref, down_ref, geo_ref, narrow_ref, wide_ref, mask_ref, modes_ref,
    buf, p_ref, line_ref, off_ref, table_ref, spread_ref, sem, side_sem,
):
    sensors, lines, width = x_hbm.shape
    reach = SHIFT * frames
    last = sub_rows - 1
    cols = sub_cols // 2

    def copy(s, e):
        return pltpu.make_async_copy(
            x_hbm.at[s, pl.ds(e * (lines - reach), reach)], buf.at[s, e], sem.at[s, e]
        )

    off_copy = pltpu.make_async_copy(off_hbm, off_ref, side_sem.at[0])
    mask_copy = pltpu.make_async_copy(mask_hbm, mask_ref, side_sem.at[1])
    modes_copy = pltpu.make_async_copy(modes_hbm, modes_ref, side_sem.at[2])
    off_copy.start()
    for s in range(sensors):
        for e in range(2):
            copy(s, e).start()
    mask_copy.start()
    modes_copy.start()
    for s in range(sensors):
        clear_weights(wide_ref.at[s], sub_cols, width)
    off_copy.wait()
    geometry(geo_ref, off_ref, table_ref, spread_ref, sensors, sub_rows, sub_cols, width)
    for s in range(sensors):
        for e in range(2):
            block_weights(geo_ref.at[s, e * last], narrow_ref.at[s, e], wide_ref.at[s, e], sub_cols, width)
            row_weights(geo_ref.at[s, e * last], line_ref.at[s, e])
    for s in range(sensors):
        for e in range(2):
            copy(s, e).wait()
    for s in range(sensors):
        for e in range(2):
            first_row = e * (SIDE - SHIFT)
            out = block_moments(
                buf.at[s, e], line_ref.at[s, e], narrow_ref.at[s, e], wide_ref.at[s, e], frames, first_row
            )
            for h in range(2):
                for a in range(2):
                    p_ref[s, e, h, a] = out[h][a]
    left = lane_iota() < HALF
    for ref, e, strip in ((down_ref, 0, -1), (up_ref, 1, sub_rows)):
        pair = []
        for h in range(2):
            both = []
            for a in range(2):
                order = [None] * 3
                for s in range(sensors):
                    order[slot_of(strip, s)] = p_ref[s, e, h, a]
                both.append(by_slot(order, cols))
            ref[h] = both[0]
            pair.append(both[1])
        ref[2] = jnp.where(left, pair[0], pltpu.roll(pair[1], HALF, axis=1))
    mask_copy.wait()
    modes_copy.wait()


def slope_terms(plain, lines, mask):
    left = lane_iota() < HALF
    live = mask > 0.0
    flux = jnp.where(left, plain, pltpu.roll(plain, HALF, axis=1))
    moment = jnp.where(left, lines, plain)
    return jnp.where(live, moment / jnp.where(live, flux, 1.0) * mask, 0.0).astype(jnp.bfloat16)


def stacked(modes_ref, picks, half, cols):
    parts = []
    for x in (1, 0):
        used = 0
        for pick in picks:
            if pick is None:
                parts.append(jnp.zeros((cols, modes_ref.shape[-1]), jnp.float32))
            else:
                s, k = pick
                rows = modes_ref[x, s, k].astype(jnp.float32)
                parts.append(rows[half * cols : (half + 1) * cols])
            used += cols
        parts.append(jnp.zeros((HALF - used, modes_ref.shape[-1]), jnp.float32))
    return jnp.concatenate(parts, axis=0).astype(jnp.bfloat16)


def kernel_moments(
    sub_rows, sub_cols, frames, x_ref, geo_ref, edge_narrow_ref, edge_wide_ref, mask_ref, modes_ref,
    pm_ref, edge_ref, em_ref, count_ref, narrow_ref, wide_ref, p_ref, line_ref,
):
    sensors = x_ref.shape[0]
    block = SIDE * frames
    last = sub_rows - 1
    cols = sub_cols // 2

    width = x_ref.shape[2]
    for s in range(sensors):
        clear_weights(wide_ref.at[s], sub_cols, width)
        for i in range(sub_rows):
            row_weights(geo_ref.at[s, i], line_ref.at[s, i])
        for i in range(1, last):
            block_weights(geo_ref.at[s, i], narrow_ref.at[s, i - 1], wide_ref.at[s, i - 1], sub_cols, width)
        for i in (0, last, *range(1, last)):
            if i in (0, last):
                weights = (edge_narrow_ref.at[s, i // last], edge_wide_ref.at[s, i // last])
            else:
                weights = (narrow_ref.at[s, i - 1], wide_ref.at[s, i - 1])
            out = block_moments(
                x_ref.at[s, i * block : (i + 1) * block], line_ref.at[s, i], *weights, frames
            )
            for h in range(2):
                for a in range(2):
                    p_ref[s, i, h, a] = out[h][a]

    def strip_total(s, k, h, a):
        total = None
        for i in (k - 1, k, k + 1):
            if 0 <= i <= last:
                v = p_ref[s, i, h, a]
                total = v if total is None else total + v
        return total

    def mask_of(s, k, h):
        return mask_ref[s, k].astype(jnp.float32)[:, h * cols : (h + 1) * cols]

    count = jnp.zeros((frames, LANES), jnp.float32)
    for e, k in enumerate((0, last)):
        order = [None] * 3
        for s in range(sensors):
            order[slot_of(k, s)] = s
        for h in range(2):
            m = side_by_side([mask_of(s, k, h) for s in order])
            em_ref[e, h] = m
            count = count + m
            for a in range(2):
                edge_ref[e, h, a] = by_slot([strip_total(s, k, h, a) for s in order], cols)
    modes = jnp.zeros((frames, modes_ref.shape[-1]), jnp.float32)
    for s in range(sensors):
        for g in range(1, last, 3):
            order = [None] * 3
            for k in range(g, min(g + 3, last)):
                order[slot_of(k, s)] = k
            for h in range(2):
                none = jnp.zeros((frames, cols), jnp.float32)
                mask = side_by_side([none if k is None else mask_of(s, k, h) for k in order])
                count = count + mask
                plain, lines = (
                    by_slot([None if k is None else strip_total(s, k, h, a) for k in order], cols)
                    for a in range(2)
                )
                modes = modes + jnp.dot(
                    slope_terms(plain, lines, mask),
                    stacked(modes_ref, [None if k is None else (s, k) for k in order], h, cols),
                    preferred_element_type=jnp.float32,
                )
    pm_ref[...] = modes
    count_ref[...] = jnp.broadcast_to(0.5 * jnp.sum(count, axis=1, keepdims=True), count_ref.shape)


def kernel_join(
    sub_rows, sub_cols, frames, tiles, blocks,
    live_ref, before_ref, after_ref, pm_ref, edge_ref, em_ref, count_ref, modes_ref, gain_ref, out_ref,
):
    sensors = modes_ref.shape[1]
    last = sub_rows - 1
    cols = sub_cols // 2
    modes = pm_ref[...]
    for e, k in enumerate((0, last)):
        halo_ref = (before_ref, after_ref)[e]
        halo_strip = (sub_rows, -1)[e]
        turn = (slot_of(k, 0) - slot_of(halo_strip, 0)) % 3
        order = [None] * 3
        for s in range(sensors):
            order[slot_of(k, s)] = s
        both = halo_ref[2]
        for h in range(2):
            lines = both if h == 0 else pltpu.roll(both, HALF, axis=1)
            plain = edge_ref[e, h, 0] + rotate(halo_ref[h], turn, cols)
            lines = edge_ref[e, h, 1] + rotate(lines, turn, cols)
            modes = modes + jnp.dot(
                slope_terms(plain, lines, em_ref[e, h]),
                stacked(modes_ref, [None if s is None else (s, k) for s in order], h, cols),
                preferred_element_type=jnp.float32,
            )
    frame = lax.broadcasted_iota(jnp.int32, (frames, 1), 0)
    live = (frame < live_ref[0]).astype(jnp.float32)
    info = gain_ref[...] * modes * live
    own = lane_iota(frames) == lax.broadcasted_iota(jnp.int32, (frames, LANES), 0)
    counts = jnp.sum(jnp.where(own, count_ref[...] * live, 0.0), axis=0, keepdims=True)
    share = modes.shape[1] // tiles
    pack = LANES // share
    rows = frames // pack
    for t in range(tiles):
        piece = jnp.concatenate(
            [info[g * rows : (g + 1) * rows, t * share : (t + 1) * share] for g in range(pack)], axis=1
        )
        piece = jnp.concatenate([piece, counts], axis=0).reshape(rows + 1, 1, LANES)
        for b in range(blocks):
            out_ref[t * blocks + b] = piece


def shifted(x, by, fill, back):
    rows = x.shape[0]
    if by % 8 == 0:
        pad = jnp.full((by, x.shape[1]), fill, x.dtype)
        if back:
            return jnp.concatenate([x[by:], pad], axis=0)
        return jnp.concatenate([pad, x[: rows - by]], axis=0)
    row = lax.broadcasted_iota(jnp.int32, (rows, 1), 0)
    if back:
        return jnp.where(row < rows - by, pltpu.roll(x, rows - by, axis=0), fill)
    return jnp.where(row >= by, pltpu.roll(x, by, axis=0), fill)


def kernel_smooth(
    tiles, blocks, frames, total_subaps, in_ref, noise_ref, gain_ref, mean_ref, var_ref, mean_scr, var_scr
):
    share = mean_ref.shape[1]
    total = blocks * frames
    tile = lax.axis_index("tile")
    time = lax.axis_index("tm")
    pack = LANES // share
    rows = frames // pack

    def own_modes(v):
        out = v[:, 0:share]
        for t in range(1, tiles):
            out = jnp.where(tile == t, v[:, t * share : (t + 1) * share], out)
        return out

    q = own_modes(noise_ref[...])
    gain = own_modes(gain_ref[...])
    own = lane_iota(frames) == lax.broadcasted_iota(jnp.int32, (frames, LANES), 0)
    infos = []
    counts = []
    for b in range(blocks):
        v = in_ref[b]
        for t in range(1, tiles):
            v = v + in_ref[t * blocks + b]
        v = v.reshape(rows + 1, LANES)
        for g in range(pack):
            infos.append(v[0:rows, g * share : (g + 1) * share])
        counts.append(jnp.sum(jnp.where(own, v[rows : rows + 1], 0.0), axis=1, keepdims=True))
    info_mean = jnp.concatenate(infos, axis=0)
    prec = gain * jnp.concatenate(counts, axis=0) / total_subaps
    row = lax.broadcasted_iota(jnp.int32, (total, 1), 0)
    first = row == 0
    retain = 1.0 / (1.0 + q * prec)
    a = jnp.where(first, 0.0, retain)
    c = jnp.where(first, 1.0 / (1.0 + prec), q * retain)
    b = c * info_mean
    e = a * info_mean
    j = a * prec
    by = 1
    while by < total:
        a1 = shifted(a, by, 1.0, False)
        b1 = shifted(b, by, 0.0, False)
        c1 = shifted(c, by, 0.0, False)
        e1 = shifted(e, by, 0.0, False)
        j1 = shifted(j, by, 0.0, False)
        damp = 1.0 / (1.0 + c1 * j)
        left = a * damp
        right = a1 * damp
        b = left * (b1 + c1 * e) + b
        c = left * a * c1 + c
        e, j = right * (e - j * b1) + e1, right * a1 * j + j1
        a = left * a1
        by *= 2
    g = jnp.where(row == total - 1, 0.0, c / (c + q))
    m = (1.0 - g) * b
    v = c * (1.0 - g)
    by = 1
    while by < total:
        g1 = shifted(g, by, 1.0, True)
        m1 = shifted(m, by, 0.0, True)
        v1 = shifted(v, by, 0.0, True)
        m = g * m1 + m
        v = g * g * v1 + v
        g = g * g1
        by *= 2
    mean_scr[...] = m
    var_scr[...] = v
    start = pl.multiple_of(time * frames, 8)
    mean_ref[...] = mean_scr[pl.ds(start, frames), :]
    var_ref[...] = var_scr[pl.ds(start, frames), :]


def body(pixels, offsets, mask, frame_count, slope_to_modes, process_noise, mode_gain):
    sensors, frames, lines, width = pixels.shape
    sub_rows, sub_cols = mask.shape[2], mask.shape[3]
    modes = process_noise.shape[0]
    tiles = lax.axis_size("tile")
    blocks = lax.axis_size("tm")
    share = modes // tiles
    total_subaps = sensors * sub_rows * tiles * sub_cols
    f32 = jnp.float32
    bf16 = jnp.bfloat16
    x = jnp.transpose(pixels, (0, 2, 1, 3)).reshape(sensors, lines * frames, width)
    off = jnp.transpose(offsets, (0, 1, 3, 2))
    msk = jnp.transpose(mask, (0, 2, 1, 3))
    pixels_v = pltpu.with_memory_space_constraint(x, pltpu.VMEM)
    x, off, msk, slope_to_modes = (
        pltpu.with_memory_space_constraint(v, pltpu.HBM) for v in (x, off, msk, slope_to_modes)
    )
    block = SIDE * frames
    narrow = (2, TILE, LANES)
    line_rows = -(-SIDE // 8) * 8
    wide = (TILE + 2 * (width - 3 * TILE), 2 * LANES)
    table_rows = -(-2 * sensors * (sub_rows + 2) // 8) * 8
    params = pltpu.CompilerParams(vmem_limit_bytes=VMEM_LIMIT)

    def cost(chunks):
        return pl.CostEstimate(
            flops=2 * chunks * block * width * 256, bytes_accessed=chunks * block * width * 2, transcendentals=0
        )

    up, down, geo, edge_narrow, edge_wide, mask_v, modes_v = pl.pallas_call(
        functools.partial(kernel_halo, sub_rows, sub_cols, frames),
        out_shape=(
            jax.ShapeDtypeStruct((3, frames, LANES), f32),
            jax.ShapeDtypeStruct((3, frames, LANES), f32),
            pltpu.VMEM((sensors, sub_rows, 8, LANES), f32),
            pltpu.VMEM((sensors, 2, *narrow), bf16),
            pltpu.VMEM((sensors, 2, *wide), bf16),
            pltpu.VMEM(msk.shape, msk.dtype),
            pltpu.VMEM(slope_to_modes.shape, bf16),
        ),
        in_specs=[HBM] * 4,
        out_specs=(VMEM,) * 7,
        scratch_shapes=[
            pltpu.VMEM((sensors, 2, SHIFT * frames, width), bf16),
            pltpu.VMEM((sensors, 2, 2, 2, frames, LANES), f32),
            pltpu.VMEM((sensors, 2, 2, 2, line_rows, LANES), f32),
            pltpu.VMEM(off.shape, off.dtype),
            pltpu.VMEM((table_rows, sub_cols), f32),
            pltpu.VMEM((2, table_rows, LANES), f32),
            pltpu.SemaphoreType.DMA((sensors, 2)),
            pltpu.SemaphoreType.DMA((3,)),
        ],
        compiler_params=params,
        cost_estimate=cost(2),
        name="halo_moments",
    )(x, off, msk, slope_to_modes)
    onward = [(i, i + 1) for i in range(tiles - 1)]
    backward = [(j, i) for i, j in onward]
    from_before = lax.ppermute(up, "tile", onward)
    from_after = lax.ppermute(down, "tile", backward)
    partial_modes, edge, edge_mask, count = pl.pallas_call(
        functools.partial(kernel_moments, sub_rows, sub_cols, frames),
        out_shape=(
            pltpu.VMEM((frames, modes), f32),
            pltpu.VMEM((2, 2, 2, frames, LANES), f32),
            pltpu.VMEM((2, 2, frames, LANES), f32),
            pltpu.VMEM((frames, LANES), f32),
        ),
        in_specs=[VMEM] * 6,
        out_specs=(VMEM,) * 4,
        scratch_shapes=[
            pltpu.VMEM((sensors, sub_rows - 2, *narrow), bf16),
            pltpu.VMEM((sensors, sub_rows - 2, *wide), bf16),
            pltpu.VMEM((sensors, sub_rows, 2, 2, frames, LANES), f32),
            pltpu.VMEM((sensors, sub_rows, 2, 2, line_rows, LANES), f32),
        ],
        compiler_params=params,
        cost_estimate=cost(sensors * sub_rows),
        name="moments",
    )(pixels_v, geo, edge_narrow, edge_wide, mask_v, modes_v)
    gain = mode_gain.reshape(1, modes)
    packed = frames * share // LANES + 1
    payload = pl.pallas_call(
        functools.partial(kernel_join, sub_rows, sub_cols, frames, tiles, blocks),
        out_shape=jax.ShapeDtypeStruct((tiles * blocks, packed, 1, LANES), f32),
        in_specs=[pl.BlockSpec(memory_space=pltpu.SMEM)] + [VMEM] * 8,
        out_specs=VMEM,
        compiler_params=params,
        name="join_halo",
    )(frame_count, from_before, from_after, partial_modes, edge, edge_mask, count, modes_v, gain)
    info = lax.all_to_all(payload, ("tile", "tm"), 0, 0)
    return pl.pallas_call(
        functools.partial(kernel_smooth, tiles, blocks, frames, float(total_subaps)),
        out_shape=(
            jax.ShapeDtypeStruct((frames, share), f32),
            jax.ShapeDtypeStruct((frames, share), f32),
        ),
        in_specs=[VMEM] * 3,
        out_specs=(VMEM, VMEM),
        scratch_shapes=[
            pltpu.VMEM((blocks * frames, share), f32),
            pltpu.VMEM((blocks * frames, share), f32),
        ],
        compiler_params=params,
        name="smooth",
    )(info, process_noise.reshape(1, modes), gain)


def solution(mesh):
    return jax.shard_map(
        body,
        mesh=mesh,
        in_specs=(
            P("grp", "tm", "tile", None),
            P("grp", None, None, None),
            P("grp", "tm", "tile", None),
            P(("grp", "tm")),
            P(None, None, "tile", None, None),
            P(),
            P(),
        ),
        out_specs=(P(("grp", "tm"), "tile"), P(("grp", "tm"), "tile")),
        check_vma=False,
    )
```

```python
import functools

import jax
import jax.numpy as jnp
from jax import lax
from jax.experimental import pallas as pl
from jax.experimental.pallas import tpu as pltpu
from jax.sharding import PartitionSpec as P

SIDE = 20
SHIFT = 6
CENTRE = (SIDE - 1) / 2.0
LANES = 128
HALF = LANES // 2
TILE = 2 * LANES
VMEM_LIMIT = 24 * 1024 * 1024
VMEM = pl.BlockSpec(memory_space=pltpu.VMEM)
HBM = pl.BlockSpec(memory_space=pl.ANY)


def slot_of(strip, sensor):
    return (strip + 1 + sensor) % 3


def half_columns(half, sub_cols, width):
    cols = sub_cols // 2
    first = max(0, half * cols * SIDE - SHIFT) // LANES * LANES
    end = min(width, -(-((half + 1) * cols * SIDE + SHIFT) // 16) * 16)
    return first, end - first


def lane_iota(rows=1):
    return lax.broadcasted_iota(jnp.int32, (rows, LANES), 1)


def half_lane(rows=1):
    lane = lane_iota(rows)
    return jnp.where(lane >= HALF, lane - HALF, lane)


def by_slot(values, cols):
    lane = half_lane()
    out = jnp.zeros_like(values[0])
    for q, v in enumerate(values):
        if v is not None:
            out = jnp.where((lane >= q * cols) & (lane < (q + 1) * cols), v, out)
    return out


def side_by_side(pieces):
    rows, cols = pieces[0].shape
    group = jnp.concatenate([*pieces, jnp.zeros((rows, HALF - 3 * cols), pieces[0].dtype)], axis=1)
    return jnp.concatenate([group, group], axis=1)


def rotate(x, slots, cols):
    shift = slots * cols
    if shift == 0:
        return x
    near = pltpu.roll(x, shift, axis=1)
    far = pltpu.roll(x, LANES - 3 * cols + shift, axis=1)
    return jnp.where(half_lane() >= shift, near, far)


def geometry(geo_ref, off_ref, table_ref, spread_ref, sensors, sub_rows, sub_cols, width):
    cols = sub_cols // 2
    lane = half_lane()
    index = lane - cols * (lane >= cols).astype(jnp.int32)
    index = index - cols * (lane >= 2 * cols).astype(jnp.int32)
    used = lane < 3 * cols
    tile = lax.axis_index("tile")
    total_rows = off_ref.shape[1]
    for s in range(sensors):
        for k in range(-1, sub_rows + 1):
            row = jnp.clip(tile * sub_rows + k, 0, total_rows - 1)
            n = 2 * (s * (sub_rows + 2) + k + 1)
            table_ref[n : n + 2, :] = off_ref[s, row].astype(jnp.float32)
    table = table_ref[...]
    for h in range(2):
        spread_ref[h] = side_by_side([table[:, h * cols : (h + 1) * cols]] * 3)
    for s in range(sensors):
        for i in range(sub_rows):
            for h in range(2):
                first, _ = half_columns(h, sub_cols, width)
                col_base = (SIDE * (index + h * cols) - first).astype(jnp.float32) + CENTRE
                cs = [None] * 3
                rs = [None] * 3
                for k in (i - 1, i, i + 1):
                    q = slot_of(k, s)
                    n = 2 * (s * (sub_rows + 2) + k + 1)
                    cs[q] = spread_ref[h, n + 1 : n + 2, :]
                    rs[q] = spread_ref[h, n : n + 1, :] + (SIDE * (k - i) + CENTRE)
                geo_ref[s, i, 2 * h : 2 * h + 1, :] = jnp.where(used, by_slot(cs, cols) + col_base, -1000.0)
                geo_ref[s, i, 2 * h + 1 : 2 * h + 2, :] = jnp.where(used, by_slot(rs, cols), -1000.0)


def window_weights(col_pos, first, count):
    base = lax.broadcasted_iota(jnp.int32, (16, LANES), 0).astype(jnp.float32) - col_pos
    bf16 = jnp.bfloat16
    left = lane_iota(16) < HALF
    plain = jnp.where(left, 1.0, 0.0).astype(bf16)
    plain_lane = plain > jnp.bfloat16(0.5)
    for t in range(count // 16):
        d = (base + float(16 * t)).astype(bf16)
        value = jnp.where(plain_lane, jnp.bfloat16(1.0), d)
        yield first + 16 * t, jnp.where(jnp.abs(d) < jnp.bfloat16(10.0), value, jnp.bfloat16(0.0))


def clear_weights(wide_ref, sub_cols, width):
    zero = jnp.zeros((16, LANES), jnp.bfloat16)
    rest = width - 3 * TILE
    end = sum(half_columns(0, sub_cols, width)) - TILE
    begin = half_columns(1, sub_cols, width)[0] - TILE
    for n in range(wide_ref.shape[0]):
        for t in range(end, TILE, 16):
            wide_ref[n, t : t + 16, 0:LANES] = zero
        for t in range(0, begin, 16):
            wide_ref[n, t : t + 16, LANES:] = zero
        for t in range(0, rest, 16):
            wide_ref[n, TILE + t : TILE + t + 16, LANES:] = zero
            wide_ref[n, TILE + rest + t : TILE + rest + t + 16, 0:LANES] = zero


def block_weights(geo_ref, narrow_ref, wide_ref, sub_cols, width):
    rest = width - 3 * TILE
    for h in range(2):
        first, count = half_columns(h, sub_cols, width)
        lanes = slice(h * LANES, (h + 1) * LANES)
        for c, piece in window_weights(geo_ref[2 * h : 2 * h + 1, :], first, count):
            if c < TILE:
                narrow_ref[0, c : c + 16, :] = piece
            elif c < 2 * TILE:
                wide_ref[c - TILE : c - TILE + 16, lanes] = piece
            elif c < 3 * TILE:
                narrow_ref[1, c - 2 * TILE : c - 2 * TILE + 16, :] = piece
            else:
                at = c - 2 * TILE
                wide_ref[at : at + 16, 0:LANES] = piece
                wide_ref[at + rest : at + rest + 16, LANES:] = piece


def row_weights(geo_ref, line_ref):
    count = line_ref.shape[2]
    row = lax.broadcasted_iota(jnp.int32, (count, LANES), 0).astype(jnp.float32)
    for h in range(2):
        d = row - geo_ref[2 * h + 1 : 2 * h + 2, :]
        inside = jnp.abs(d) < 10.0
        line_ref[h, 0] = jnp.where(inside, 1.0, 0.0)
        line_ref[h, 1] = jnp.where(inside, d, 0.0)


def block_moments(pixels, line_ref, narrow_ref, wide_ref, frames, first_row=0):
    f32 = jnp.float32
    rows, width = pixels.shape
    rest = width - 3 * TILE
    a = jnp.dot(pixels[:, 0:TILE], narrow_ref[0], preferred_element_type=f32)
    m = jnp.dot(pixels[:, TILE : 2 * TILE], wide_ref[0:TILE, :], preferred_element_type=f32)
    b = jnp.dot(pixels[:, 2 * TILE : 3 * TILE], narrow_ref[1], preferred_element_type=f32)
    split = rows // 2 if (rows // 2) % 16 == 0 else rows
    tail = pixels[0:split, 3 * TILE :]
    if split < rows:
        tail = jnp.concatenate([tail, pixels[split:, 3 * TILE :]], axis=1)
        r = jnp.dot(tail, wide_ref[TILE:, :], preferred_element_type=f32)
    else:
        r = jnp.dot(tail, wide_ref[TILE : TILE + rest, 0:LANES], preferred_element_type=f32)
    out = [[jnp.zeros((frames, LANES), f32) for _ in range(2)] for _ in range(2)]
    for y in range(rows // frames):
        at = slice(y * frames, (y + 1) * frames)
        if y * frames < split:
            extra = r[at, 0:LANES]
        else:
            extra = r[y * frames - split : (y + 1) * frames - split, LANES:]
        pieces = (a[at] + m[at, 0:LANES], m[at, LANES:] + b[at] + extra)
        for h in range(2):
            at_row = slice(first_row + y, first_row + y + 1)
            out[h][0] = out[h][0] + line_ref[h, 0, at_row, :] * pieces[h]
            out[h][1] = out[h][1] + line_ref[h, 1, at_row, :] * pieces[h]
    return out


def kernel_halo(
    sub_rows, sub_cols, frames, x_hbm, off_hbm, mask_hbm, modes_hbm,
    up_ref, down_ref, geo_ref, narrow_ref, wide_ref, mask_ref, modes_ref,
    buf, p_ref, line_ref, off_ref, table_ref, spread_ref, sem, side_sem,
):
    sensors, lines, width = x_hbm.shape
    reach = SHIFT * frames
    last = sub_rows - 1
    cols = sub_cols // 2

    def copy(s, e):
        return pltpu.make_async_copy(
            x_hbm.at[s, pl.ds(e * (lines - reach), reach)], buf.at[s, e], sem.at[s, e]
        )

    off_copy = pltpu.make_async_copy(off_hbm, off_ref, side_sem.at[0])
    mask_copy = pltpu.make_async_copy(mask_hbm, mask_ref, side_sem.at[1])
    modes_copy = pltpu.make_async_copy(modes_hbm, modes_ref, side_sem.at[2])
    off_copy.start()
    for s in range(sensors):
        for e in range(2):
            copy(s, e).start()
    mask_copy.start()
    modes_copy.start()
    for s in range(sensors):
        clear_weights(wide_ref.at[s], sub_cols, width)
    off_copy.wait()
    geometry(geo_ref, off_ref, table_ref, spread_ref, sensors, sub_rows, sub_cols, width)
    for s in range(sensors):
        for e in range(2):
            block_weights(geo_ref.at[s, e * last], narrow_ref.at[s, e], wide_ref.at[s, e], sub_cols, width)
            row_weights(geo_ref.at[s, e * last], line_ref.at[s, e])
    for s in range(sensors):
        for e in range(2):
            copy(s, e).wait()
    for s in range(sensors):
        for e in range(2):
            first_row = e * (SIDE - SHIFT)
            out = block_moments(
                buf.at[s, e], line_ref.at[s, e], narrow_ref.at[s, e], wide_ref.at[s, e], frames, first_row
            )
            for h in range(2):
                for a in range(2):
                    p_ref[s, e, h, a] = out[h][a]
    left = lane_iota() < HALF
    for ref, e, strip in ((down_ref, 0, -1), (up_ref, 1, sub_rows)):
        pair = []
        for h in range(2):
            both = []
            for a in range(2):
                order = [None] * 3
                for s in range(sensors):
                    order[slot_of(strip, s)] = p_ref[s, e, h, a]
                both.append(by_slot(order, cols))
            ref[h] = both[0]
            pair.append(both[1])
        ref[2] = jnp.where(left, pair[0], pltpu.roll(pair[1], HALF, axis=1))
    mask_copy.wait()
    modes_copy.wait()


def slope_terms(plain, lines, mask):
    left = lane_iota() < HALF
    live = mask > 0.0
    flux = jnp.where(left, plain, pltpu.roll(plain, HALF, axis=1))
    moment = jnp.where(left, lines, plain)
    return jnp.where(live, moment / jnp.where(live, flux, 1.0) * mask, 0.0).astype(jnp.bfloat16)


def stacked(modes_ref, picks, half, cols):
    parts = []
    for x in (1, 0):
        used = 0
        for pick in picks:
            if pick is None:
                parts.append(jnp.zeros((cols, modes_ref.shape[-1]), jnp.float32))
            else:
                s, k = pick
                rows = modes_ref[x, s, k].astype(jnp.float32)
                parts.append(rows[half * cols : (half + 1) * cols])
            used += cols
        parts.append(jnp.zeros((HALF - used, modes_ref.shape[-1]), jnp.float32))
    return jnp.concatenate(parts, axis=0).astype(jnp.bfloat16)


def kernel_moments(
    sub_rows, sub_cols, frames, x_ref, geo_ref, edge_narrow_ref, edge_wide_ref, mask_ref, modes_ref,
    pm_ref, edge_ref, em_ref, count_ref, narrow_ref, wide_ref, p_ref, line_ref,
):
    sensors = x_ref.shape[0]
    block = SIDE * frames
    last = sub_rows - 1
    cols = sub_cols // 2

    def strip_total(s, k, h, a):
        total = None
        for i in (k - 1, k, k + 1):
            if 0 <= i <= last:
                v = p_ref[s, i, h, a]
                total = v if total is None else total + v
        return total

    def mask_of(s, k, h):
        return mask_ref[s, k].astype(jnp.float32)[:, h * cols : (h + 1) * cols]

    modes = jnp.zeros((frames, modes_ref.shape[-1]), jnp.float32)
    count = jnp.zeros((frames, LANES), jnp.float32)
    width = x_ref.shape[2]
    for s in range(sensors):
        clear_weights(wide_ref.at[s], sub_cols, width)
        for i in range(sub_rows):
            row_weights(geo_ref.at[s, i], line_ref.at[s, i])
        for i in range(1, last):
            block_weights(geo_ref.at[s, i], narrow_ref.at[s, i - 1], wide_ref.at[s, i - 1], sub_cols, width)
        for i in (0, last, *range(1, last)):
            if i in (0, last):
                weights = (edge_narrow_ref.at[s, i // last], edge_wide_ref.at[s, i // last])
            else:
                weights = (narrow_ref.at[s, i - 1], wide_ref.at[s, i - 1])
            out = block_moments(
                x_ref.at[s, i * block : (i + 1) * block], line_ref.at[s, i], *weights, frames
            )
            for h in range(2):
                for a in range(2):
                    p_ref[s, i, h, a] = out[h][a]
        for g in range(1, last, 3):
            order = [None] * 3
            for k in range(g, min(g + 3, last)):
                order[slot_of(k, s)] = k
            for h in range(2):
                none = jnp.zeros((frames, cols), jnp.float32)
                mask = side_by_side([none if k is None else mask_of(s, k, h) for k in order])
                count = count + mask
                plain, lines = (
                    by_slot([None if k is None else strip_total(s, k, h, a) for k in order], cols)
                    for a in range(2)
                )
                modes = modes + jnp.dot(
                    slope_terms(plain, lines, mask),
                    stacked(modes_ref, [None if k is None else (s, k) for k in order], h, cols),
                    preferred_element_type=jnp.float32,
                )
    for e, k in enumerate((0, last)):
        order = [None] * 3
        for s in range(sensors):
            order[slot_of(k, s)] = s
        for h in range(2):
            m = side_by_side([mask_of(s, k, h) for s in order])
            em_ref[e, h] = m
            count = count + m
            for a in range(2):
                edge_ref[e, h, a] = by_slot([strip_total(s, k, h, a) for s in order], cols)
    pm_ref[...] = modes
    count_ref[...] = jnp.broadcast_to(0.5 * jnp.sum(count, axis=1, keepdims=True), count_ref.shape)


def kernel_join(
    sub_rows, sub_cols, frames, tiles, blocks,
    live_ref, before_ref, after_ref, pm_ref, edge_ref, em_ref, count_ref, modes_ref, gain_ref, out_ref,
):
    sensors = modes_ref.shape[1]
    last = sub_rows - 1
    cols = sub_cols // 2
    modes = pm_ref[...]
    for e, k in enumerate((0, last)):
        halo_ref = (before_ref, after_ref)[e]
        halo_strip = (sub_rows, -1)[e]
        turn = (slot_of(k, 0) - slot_of(halo_strip, 0)) % 3
        order = [None] * 3
        for s in range(sensors):
            order[slot_of(k, s)] = s
        both = halo_ref[2]
        for h in range(2):
            lines = both if h == 0 else pltpu.roll(both, HALF, axis=1)
            plain = edge_ref[e, h, 0] + rotate(halo_ref[h], turn, cols)
            lines = edge_ref[e, h, 1] + rotate(lines, turn, cols)
            modes = modes + jnp.dot(
                slope_terms(plain, lines, em_ref[e, h]),
                stacked(modes_ref, [None if s is None else (s, k) for s in order], h, cols),
                preferred_element_type=jnp.float32,
            )
    frame = lax.broadcasted_iota(jnp.int32, (frames, 1), 0)
    live = (frame < live_ref[0]).astype(jnp.float32)
    info = gain_ref[...] * modes * live
    own = lane_iota(frames) == lax.broadcasted_iota(jnp.int32, (frames, LANES), 0)
    counts = jnp.sum(jnp.where(own, count_ref[...] * live, 0.0), axis=0, keepdims=True)
    share = modes.shape[1] // tiles
    pack = LANES // share
    rows = frames // pack
    for t in range(tiles):
        piece = jnp.concatenate(
            [info[g * rows : (g + 1) * rows, t * share : (t + 1) * share] for g in range(pack)], axis=1
        )
        piece = jnp.concatenate([piece, counts], axis=0).reshape(rows + 1, 1, LANES)
        for b in range(blocks):
            out_ref[t * blocks + b] = piece


def shifted(x, by, fill, back):
    rows = x.shape[0]
    if by % 8 == 0:
        pad = jnp.full((by, x.shape[1]), fill, x.dtype)
        if back:
            return jnp.concatenate([x[by:], pad], axis=0)
        return jnp.concatenate([pad, x[: rows - by]], axis=0)
    row = lax.broadcasted_iota(jnp.int32, (rows, 1), 0)
    if back:
        return jnp.where(row < rows - by, pltpu.roll(x, rows - by, axis=0), fill)
    return jnp.where(row >= by, pltpu.roll(x, by, axis=0), fill)


def kernel_smooth(
    tiles, blocks, frames, total_subaps, in_ref, noise_ref, gain_ref, mean_ref, var_ref, mean_scr, var_scr
):
    share = mean_ref.shape[1]
    total = blocks * frames
    tile = lax.axis_index("tile")
    time = lax.axis_index("tm")
    pack = LANES // share
    rows = frames // pack

    def own_modes(v):
        out = v[:, 0:share]
        for t in range(1, tiles):
            out = jnp.where(tile == t, v[:, t * share : (t + 1) * share], out)
        return out

    q = own_modes(noise_ref[...])
    gain = own_modes(gain_ref[...])
    own = lane_iota(frames) == lax.broadcasted_iota(jnp.int32, (frames, LANES), 0)
    infos = []
    counts = []
    for b in range(blocks):
        v = in_ref[b]
        for t in range(1, tiles):
            v = v + in_ref[t * blocks + b]
        v = v.reshape(rows + 1, LANES)
        for g in range(pack):
            infos.append(v[0:rows, g * share : (g + 1) * share])
        counts.append(jnp.sum(jnp.where(own, v[rows : rows + 1], 0.0), axis=1, keepdims=True))
    info_mean = jnp.concatenate(infos, axis=0)
    prec = gain * jnp.concatenate(counts, axis=0) / total_subaps
    row = lax.broadcasted_iota(jnp.int32, (total, 1), 0)
    first = row == 0
    retain = 1.0 / (1.0 + q * prec)
    a = jnp.where(first, 0.0, retain)
    c = jnp.where(first, 1.0 / (1.0 + prec), q * retain)
    b = c * info_mean
    e = a * info_mean
    j = a * prec
    by = 1
    while by < total:
        a1 = shifted(a, by, 1.0, False)
        b1 = shifted(b, by, 0.0, False)
        c1 = shifted(c, by, 0.0, False)
        e1 = shifted(e, by, 0.0, False)
        j1 = shifted(j, by, 0.0, False)
        damp = 1.0 / (1.0 + c1 * j)
        left = a * damp
        right = a1 * damp
        b = left * (b1 + c1 * e) + b
        c = left * a * c1 + c
        e, j = right * (e - j * b1) + e1, right * a1 * j + j1
        a = left * a1
        by *= 2
    g = jnp.where(row == total - 1, 0.0, c / (c + q))
    m = (1.0 - g) * b
    v = c * (1.0 - g)
    by = 1
    while by < total:
        g1 = shifted(g, by, 1.0, True)
        m1 = shifted(m, by, 0.0, True)
        v1 = shifted(v, by, 0.0, True)
        m = g * m1 + m
        v = g * g * v1 + v
        g = g * g1
        by *= 2
    mean_scr[...] = m
    var_scr[...] = v
    start = pl.multiple_of(time * frames, 8)
    mean_ref[...] = mean_scr[pl.ds(start, frames), :]
    var_ref[...] = var_scr[pl.ds(start, frames), :]


def body(pixels, offsets, mask, frame_count, slope_to_modes, process_noise, mode_gain):
    sensors, frames, lines, width = pixels.shape
    sub_rows, sub_cols = mask.shape[2], mask.shape[3]
    modes = process_noise.shape[0]
    tiles = lax.axis_size("tile")
    blocks = lax.axis_size("tm")
    share = modes // tiles
    total_subaps = sensors * sub_rows * tiles * sub_cols
    f32 = jnp.float32
    bf16 = jnp.bfloat16
    x = jnp.transpose(pixels, (0, 2, 1, 3)).reshape(sensors, lines * frames, width)
    off = jnp.transpose(offsets, (0, 1, 3, 2))
    msk = jnp.transpose(mask, (0, 2, 1, 3))
    pixels_v = pltpu.with_memory_space_constraint(x, pltpu.VMEM)
    x, off, msk, slope_to_modes = (
        pltpu.with_memory_space_constraint(v, pltpu.HBM) for v in (x, off, msk, slope_to_modes)
    )
    block = SIDE * frames
    narrow = (2, TILE, LANES)
    line_rows = -(-SIDE // 8) * 8
    wide = (TILE + 2 * (width - 3 * TILE), 2 * LANES)
    table_rows = -(-2 * sensors * (sub_rows + 2) // 8) * 8
    params = pltpu.CompilerParams(vmem_limit_bytes=VMEM_LIMIT)

    def cost(chunks):
        return pl.CostEstimate(
            flops=2 * chunks * block * width * 256, bytes_accessed=chunks * block * width * 2, transcendentals=0
        )

    up, down, geo, edge_narrow, edge_wide, mask_v, modes_v = pl.pallas_call(
        functools.partial(kernel_halo, sub_rows, sub_cols, frames),
        out_shape=(
            jax.ShapeDtypeStruct((3, frames, LANES), f32),
            jax.ShapeDtypeStruct((3, frames, LANES), f32),
            pltpu.VMEM((sensors, sub_rows, 8, LANES), f32),
            pltpu.VMEM((sensors, 2, *narrow), bf16),
            pltpu.VMEM((sensors, 2, *wide), bf16),
            pltpu.VMEM(msk.shape, msk.dtype),
            pltpu.VMEM(slope_to_modes.shape, bf16),
        ),
        in_specs=[HBM] * 4,
        out_specs=(VMEM,) * 7,
        scratch_shapes=[
            pltpu.VMEM((sensors, 2, SHIFT * frames, width), bf16),
            pltpu.VMEM((sensors, 2, 2, 2, frames, LANES), f32),
            pltpu.VMEM((sensors, 2, 2, 2, line_rows, LANES), f32),
            pltpu.VMEM(off.shape, off.dtype),
            pltpu.VMEM((table_rows, sub_cols), f32),
            pltpu.VMEM((2, table_rows, LANES), f32),
            pltpu.SemaphoreType.DMA((sensors, 2)),
            pltpu.SemaphoreType.DMA((3,)),
        ],
        compiler_params=params,
        cost_estimate=cost(2),
        name="halo_moments",
    )(x, off, msk, slope_to_modes)
    onward = [(i, i + 1) for i in range(tiles - 1)]
    backward = [(j, i) for i, j in onward]
    from_before = lax.ppermute(up, "tile", onward)
    from_after = lax.ppermute(down, "tile", backward)
    partial_modes, edge, edge_mask, count = pl.pallas_call(
        functools.partial(kernel_moments, sub_rows, sub_cols, frames),
        out_shape=(
            pltpu.VMEM((frames, modes), f32),
            pltpu.VMEM((2, 2, 2, frames, LANES), f32),
            pltpu.VMEM((2, 2, frames, LANES), f32),
            pltpu.VMEM((frames, LANES), f32),
        ),
        in_specs=[VMEM] * 6,
        out_specs=(VMEM,) * 4,
        scratch_shapes=[
            pltpu.VMEM((sensors, sub_rows - 2, *narrow), bf16),
            pltpu.VMEM((sensors, sub_rows - 2, *wide), bf16),
            pltpu.VMEM((sensors, sub_rows, 2, 2, frames, LANES), f32),
            pltpu.VMEM((sensors, sub_rows, 2, 2, line_rows, LANES), f32),
        ],
        compiler_params=params,
        cost_estimate=cost(sensors * sub_rows),
        name="moments",
    )(pixels_v, geo, edge_narrow, edge_wide, mask_v, modes_v)
    gain = mode_gain.reshape(1, modes)
    packed = frames * share // LANES + 1
    payload = pl.pallas_call(
        functools.partial(kernel_join, sub_rows, sub_cols, frames, tiles, blocks),
        out_shape=jax.ShapeDtypeStruct((tiles * blocks, packed, 1, LANES), f32),
        in_specs=[pl.BlockSpec(memory_space=pltpu.SMEM)] + [VMEM] * 8,
        out_specs=VMEM,
        compiler_params=params,
        name="join_halo",
    )(frame_count, from_before, from_after, partial_modes, edge, edge_mask, count, modes_v, gain)
    info = lax.all_to_all(payload, ("tile", "tm"), 0, 0)
    return pl.pallas_call(
        functools.partial(kernel_smooth, tiles, blocks, frames, float(total_subaps)),
        out_shape=(
            jax.ShapeDtypeStruct((frames, share), f32),
            jax.ShapeDtypeStruct((frames, share), f32),
        ),
        in_specs=[VMEM] * 3,
        out_specs=(VMEM, VMEM),
        scratch_shapes=[
            pltpu.VMEM((blocks * frames, share), f32),
            pltpu.VMEM((blocks * frames, share), f32),
        ],
        compiler_params=params,
        name="smooth",
    )(info, process_noise.reshape(1, modes), gain)


def solution(mesh):
    return jax.shard_map(
        body,
        mesh=mesh,
        in_specs=(
            P("grp", "tm", "tile", None),
            P("grp", None, None, None),
            P("grp", "tm", "tile", None),
            P(("grp", "tm")),
            P(None, None, "tile", None, None),
            P(),
            P(),
        ),
        out_specs=(P(("grp", "tm"), "tile"), P(("grp", "tm"), "tile")),
        check_vma=False,
    )
```
